32 devices in a mesh: section: 2 (over core), dp: 4 (over y, x), seq: 4 (over z).
Axes of the slice: x: 2, y: 2, z: 4, core: 2. Of those that a mesh axis runs over, the one named last changes fastest.
Arguments:
- inputs: bfloat16 [2, 4, 2048, 512], P(None, 'dp', 'seq'), may hold values from -6 to 6
- cotangent: bfloat16 [2, 4, 2048, 512], P(None, 'dp', 'seq'), may hold values from -6 to 6
- doc_lengths: int32 [2, 4, 4], P(None, 'dp'), may hold values from 1 to 2045, as said below
- feature_proj: float32 [2, 8, 64, 256], P('section'), may hold values from -6 to 6
- w_query: float32 [2, 512, 512], P('section', ('dp', 'seq')), may hold values from -0.25 to 0.25
- w_key: float32 [2, 512, 512], P('section', ('dp', 'seq')), may hold values from -0.25 to 0.25
- w_value: float32 [2, 512, 512], P('section', ('dp', 'seq')), may hold values from -0.25 to 0.25
- w_out: float32 [2, 512, 512], P('section', ('dp', 'seq')), may hold values from -1.5 to 1.5
- w_up: float32 [2, 512, 2048], P('section', ('dp', 'seq')), may hold values from -0.25 to 0.25
- w_down: float32 [2, 2048, 512], P('section', ('dp', 'seq')), may hold values from -0.125 to 0.125
- gain_attn: float32 [2, 512], P('section', ('dp', 'seq')), may hold values from 0.1 to 1.9
- gain_ffn: float32 [2, 512], P('section', ('dp', 'seq')), may hold values from 0.1 to 1.9
Outputs:
- activations: bfloat16 [2, 2, 4, 2048, 512], P('section', None, 'dp', 'seq')
- input_grad: bfloat16 [2, 2, 4, 2048, 512], P('section', None, 'dp', 'seq')
- grad_query: float32 [2, 512, 512], P('section', ('dp', 'seq'))
- grad_key: float32 [2, 512, 512], P('section', ('dp', 'seq'))
- grad_value: float32 [2, 512, 512], P('section', ('dp', 'seq'))
- grad_out: float32 [2, 512, 512], P('section', ('dp', 'seq'))
- grad_up: float32 [2, 512, 2048], P('section', ('dp', 'seq'))
- grad_down: float32 [2, 2048, 512], P('section', ('dp', 'seq'))
- grad_gain_attn: float32 [2, 512], P('section', ('dp', 'seq'))
- grad_gain_ffn: float32 [2, 512], P('section', ('dp', 'seq'))
The draws below stay inside these ranges and needn't reach their ends.
Inputs may be any that keep to these rules, and one draw needn't show every extreme that they name: `doc_lengths`: each row of 4 lengths sums to 2048; its second document covers the positions 256 to 1791.
All inputs are finite; a program needn't handle non-finite values.
Results may differ from the reference program's by a relative error of at most 0.023.
The reference program's roundings to bfloat16 on the way count: a program that leaves them out, or rounds other values in their place, can miss the bound.
Values may be sent and summed in bfloat16 or wider, within the bound.
A program may use at most 256 MiB of HBM per device.

```python
import jax
import jax.numpy as jnp
from jax import lax

D = 512
HEADS = 8
HD = 64
FEATS = 256
FF = 2048
ROWS = 512
MB = 2
NDOCS = 4
PACKS = 4
PACK_LEN = 2048


def draw_doc_lengths(key, part):
    key = jax.random.fold_in(key, 7)
    keys = jax.random.split(key, 3)
    shape_rows = (MB, PACKS)
    corner = (jnp.arange(MB, dtype=jnp.int32)[:, None] == 0) & (jnp.arange(PACKS, dtype=jnp.int32)[None, :] == 0)
    first_len = jax.random.randint(keys[0], shape_rows, 1, ROWS // 2 + 1)
    rest_len = jax.random.randint(keys[1], shape_rows, 2, ROWS // 2 + 1)
    first_len = jnp.where(corner, 1, first_len)
    rest_len = jnp.where(corner, 2, rest_len)
    split_len = jax.random.randint(keys[2], shape_rows, 0, 2 ** 20) % (rest_len - 1) + 1
    long_len = PACK_LEN - first_len - rest_len
    return jnp.stack([first_len, long_len, split_len, rest_len - split_len], axis=-1).astype(jnp.int32)


def levels(stream_key, shape, cuts, smallest, high):
    loudness = 1.0
    for axis_at, parts in cuts:
        steps = jax.random.uniform(jax.random.fold_in(jax.random.fold_in(stream_key, 6), axis_at), (parts,), jnp.float32, smallest / len(cuts), high / len(cuts))
        loudness = loudness * jnp.repeat(jnp.exp(steps), shape[axis_at] // parts).reshape((-1,) + (1,) * (len(shape) - 1 - axis_at))
    return loudness


def normal_values(own_key, dims, scale, limit, pieces=(), held_as=jnp.bfloat16):
    drawn = jax.random.normal(own_key, dims, jnp.float32) * scale
    if len(pieces) > 0:
        drawn = levels(own_key, dims, pieces, -0.22, 0.18) * drawn
    return jnp.clip(drawn, min=-limit, max=limit).astype(held_as)


def setup_inputs(seed: int = 0) -> dict:
    key_list = jax.random.split(jax.random.key(seed), 13)
    return {
        "inputs": normal_values(key_list[0], (MB, PACKS, PACK_LEN, D), 1.0, 6.0, ((1, 4), (2, 4))),
        "cotangent": normal_values(key_list[1], (MB, PACKS, PACK_LEN, D), 1.0, 6.0, ((1, 4), (2, 4))),
        "doc_lengths": draw_doc_lengths(jax.random.fold_in(key_list[12], 71), 0),
        "feature_proj": normal_values(key_list[3], (2, HEADS, HD, FEATS), 1.0, 6.0, ((0, 2),), jnp.float32),
        "w_query": normal_values(key_list[4], (2, D, D), D ** -0.5, 0.25, ((0, 2), (1, 16)), jnp.float32),
        "w_key": normal_values(key_list[5], (2, D, D), D ** -0.5, 0.25, ((0, 2), (1, 16)), jnp.float32),
        "w_value": normal_values(key_list[6], (2, D, D), D ** -0.5, 0.25, ((0, 2), (1, 16)), jnp.float32),
        "w_out": normal_values(key_list[7], (2, D, D), (D // 32) ** -0.5, 1.5, ((0, 2), (1, 16)), jnp.float32),
        "w_up": normal_values(key_list[8], (2, D, FF), D ** -0.5, 0.25, ((0, 2), (1, 16)), jnp.float32),
        "w_down": normal_values(key_list[9], (2, FF, D), FF ** -0.5, 0.125, ((0, 2), (1, 16)), jnp.float32),
        "gain_attn": jnp.clip(1.0 + 0.18 * jax.random.normal(key_list[10], (2, D), jnp.float32), 0.1, 1.9),
        "gain_ffn": jnp.clip(1.0 + 0.18 * jax.random.normal(key_list[11], (2, D), jnp.float32), 0.1, 1.9),
    }


HIGH_PRECISION = lax.Precision.HIGHEST

@jax.custom_vjp
def low(v):
    return lax.optimization_barrier(v.astype(jnp.bfloat16)).astype(jnp.float32)

@jax.custom_vjp
def low_back(v):
    return v

def low_keep(v):
    return (low(v), None)

def low_pass(kept, grad):
    return (grad,)

def back_keep(v):
    return (v, None)

def back_low(kept, grad):
    return (low(grad),)
low.defvjp(low_keep, low_pass)
low_back.defvjp(back_keep, back_low)

def product(left, right):
    return jnp.dot(left, right, precision=HIGH_PRECISION)

def norm_rows(values):
    centre = values - lax.optimization_barrier(jnp.mean(values, axis=-1, keepdims=True))
    return centre * lax.rsqrt(lax.optimization_barrier(jnp.mean(centre * centre, axis=-1, keepdims=True)) + 1e-05)

def lift(values, projection):
    heads, depth, feats = projection.shape
    scaled = values.reshape(values.shape[0], heads, depth) * depth ** (-0.25)
    raised = jnp.einsum('nhd,hdm->nhm', scaled, projection, precision=HIGH_PRECISION)
    return jnp.exp(raised - 0.5 * lax.optimization_barrier(jnp.sum(scaled * scaled, axis=-1, keepdims=True))) * feats ** (-0.5)

def doc_masks(lengths, first_row, row_count):
    doc_ends = jnp.cumsum(lengths, dtype=jnp.int32)
    starts = doc_ends - lengths
    positions = first_row + jnp.arange(row_count, dtype=jnp.int32)
    begun_at = starts[None, :] <= positions[:, None]
    doc_ids = lax.optimization_barrier(jnp.sum(begun_at.astype(jnp.int32), axis=1))
    order_idx = jnp.arange(row_count, dtype=jnp.int32)
    same_doc = ((doc_ids[:, None] == doc_ids[None, :]) & (order_idx[None, :] <= order_idx[:, None])).astype(jnp.float32)
    inside = (starts >= first_row) & (starts < first_row + row_count)
    mask_per_head = (lax.optimization_barrier(jnp.sum((begun_at & inside[None, :]).astype(jnp.int32), axis=1)) == 0).astype(jnp.float32)
    tail_mask = (lax.optimization_barrier(jnp.sum((~begun_at & inside[None, :]).astype(jnp.int32), axis=1)) == 0).astype(jnp.float32)
    kept_flag = (jnp.sum(inside.astype(jnp.int32)) == 0).astype(jnp.float32)
    return (same_doc, mask_per_head, tail_mask, kept_flag)

def attend(query_features, feats_k, value_heads, incoming_state, norm_in, same_doc, mask_per_head):
    scores = jnp.einsum('thm,shm->hts', query_features, feats_k, precision=HIGH_PRECISION) * same_doc[None]
    attention_numerator = jnp.einsum('hts,shd->thd', scores, value_heads, precision=HIGH_PRECISION)
    attention_numerator = attention_numerator + mask_per_head[:, None, None] * jnp.einsum('kec,ecz->kez', query_features, incoming_state, precision=HIGH_PRECISION)
    denominator = lax.optimization_barrier(jnp.sum(scores, axis=2)).T + mask_per_head[:, None] * jnp.einsum('thm,hm->th', query_features, norm_in, precision=HIGH_PRECISION)
    return (attention_numerator / denominator[:, :, None]).reshape(query_features.shape[0], -1)

def tail_sums(feats_k, value_heads, tail_mask):
    weighted_values = feats_k * tail_mask[:, None, None]
    return (jnp.einsum('zlu,zlv->luv', weighted_values, value_heads, precision=HIGH_PRECISION), lax.optimization_barrier(jnp.sum(weighted_values, axis=0)))

def linear_attention(query_features, feats_k, values, lengths):
    row_total, heads, width = query_features.shape
    depth = values.shape[1] // heads
    blocks = row_total // ROWS

    def block(carried, block_in):
        incoming_state, norm_in = carried
        part_q, part_k, part_v, first_row = block_in
        same_doc, mask_per_head, tail_mask, kept_flag = doc_masks(lengths, first_row, ROWS)
        value_heads = part_v.reshape(ROWS, heads, depth)
        mixed_heads = attend(part_q, part_k, value_heads, incoming_state, norm_in, same_doc, mask_per_head)
        state_tail, norm_tail = tail_sums(part_k, value_heads, tail_mask)
        return ((kept_flag * incoming_state + state_tail, kept_flag * norm_in + norm_tail), mixed_heads)
    start_state = (jnp.zeros((heads, width, depth), jnp.float32), jnp.zeros((heads, width), jnp.float32))
    starts = jnp.arange(blocks, dtype=jnp.int32) * ROWS
    block_data = (query_features.reshape(blocks, ROWS, heads, width), feats_k.reshape(blocks, ROWS, heads, width), values.reshape(blocks, ROWS, -1), starts)
    _, mixed = lax.scan(jax.checkpoint(block), start_state, block_data)
    return mixed.reshape(row_total, -1)

def layer_apply(row_in, weights, projection, lengths):
    w_query, w_key, w_value, w_out, w_up, w_down, gain_attn, gain_ffn = [low(part) for part in weights]
    h_attn = low(norm_rows(row_in) * gain_attn)
    queries = low_back(product(h_attn, w_query))
    keys_out = low_back(product(h_attn, w_key))
    values = low_back(product(h_attn, w_value))
    attended = linear_attention(lift(queries, projection), lift(keys_out, projection), values, lengths)
    mixed = low(attended)
    branch = row_in + low_back(product(mixed, w_out))
    h_ffn = low(norm_rows(branch) * gain_ffn)
    hidden = low(jax.nn.gelu(low_back(product(h_ffn, w_up))))
    return branch + low_back(product(hidden, w_down))

def reference(inputs, cotangent, doc_lengths, feature_proj, w_query, w_key, w_value, w_out, w_up, w_down, gain_attn, gain_ffn):
    params = (w_query, w_key, w_value, w_out, w_up, w_down, gain_attn, gain_ffn)
    first_layer = tuple((part[0] for part in params))
    second_layer = tuple((part[1] for part in params))
    rows_all = inputs.astype(jnp.float32).reshape(MB * PACKS, PACK_LEN, D)
    cots_all = cotangent.astype(jnp.float32).reshape(MB * PACKS, PACK_LEN, D)
    lengths_all = doc_lengths.reshape(MB * PACKS, NDOCS)

    def whole(row_in, mid_offset, layer_one, layer_two, lengths):
        first_out = layer_apply(row_in, layer_one, feature_proj[0], lengths)
        middle = low(low_back(first_out + mid_offset))
        return (middle, layer_apply(middle, layer_two, feature_proj[1], lengths))

    def per_row(summed, row_data):
        row_in, row_cot, lengths = row_data
        mid_offset = jnp.zeros_like(row_in)
        outs_pair, pull_back = jax.vjp(lambda a, b, c, d: whole(a, b, c, d, lengths), row_in, mid_offset, first_layer, second_layer)
        middle, final_out = outs_pair
        grad_inputs, grad_middle, grads_one, grads_two = pull_back((jnp.zeros_like(middle), row_cot))
        summed = jax.tree.map(lambda s, t: s + t, summed, (grads_one, grads_two))
        return (summed, (middle, final_out, grad_inputs, grad_middle))
    zero_sums = jax.tree.map(jnp.zeros_like, (first_layer, second_layer))
    grads, rows_out = lax.scan(per_row, zero_sums, (rows_all, cots_all, lengths_all))
    middle, final_out, grad_inputs, grad_middle = rows_out
    shape_out = (2, MB, PACKS, PACK_LEN, D)
    activations = jnp.stack([middle, final_out]).reshape(shape_out).astype(jnp.bfloat16)
    input_grad = jnp.stack([grad_inputs, grad_middle]).reshape(shape_out).astype(jnp.bfloat16)

    def paired(index):
        return jnp.stack([grads[0][index], grads[1][index]])
    return (activations, input_grad, paired(0), paired(1), paired(2), paired(3), paired(4), paired(5), paired(6), paired(7))
```

```python
import functools

import jax
import jax.numpy as jnp
from jax import lax
from jax.experimental import pallas as pl
from jax.experimental.pallas import tpu as pltpu
from jax.sharding import PartitionSpec as P

MESH = pl.DeviceIdType.MESH
F32 = jnp.float32
BF16 = jnp.bfloat16
VMEM_LIMIT = 63 << 20

ROW_Q, ROW_K, ROW_V, ROW_O, ROW_UP, ROW_DOWN, SLAB = 32, 64, 96, 128, 160, 288, 416
PORTIONS = ((0, 64), (128, 144))


def dot(a, b):
    return lax.dot_general(a, b, (((1,), (0,)), ((), ())), preferred_element_type=F32)


def dot_nt(a, b):
    return lax.dot_general(a, b, (((1,), (1,)), ((), ())), preferred_element_type=F32)


def dot_tn(a, b):
    return lax.dot_general(a, b, (((0,), (0,)), ((), ())), preferred_element_type=F32)


def remote(src, dst, ssem, rsem, dev):
    return pltpu.make_async_remote_copy(
        src_ref=src, dst_ref=dst, send_sem=ssem, recv_sem=rsem, device_id=dev, device_id_type=MESH
    )


class Place:
    def __init__(self):
        self.c = lax.axis_index("section")
        self.d = lax.axis_index("dp")
        self.z = lax.axis_index("seq")
        self.o = 1 - self.c
        self.xn = self.d + 1 - 2 * lax.rem(self.d, 2)
        self.yn = lax.rem(self.d + 2, 4)
        self.first = self.xn + self.c * (self.yn - self.xn)
        self.second = self.yn + self.c * (self.xn - self.yn)
        self.diag = 3 - self.d
        self.me = self.d * 4 + self.z

    def at(self, d, z):
        return (self.c, d, z)

    def sibling(self):
        return (self.o, self.d, self.z)

    def peers(self):
        out = [self.sibling(), self.at(self.xn, self.z), self.at(self.yn, self.z)]
        return out + [self.at(self.d, lax.rem(self.z + k, 4)) for k in (1, 2, 3)]

    def barrier(self):
        bar = pltpu.get_barrier_semaphore()
        peers = self.peers()
        for dev in peers:
            pl.semaphore_signal(bar, inc=1, device_id=dev, device_id_type=MESH)
        pl.semaphore_wait(bar, len(peers))


def weight(G, l, row, n=32):
    return G[l, :, row : row + n, :].reshape(16 * n, 512)


class Gather:
    def __init__(self, pc, G, l, por, ssem, rsem, dsend, drecv):
        base, self.n = PORTIONS[por]
        self.pc, self.G, self.l, self.por = pc, G, l, por
        self.sems = ssem, rsem, dsend, drecv
        self.start = pl.multiple_of(base + pc.c * self.n, 16)
        self.other = pl.multiple_of(base + pc.o * self.n, 16)

    def ref(self, g):
        return self.G.at[self.l, g, pl.ds(self.start, self.n)]

    def link(self, g, i, dev):
        ssem, rsem, _, _ = self.sems
        return remote(self.ref(g), self.ref(g), ssem.at[self.l, self.por, i], rsem.at[self.l, self.por, g], dev)

    def sib(self, g):
        _, _, dsend, drecv = self.sems
        return remote(
            self.ref(g), self.ref(g), dsend.at[self.l, self.por, g], drecv.at[self.l, self.por, g], self.pc.sibling()
        )

    def arrive(self, g):
        self.link(g, 0, self.pc.sibling()).wait_recv()

    def own(self):
        pc = self.pc
        for k in (2, 1, 3):
            self.link(pc.me, k, pc.at(pc.d, lax.rem(pc.z + k, 4))).start()
        self.link(pc.me, 4, pc.at(pc.first, pc.z)).start()
        self.link(pc.me, 8, pc.at(pc.second, pc.z)).start()

    def column(self, k):
        pc = self.pc

        def step():
            g = pc.d * 4 + lax.rem(pc.z + k, 4)
            self.arrive(g)
            self.link(g, 4 + k, pc.at(pc.first, pc.z)).start()
            self.link(g, 8 + k, pc.at(pc.second, pc.z)).start()
            self.sib(g).start()

        if not isinstance(k, int):
            pl.when(k > 0)(step)
        elif k > 0:
            step()

    def across(self, k):
        pc = self.pc
        g = pc.first * 4 + lax.rem(pc.z + k, 4)
        self.arrive(g)
        self.link(g, 12 + k, pc.at(pc.second, pc.z)).start()
        self.sib(g).start()

    def far(self, k):
        pc = self.pc
        zz = lax.rem(pc.z + k, 4)
        for dp in (pc.second, pc.diag):
            g = dp * 4 + zz
            self.arrive(g)
            self.sib(g).start()

    def finish(self):
        _, _, dsend, drecv = self.sems
        pc = self.pc

        def wait(g):
            ref = self.G.at[self.l, g, pl.ds(self.other, self.n)]
            remote(ref, ref, dsend.at[self.l, self.por, g], drecv.at[self.l, self.por, g], pc.sibling()).wait_recv()

        def step(i, _):
            wait(lax.rem(pc.me + 1 + i, 16))
            return 0

        lax.fori_loop(0, 15, step, 0)

    def drain(self):
        pc = self.pc

        def step(i, _):
            self.link(pc.me, 1 + i, pc.at(pc.first, pc.z)).wait_send()
            self.sib(lax.rem(pc.me + 1 + i, 16)).wait_send()
            return 0

        lax.fori_loop(0, 15, step, 0)


def last_start(lengths, c, first_row, pos):
    starts = []
    at = 0
    for i in range(3):
        at = at + lengths[c, 0, i]
        starts.append(at - first_row)
    out = jnp.full(pos.shape, -first_row, jnp.int32)
    for s in starts:
        out = jnp.where(pos >= s, s, out)
    return out, starts


def norm(x):
    c = x - jnp.mean(x, axis=-1, keepdims=True)
    rstd = lax.rsqrt(jnp.mean(c * c, axis=-1, keepdims=True) + 1e-05)
    return c * rstd, rstd


def lane_low(shape):
    return lax.rem(lax.broadcasted_iota(jnp.int32, shape, 1), 128) < 64


def lift_pair(w, proj):
    hi = w.astype(BF16)
    low = (w - hi.astype(F32)).astype(BF16)
    sq = (w * w).astype(BF16)
    e = dot(jnp.concatenate([hi, sq, low, hi], axis=1), proj)
    return (jnp.exp(e) * 0.0625).astype(BF16)


def forward_kernel(
    inputs, lengths, wq_in, wk_in, wv_in, wo_in, wup_in, wdown_in, gains_in, proj,
    act, G_out, fq_out, fk_out, v_out, att_out, rden_out, branch_out, w_out, x_out, sin_out, pb_out,
    G, px, pk, mask, xbuf, hbuf, qbuf, kbuf, fq, fk, vext, att, rden, branch, wqk, xin, sin, tail, sbuf,
    gains, ybuf, hf, acc,
    ssem, rsem, dsend, drecv, osem, osem2, psem, csend, crecv, asem, wsem,
):
    pc = Place()
    c, z = pc.c, pc.z
    G[c, pc.me, 0:ROW_Q, :] = gains_in[...]
    for ref, row in ((wq_in, ROW_Q), (wk_in, ROW_K), (wv_in, ROW_V), (wo_in, ROW_O)):
        G[c, pc.me, row : row + 32, :] = ref[0].astype(BF16)
    for j in range(4):
        row = ROW_UP + 32 * j
        G[c, pc.me, row : row + 32, :] = wup_in[0, :, 512 * j : 512 * j + 512].astype(BF16)
    G[c, pc.me, ROW_DOWN:SLAB, :] = wdown_in[0].astype(BF16)
    hi = proj[0].astype(BF16)
    px[c, 0] = hi
    px[c, 1] = (proj[0] - hi.astype(F32)).astype(BF16)
    pc.barrier()
    halves = {}
    for por, (base, n) in enumerate(PORTIONS):
        for half, at in ((0, pc.o), (1, c)):
            ref = G.at[c, pc.me, pl.ds(pl.multiple_of(base + at * n, 16), n)]
            halves[por, half] = remote(ref, ref, osem2.at[0, por, half], osem2.at[1, por, half], pc.sibling())
            halves[por, half].start()
    psend = remote(px.at[c], px.at[c], psem.at[0], psem.at[1], pc.sibling())
    psend.start()
    moves = {
        (l, por): Gather(pc, G, l, por, ssem, rsem, dsend, drecv) for l in (0, 1) for por in range(2)
    }

    def four(step):
        for k in range(4):
            step(k)

    for por in (0, 1):
        for half in (0, 1):
            halves[por, half].wait()
    moves[0, 0].own()

    first_row = z * 512
    rows = lax.broadcasted_iota(jnp.int32, (512, 512), 0)
    cols = lax.broadcasted_iota(jnp.int32, (512, 512), 1)
    begin, starts = last_start(lengths, c, first_row, rows)
    mask[...] = ((cols <= rows) & (cols >= begin)).astype(F32)
    prow = lax.broadcasted_iota(jnp.int32, (512, 1), 0)
    begin_col, _ = last_start(lengths, c, first_row, prow)
    head_mask = (begin_col < 0).astype(F32)
    lane = lax.broadcasted_iota(jnp.int32, (1, 512), 1)
    inner = [jnp.where((s < 512) & (s >= 0), s, 0) for s in starts]
    cut = jnp.maximum(jnp.maximum(inner[0], inner[1]), inner[2])
    tail_mask = (lane >= cut).astype(F32)

    moves[0, 1].own()
    psend.wait()
    pk[...] = jnp.zeros_like(pk)
    for l in (0, 1):
        for p in range(4):
            for h in (0, 1):
                at = slice(64 * h, 64 * h + 64)
                to = slice(256 * h, 256 * h + 256)
                pk[l, p, at, to] = px[l, 0, 2 * p + h]
                pk[l, p, 128 + 64 * h : 192 + 64 * h, to] = jnp.full((64, 256), -0.5, BF16)
                pk[l, p, 256 + 64 * h : 320 + 64 * h, to] = px[l, 0, 2 * p + h]
                pk[l, p, 384 + 64 * h : 448 + 64 * h, to] = px[l, 1, 2 * p + h]
    vext[:, :, :, 128:] = jnp.ones((2, 4, 512, 128), BF16)

    @pl.when(z == 0)
    def _():
        sin[...] = jnp.zeros_like(sin)

    xbuf[...] = inputs[c, 0].astype(F32)
    four(moves[0, 0].column)
    moves[1, 0].own()
    four(moves[0, 0].across)
    moves[1, 1].own()
    four(moves[0, 1].column)
    four(moves[0, 0].far)
    four(moves[0, 1].across)
    moves[0, 0].finish()
    below = (c, pc.d, jnp.minimum(z + 1, 3))
    low = lane_low((512, 128))
    row_low = lax.broadcasted_iota(jnp.int32, (144, 256), 0)
    tail_is_first = (row_low < 64) | ((row_low >= 128) & (row_low < 136))
    low256 = lane_low((256, 128))

    def chain(l, p):
        return remote(sbuf.at[l, p], sin.at[l, p], csend.at[l, p], crecv.at[l, p], below)

    def layer(l, during):
        gains[...] = jnp.sum(G[l, :, 0:16, :].astype(F32), axis=0)

        def norm_tile(i, _):
            at = pl.ds(pl.multiple_of(i * 128, 128), 128)
            x = xbuf[at, :]
            xin[l, at, :] = x.astype(BF16)
            hbuf[at, :] = (norm(x)[0] * gains[0:1, :]).astype(BF16)
            return 0

        lax.fori_loop(0, 4, norm_tile, 0)
        scale = 64 ** (-0.25)
        kbuf[...] = dot(hbuf[...], weight(G, l, ROW_K)) * scale
        qbuf[...] = dot(hbuf[...], weight(G, l, ROW_V))

        def key_pair(p, _):
            if "key" in during:
                during["key"](p)
            at = pl.ds(pl.multiple_of(p * 128, 128), 128)
            w = kbuf[:, at]
            wqk[l, 1, p] = w.astype(BF16)
            f = lift_pair(w, pk[l, p])
            fk[l, p] = f
            v = qbuf[:, at]
            vext[l, p, :, 0:128] = v.astype(BF16)
            vt = jnp.concatenate([v.T * tail_mask, jnp.broadcast_to(tail_mask, (16, 512))], axis=0).astype(BF16)
            t = jnp.where(tail_is_first, dot(vt, f[:, 0:256]), dot(vt, f[:, 256:512]))
            tail[p] = t

            @pl.when(z == 0)
            def _():
                sbuf[l, p] = t.astype(BF16)
                chain(l, p).start()

            return 0

        lax.fori_loop(0, 4, key_pair, 0)
        qbuf[...] = dot(hbuf[...], weight(G, l, ROW_Q)) * scale

        def query_pair(p, _):
            if "query" in during:
                during["query"](p)
            at = pl.ds(pl.multiple_of(p * 128, 128), 128)
            w = qbuf[:, at]
            wqk[l, 0, p] = w.astype(BF16)
            fq[l, p] = lift_pair(w, pk[l, p])
            return 0

        lax.fori_loop(0, 4, query_pair, 0)

        def attend_pair(p, _):
            if "attend" in during:
                during["attend"](p)
            at = pl.ds(pl.multiple_of(p * 128, 128), 128)

            @pl.when(z > 0)
            def _():
                chain(l, p).wait_recv()

            @pl.when((z > 0) & (z < 3))
            def _():
                sbuf[l, p] = (tail[p] + sin[l, p].astype(F32)).astype(BF16)
                chain(l, p).start()

            for t in (0, 1):
                n = 256 * (t + 1)
                tr = slice(256 * t, 256 * t + 256)
                res = []
                for h in (0, 1):
                    fl = slice(256 * h, 256 * h + 256)
                    fqh = fq[l, p, tr, fl]
                    a = (dot_nt(fqh, fk[l, p, 0:n, fl]) * mask[tr, 0:n]).astype(BF16)
                    zrow = sin[l, p, 128:144, :].astype(F32)[8 * h : 8 * h + 1, :]
                    st = jnp.concatenate(
                        [sin[l, p, 0:128, :], jnp.broadcast_to(zrow, (128, 256)).astype(BF16)], axis=0
                    )
                    res.append(dot(a, vext[l, p, 0:n, :]) + head_mask[tr, :] * dot_nt(fqh, st))
                num = jnp.where(low256, res[0][:, 0:128], res[1][:, 0:128])
                den = jnp.where(low256, res[0][:, 128:256], res[1][:, 128:256])
                r = 1.0 / den
                att[l, tr, at] = num * r
                rden[l, tr, at] = r
            return 0

        lax.fori_loop(0, 4, attend_pair, 0)

        if "branch" in during:
            during["branch"]()

        def branch_tile(i, _):
            at = pl.ds(pl.multiple_of(i * 256, 256), 256)
            b = xbuf[at, :] + dot(att[l, at, :].astype(BF16), weight(G, l, ROW_O))
            branch[l, at, :] = b
            hf[at, :] = (norm(b)[0] * gains[1:2, :]).astype(BF16)
            acc[at, :] = b
            return 0

        lax.fori_loop(0, 2, branch_tile, 0)

        def ffn_tile(j, _):
            if "ffn" in during:
                during["ffn"](j)
            up = G[l, :, pl.ds(pl.multiple_of(ROW_UP + 32 * j, 32), 32), :].reshape(512, 512)
            down = G[l, pl.ds(4 * j, 4), ROW_DOWN:SLAB, :].reshape(512, 512)
            for i in (0, 1):
                at = slice(256 * i, 256 * i + 256)
                pre = dot(hf[at, :], up)
                hid = jax.nn.gelu(pre).astype(BF16)
                acc[at, :] += dot(hid, down)
            return 0

        lax.fori_loop(0, 4, ffn_tile, 0)
        y = acc[...].astype(BF16)
        ybuf[l] = y
        xbuf[...] = y.astype(F32)
        for i, (src, dst) in enumerate(saved):
            pltpu.make_async_copy(src.at[l], dst.at[l], wsem.at[l, i]).start()

    saved = (
        (G, G_out), (fq, fq_out), (fk, fk_out), (vext, v_out), (att, att_out), (rden, rden_out),
        (branch, branch_out), (wqk, w_out), (xin, x_out), (sin, sin_out),
    )

    def before_branch(l):
        if l == 0:
            four(moves[0, 1].far)
        moves[l, 1].finish()

    layer(0, {"key": moves[1, 0].column, "query": moves[1, 1].column, "attend": moves[1, 0].across,
              "branch": lambda: before_branch(0), "ffn": moves[1, 1].across})
    four(moves[1, 0].far)
    moves[1, 0].finish()
    layer(1, {"query": moves[1, 1].far, "branch": lambda: before_branch(1)})
    keep = pltpu.make_async_copy(pk.at[:, :, 0:256, :], pb_out, osem)
    keep.start()
    own_act = pltpu.make_async_copy(ybuf.at[c], act.at[c], asem.at[0])
    own_act.start()
    far_act = remote(ybuf.at[pc.o], act.at[c], asem.at[1], asem.at[2], pc.sibling())
    far_act.start()
    own_act.wait()
    far_act.wait()
    keep.wait()
    for l in (0, 1):
        for i, (src, dst) in enumerate(saved):
            pltpu.make_async_copy(src.at[l], dst.at[l], wsem.at[l, i]).wait()

    @pl.when(z < 3)
    def _():
        for l in (0, 1):
            for p in range(4):
                chain(l, p).wait_send()

    for move in moves.values():
        move.drain()


def forward_call(inputs, lengths, weights, gain_rows, proj):
    sds = jax.ShapeDtypeStruct
    dma = pltpu.SemaphoreType.DMA
    vm = pl.BlockSpec(memory_space=pltpu.VMEM)
    hbm = pl.BlockSpec(memory_space=pl.ANY)
    saved = [
        sds((2, 16, SLAB, 512), BF16), sds((2, 4, 512, 512), BF16), sds((2, 4, 512, 512), BF16),
        sds((2, 4, 512, 256), BF16), sds((2, 512, 512), F32), sds((2, 512, 512), F32), sds((2, 512, 512), F32),
        sds((2, 2, 4, 512, 128), BF16), sds((2, 512, 512), BF16), sds((2, 4, 144, 256), BF16),
        sds((2, 4, 256, 512), BF16),
    ]
    scratch = [
        pltpu.VMEM((2, 16, SLAB, 512), BF16),
        pltpu.VMEM((2, 2, 8, 64, 256), BF16),
        pltpu.VMEM((2, 4, 512, 512), BF16),
        pltpu.VMEM((512, 512), F32),
        pltpu.VMEM((512, 512), F32),
        pltpu.VMEM((512, 512), BF16),
        pltpu.VMEM((512, 512), F32),
        pltpu.VMEM((512, 512), F32),
        pltpu.VMEM((2, 4, 512, 512), BF16),
        pltpu.VMEM((2, 4, 512, 512), BF16),
        pltpu.VMEM((2, 4, 512, 256), BF16),
        pltpu.VMEM((2, 512, 512), F32),
        pltpu.VMEM((2, 512, 512), F32),
        pltpu.VMEM((2, 512, 512), F32),
        pltpu.VMEM((2, 2, 4, 512, 128), BF16),
        pltpu.VMEM((2, 512, 512), BF16),
        pltpu.VMEM((2, 4, 144, 256), BF16),
        pltpu.VMEM((4, 144, 256), F32),
        pltpu.VMEM((2, 4, 144, 256), BF16),
        pltpu.VMEM((16, 512), F32),
        pltpu.VMEM((2, 512, 512), BF16),
        pltpu.VMEM((512, 512), BF16),
        pltpu.VMEM((512, 512), F32),
        dma((2, 2, 16)), dma((2, 2, 16)), dma((2, 2, 16)), dma((2, 2, 16)), dma, dma((2, 2, 2)), dma((2,)),
        dma((2, 4)), dma((2, 4)), dma((3,)), dma((2, 10)),
    ]
    return pl.pallas_call(
        forward_kernel,
        out_shape=[sds((2, 512, 512), BF16)] + saved,
        in_specs=[vm, pl.BlockSpec(memory_space=pltpu.SMEM)] + [vm] * 8,
        out_specs=[vm] + [hbm] * len(saved),
        scratch_shapes=scratch,
        compiler_params=pltpu.CompilerParams(
            collective_id=0, has_side_effects=True, vmem_limit_bytes=VMEM_LIMIT
        ),
        name="forward",
    )(inputs, lengths, *weights, gain_rows, proj)


def make_gain_rows(gain_attn, gain_ffn):
    g = lax.axis_index("dp") * 4 + lax.axis_index("seq")
    lane = lax.broadcasted_iota(jnp.int32, (1, 512), 1)
    mine = lane // 32 == g

    def gain_row(gain):
        return jnp.where(mine, jnp.tile(gain[None, :].astype(BF16), (1, 16)), jnp.zeros((), BF16))

    return jnp.concatenate([gain_row(gain_attn), gain_row(gain_ffn), jnp.zeros((30, 512), BF16)], axis=0)


def gelu_parts(x):
    k = 0.7978845608028654
    x2 = x * x
    t = jnp.tanh(k * x * (1.0 + 0.044715 * x2))
    half = 0.5 * (1.0 + t)
    return x * half, half + 0.5 * x * (1.0 - t * t) * k * (1.0 + 0.134145 * x2)


def norm_back(y, rstd, dy):
    m1 = jnp.mean(dy, axis=-1, keepdims=True)
    m2 = jnp.mean(dy * y, axis=-1, keepdims=True)
    return rstd * (dy - m1 - y * m2)


HALF = SLAB // 2
SUM_PORTIONS = ((ROW_UP, 128), (0, 80))


class Sums:
    def __init__(self, pc, slabs, bufs, sems, l, por):
        base, self.n = SUM_PORTIONS[por]
        self.pc, self.slabs, self.l, self.por = pc, slabs, l, por
        self.sb, self.r1, self.r2, self.r3, self.keep = bufs
        self.sems = sems
        self.mine = pl.multiple_of(base + pc.c * self.n, 16)
        self.other = pl.multiple_of(base + pc.o * self.n, 16)
        self.at = pl.ds(sum(2 * n for _, n in SUM_PORTIONS[:por]) // 2, self.n)

    def copy(self, i, j, src, dst, dev):
        ssem, rsem = self.sems
        return remote(src, dst, ssem.at[self.l, self.por, i, j], rsem.at[self.l, self.por, i, j], dev)

    def to_sibling(self, g):
        src = self.slabs.at[self.l, g, pl.ds(self.other, self.n)]
        return self.copy(0, g, src, self.sb.at[self.l, g, self.at], self.pc.sibling())

    def to_second(self, j, zz, g):
        src, dst = self.sb.at[self.l, g, self.at], self.r1.at[self.l, j, zz, self.at]
        return self.copy(1, 4 * j + zz, src, dst, self.pc.at(self.pc.second, self.pc.z))

    def to_first(self, zz, g):
        src, dst = self.sb.at[self.l, g, self.at], self.r2.at[self.l, zz, self.at]
        return self.copy(2, zz, src, dst, self.pc.at(self.pc.first, self.pc.z))

    def along(self, k, g):
        src, dst = self.sb.at[self.l, g, self.at], self.r3.at[self.l, 3 - k, self.at]
        return self.copy(3, 3 - k, src, dst, self.pc.at(self.pc.d, lax.rem(self.pc.z + k, 4)))

    def begin(self):
        pc = self.pc
        for col in (pc.diag, pc.second, pc.first, pc.d):
            for k in (1, 2, 3, 0):
                self.to_sibling(col * 4 + lax.rem(pc.z + k, 4)).start()

    def pair(self, g):
        self.to_sibling(g).wait_recv()
        own = self.slabs[self.l, g, pl.ds(self.mine, self.n), :]
        return own.astype(F32) + self.sb[self.l, g, self.at, :].astype(F32)

    def stage1(self, j, i):
        pc = self.pc
        zz = lax.rem(pc.z + 1 + i, 4)
        g = (pc.diag if j == 0 else pc.second) * 4 + zz
        self.sb[self.l, g, self.at, :] = self.pair(g).astype(BF16)
        self.to_second(j, zz, g).start()

    def stage2(self, i):
        pc = self.pc
        zz = lax.rem(pc.z + 1 + i, 4)
        g = pc.first * 4 + zz
        s = self.pair(g)
        self.to_second(0, zz, g).wait_recv()
        self.sb[self.l, g, self.at, :] = (s + self.r1[self.l, 0, zz, self.at, :].astype(F32)).astype(BF16)
        self.to_first(zz, g).start()

    def stage3(self, k):
        pc = self.pc
        zz = lax.rem(pc.z + k, 4)
        g = pc.d * 4 + zz
        s = self.pair(g)
        self.to_second(1, zz, g).wait_recv()
        s = s + self.r1[self.l, 1, zz, self.at, :].astype(F32)
        self.to_first(zz, g).wait_recv()
        s = s + self.r2[self.l, zz, self.at, :].astype(F32)
        if k:
            self.sb[self.l, g, self.at, :] = s.astype(BF16)
            self.along(k, g).start()
        else:
            self.keep[self.l, self.at, :] = s

    def stage4(self, l):
        s = self.keep[l, self.at, :]
        for i in range(3):
            s = s + self.r3[l, i, self.at, :].astype(F32)
        return s

    def arrive(self):
        for k in (1, 2, 3):
            self.along(k, self.pc.me).wait_recv()

    def drain(self):
        for i in range(16):
            self.to_sibling(i).wait_send()
        for j in (0, 1):
            for zz in range(4):
                self.to_second(j, zz, 0).wait_send()
        for zz in range(4):
            self.to_first(zz, 0).wait_send()
        for k in (1, 2, 3):
            self.along(k, 0).wait_send()


def backward_kernel(
    cotangent, lengths, G_in, fq_in, fk_in, v_in, att_in, rden_in, branch_in, w_in, x_in, sin_in, pb_in,
    gin, gq_out, gk_out, gv_out, go_out, gup_out, gdown_out, gg_out,
    G, fq, fk, vext, att, rden, branch, wqk, xin, sin, pb,
    mask, mask_t, gbuf, gbr, hbuf, hT, gb, dh, gq, gk, gv, le, rin, rtail, rbuf, gains, gsum, xout, slabs,
    sb, r1, r2, r3, keep, total,
    lsem, csend, crecv, asem, ssem, rsem, fsem,
):
    pc = Place()
    c, z = pc.c, pc.z
    loads = (
        (G_in, G), (fq_in, fq), (fk_in, fk), (v_in, vext), (att_in, att), (rden_in, rden), (branch_in, branch),
        (w_in, wqk), (x_in, xin), (sin_in, sin), (pb_in, pb),
    )

    def load(l, i):
        src, dst = loads[i]
        return pltpu.make_async_copy(src.at[l], dst, lsem.at[i])

    pc.barrier()
    for i in range(len(loads)):
        load(1, i).start()

    first_row = z * 512
    rows = lax.broadcasted_iota(jnp.int32, (512, 512), 0)
    cols = lax.broadcasted_iota(jnp.int32, (512, 512), 1)
    begin, starts = last_start(lengths, c, first_row, rows)
    mask[...] = ((cols <= rows) & (cols >= begin)).astype(F32).astype(BF16)
    begin, _ = last_start(lengths, c, first_row, cols)
    mask_t[...] = ((rows <= cols) & (rows >= begin)).astype(F32).astype(BF16)
    prow = lax.broadcasted_iota(jnp.int32, (512, 1), 0)
    begin_col, _ = last_start(lengths, c, first_row, prow)
    head_col = (begin_col < 0).astype(F32)
    lane = lax.broadcasted_iota(jnp.int32, (1, 512), 1)
    begin_row, _ = last_start(lengths, c, first_row, lane)
    head_row = (begin_row < 0).astype(F32)
    inner = [jnp.where((s < 512) & (s >= 0), s, 0) for s in starts]
    cut = jnp.maximum(jnp.maximum(inner[0], inner[1]), inner[2])
    tail_col = (prow >= cut).astype(F32)

    @pl.when(z == 3)
    def _():
        rin[...] = jnp.zeros_like(rin)

    gbuf[...] = cotangent[c, 0].astype(F32)
    above = (c, pc.d, jnp.maximum(z - 1, 0))
    row_low = lax.broadcasted_iota(jnp.int32, (144, 256), 0)
    tail_is_first = (row_low < 64) | ((row_low >= 128) & (row_low < 136))
    low = lane_low((512, 128))
    ones_i = lax.broadcasted_iota(jnp.int32, (256, 128), 0)
    ones_j = lax.broadcasted_iota(jnp.int32, (256, 128), 1)
    head_ones = (lax.rem(ones_i, 128) // 64 == ones_j // 64).astype(BF16)
    scale = 64 ** (-0.25)

    def chain(l, p):
        return remote(rbuf.at[l, p], rin.at[l, p], csend.at[l, p], crecv.at[l, p], above)

    sums = {(l, por): Sums(pc, slabs, (sb, r1, r2, r3, keep), (ssem, rsem), l, por) for l in (0, 1) for por in (0, 1)}

    def put(l, row, n, value):
        slabs[l, :, row : row + n, :] = value.astype(BF16).reshape(16, n, 512)

    def layer(l, during):
        def at_point(name, *args):
            if name in during:
                during[name](*args)

        for i in range(len(loads)):
            load(l, i).wait()
        gains[...] = jnp.sum(G[:, 0:16, :].astype(F32), axis=0)
        gsum[...] = jnp.zeros_like(gsum)

        def norm_tile(i, _):
            at = pl.ds(pl.multiple_of(i * 128, 128), 128)
            hbuf[at, :] = (norm(branch[at, :])[0] * gains[1:2, :]).astype(BF16)
            gb[at, :] = gbuf[at, :].astype(BF16)
            return 0

        lax.fori_loop(0, 4, norm_tile, 0)
        hT[...] = hbuf[...].T
        dh[...] = jnp.zeros_like(dh)

        def ffn_tile(j, _):
            at_point("ffn", j)
            up_at = pl.ds(pl.multiple_of(ROW_UP + 32 * j, 32), 32)
            up = G[:, up_at, :].reshape(512, 512)
            down = G[pl.ds(4 * j, 4), ROW_DOWN:SLAB, :].reshape(512, 512)
            for i in (0, 1):
                at = slice(256 * i, 256 * i + 256)
                hid, slope = gelu_parts(dot(hbuf[at, :], up))
                gq[at, :] = hid.astype(BF16)
                gk[at, :] = (slope * dot_nt(gb[at, :], down)).astype(BF16)
            slabs[l, pl.ds(4 * j, 4), ROW_DOWN:SLAB, :] = dot_tn(gq[...], gb[...]).astype(BF16).reshape(4, 128, 512)
            g = gk[...]
            slabs[l, :, up_at, :] = dot(hT[...], g).astype(BF16).reshape(16, 32, 512)
            dh[...] += dot_nt(g, up)
            return 0

        lax.fori_loop(0, 4, ffn_tile, 0)

        sums[l, 0].begin()

        def branch_tile(i, _):
            at_point("branch", i)
            at = pl.ds(pl.multiple_of(i * 128, 128), 128)
            y, rstd = norm(branch[at, :])
            d = dh[at, :]
            gsum[1:2, :] += jnp.sum(d * y, axis=0, keepdims=True)
            g = gbuf[at, :] + norm_back(y, rstd, d * gains[1:2, :])
            gbr[at, :] = g
            gb[at, :] = g.astype(BF16)
            hbuf[at, :] = att[at, :].astype(BF16)
            return 0

        lax.fori_loop(0, 4, branch_tile, 0)
        put(l, ROW_O, 32, dot_tn(hbuf[...], gb[...]))
        dh[...] = dot_nt(gb[...], G[:, ROW_O : ROW_O + 32, :].reshape(512, 512))

        def tail_pair(p, _):
            at_point("tail", p)
            at = pl.ds(pl.multiple_of(p * 128, 128), 128)
            g = dh[:, at]
            r = rden[:, at]
            t = g * att[:, at]
            hi = t.astype(BF16)
            lo = (t - hi.astype(F32)).astype(BF16)
            dden = -dot(jnp.concatenate([hi, lo], axis=1), head_ones) * r
            dnum = g * r
            le[p] = jnp.concatenate([dnum, dden * (1.0 / 64.0)], axis=1).astype(BF16)
            dt = (dden.T) * head_row
            lhs = jnp.concatenate([dnum.T * head_row, dt[0:8], dt[64:72]], axis=0).astype(BF16)
            tl = jnp.where(tail_is_first, dot(lhs, fq[p, :, 0:256]), dot(lhs, fq[p, :, 256:512]))
            rtail[p] = tl

            @pl.when(z == 3)
            def _():
                rbuf[l, p] = tl.astype(BF16)
                chain(l, p).start()

            return 0

        lax.fori_loop(0, 4, tail_pair, 0)

        def attend_pair(p, _):
            at_point("attend", p)
            at = pl.ds(pl.multiple_of(p * 128, 128), 128)

            @pl.when(z < 3)
            def _():
                chain(l, p).wait_recv()

            @pl.when((z > 0) & (z < 3))
            def _():
                rbuf[l, p] = (rtail[p] + rin[l, p].astype(F32)).astype(BF16)
                chain(l, p).start()

            ve = vext[p]
            lep = le[p]
            dq, dk, dv = [], [], []
            for h in (0, 1):
                fl = slice(256 * h, 256 * h + 256)
                keep = lane_low((512, 256)) if h == 0 else jnp.logical_not(lane_low((512, 256)))
                leh = jnp.where(keep, lep, jnp.zeros((), BF16))
                fqh, fkh = fq[p, :, fl], fk[p, :, fl]
                zrow = sin[p, 128:144, :].astype(F32)[8 * h : 8 * h + 1, :]
                st = jnp.concatenate([sin[p, 0:128, :], jnp.broadcast_to(zrow, (128, 256)).astype(BF16)], axis=0)
                rrow = rin[l, p, 128:144, :].astype(F32)[8 * h : 8 * h + 1, :] * (1.0 / 128.0)
                rows_h = lax.broadcasted_iota(jnp.int32, (128, 256), 0) // 64 == h
                rt = jnp.where(rows_h, rin[l, p, 0:128, :], jnp.zeros((), BF16))
                rte = jnp.concatenate([rt, jnp.broadcast_to(rrow, (128, 256)).astype(BF16)], axis=0)
                dqh = head_col * dot(leh, st)
                da0 = dot_nt(leh[0:256], ve[0:256]).astype(BF16) * mask[0:256, 0:256]
                da1 = dot_nt(leh[256:512], ve).astype(BF16) * mask[256:512, :]
                dqh = dqh + jnp.concatenate([dot(da0, fkh[0:256]), dot(da1, fkh)], axis=0)
                at0 = dot_nt(fkh[0:256], fqh).astype(BF16) * mask_t[0:256, :]
                at1 = dot_nt(fkh[256:512], fqh[256:512]).astype(BF16) * mask_t[256:512, 256:512]
                dvh = tail_col * dot_nt(fkh, rin[l, p, 0:128, :])
                dvh = dvh + jnp.concatenate([dot(at0, lep[:, 0:128]), dot(at1, lep[256:512, 0:128])], axis=0)
                dt0 = dot_nt(ve[0:256], leh).astype(BF16) * mask_t[0:256, :]
                dt1 = dot_nt(ve[256:512], leh[256:512]).astype(BF16) * mask_t[256:512, 256:512]
                dkh = tail_col * dot(ve, rte)
                dkh = dkh + jnp.concatenate([dot(dt0, fqh), dot(dt1, fqh[256:512])], axis=0)
                dq.append((dqh * fqh.astype(F32)).astype(BF16))
                dk.append((dkh * fkh.astype(F32)).astype(BF16))
                dv.append(dvh)
            gv[:, at] = jnp.where(low, dv[0], dv[1]).astype(BF16)
            for k, e, out in ((0, dq, gq), (1, dk, gk)):
                gw = dot_nt(jnp.concatenate(e, axis=1), pb[p])
                gw = gw[:, 0:128] + 2.0 * wqk[k, p].astype(F32) * gw[:, 128:256]
                out[:, at] = (gw * scale).astype(BF16)
            return 0

        lax.fori_loop(0, 4, attend_pair, 0)

        def norm_tile2(i, _):
            at_point("norm", i)
            at = pl.ds(pl.multiple_of(i * 128, 128), 128)
            hbuf[at, :] = (norm(xin[at, :].astype(F32))[0] * gains[0:1, :]).astype(BF16)
            return 0

        lax.fori_loop(0, 4, norm_tile2, 0)
        hT[...] = hbuf[...].T
        for row, g in ((ROW_Q, gq), (ROW_K, gk), (ROW_V, gv)):
            put(l, row, 32, dot(hT[...], g[...]))
        dh[...] = dot_nt(gq[...], G[:, ROW_Q : ROW_Q + 32, :].reshape(512, 512))
        dh[...] += dot_nt(gk[...], G[:, ROW_K : ROW_K + 32, :].reshape(512, 512))
        dh[...] += dot_nt(gv[...], G[:, ROW_V : ROW_V + 32, :].reshape(512, 512))

        def out_tile(i, _):
            at_point("out", i)
            at = pl.ds(pl.multiple_of(i * 128, 128), 128)
            y, rstd = norm(xin[at, :].astype(F32))
            d = dh[at, :]
            gsum[0:1, :] += jnp.sum(d * y, axis=0, keepdims=True)
            g = (gbr[at, :] + norm_back(y, rstd, d * gains[0:1, :])).astype(BF16)
            xout[l, at, :] = g
            gbuf[at, :] = g.astype(F32)
            return 0

        lax.fori_loop(0, 4, out_tile, 0)
        slabs[l, :, 0:16, :] = jnp.broadcast_to(gsum[...].astype(BF16)[None], (16, 16, 512))
        slabs[l, :, 16:32, :] = jnp.zeros((16, 16, 512), BF16)

        sums[l, 1].begin()
        if l == 1:
            for i in range(len(loads)):
                load(0, i).start()


    def four(step, *args):
        for i in range(4):
            step(*args, i)

    layer(1, {"tail": lambda p: sums[1, 0].stage1(0, p), "attend": lambda p: sums[1, 0].stage1(1, p),
              "norm": sums[1, 0].stage2})
    for k in (1, 2, 3, 0):
        sums[1, 0].stage3(k)
    layer(0, {"ffn": lambda p: (sums[1, 1].stage1(0, p), sums[1, 1].stage1(1, p)), "branch": sums[1, 1].stage2,
              "tail": lambda p: sums[0, 0].stage1(0, p), "attend": lambda p: sums[0, 0].stage1(1, p),
              "norm": sums[0, 0].stage2})
    own_act = pltpu.make_async_copy(xout.at[c], gin.at[c], asem.at[0])
    own_act.start()
    far_act = remote(xout.at[pc.o], gin.at[c], asem.at[1], asem.at[2], pc.sibling())
    far_act.start()
    own_act.wait()
    far_act.wait()

    four(sums[0, 1].stage1, 0)
    four(sums[0, 1].stage1, 1)
    for k in (1, 2, 3, 0):
        sums[1, 1].stage3(k)
    for k in (1, 2, 3, 0):
        sums[0, 0].stage3(k)
    four(sums[0, 1].stage2)
    for k in (1, 2, 3, 0):
        sums[0, 1].stage3(k)
    for m in sums.values():
        m.arrive()
    for por in (0, 1):
        m = sums[0, por]
        gbr[m.at, :] = m.stage4(pc.o)
    parts = []
    for por in (0, 1):
        m = sums[0, por]
        part = remote(gbr.at[m.at], total.at[pl.ds(m.mine, m.n)], fsem.at[0, por], fsem.at[1, por], pc.sibling())
        part.start()
        parts.append(part)
    for por in (0, 1):
        m = sums[0, por]
        total[pl.ds(m.mine, m.n), :] = m.stage4(c)
    for part in parts:
        part.wait()
    for ref, row in ((gq_out, ROW_Q), (gk_out, ROW_K), (gv_out, ROW_V), (go_out, ROW_O)):
        ref[...] = total[row : row + 32, :]
    for j in range(4):
        gup_out[:, 512 * j : 512 * j + 512] = total[ROW_UP + 32 * j : ROW_UP + 32 * j + 32, :]
    gdown_out[...] = total[ROW_DOWN:SLAB, :]
    gg_out[...] = pltpu.roll(total[0:8, :], lax.rem(512 - 32 * pc.me, 512), 1)
    for m in sums.values():
        m.drain()

    @pl.when(z > 0)
    def _():
        for l in (0, 1):
            for p in range(4):
                chain(l, p).wait_send()


def backward_call(cotangent, lengths, saved):
    sds = jax.ShapeDtypeStruct
    dma = pltpu.SemaphoreType.DMA
    vm = pl.BlockSpec(memory_space=pltpu.VMEM)
    hbm = pl.BlockSpec(memory_space=pl.ANY)
    bufs = [pltpu.VMEM(a.shape[1:], a.dtype) for a in saved]
    full = (512, 512)
    scratch = bufs + [
        pltpu.VMEM(full, BF16),
        pltpu.VMEM(full, BF16),
        pltpu.VMEM(full, F32),
        pltpu.VMEM(full, F32),
        pltpu.VMEM(full, BF16),
        pltpu.VMEM(full, BF16),
        pltpu.VMEM(full, BF16),
        pltpu.VMEM(full, F32),
        pltpu.VMEM(full, BF16),
        pltpu.VMEM(full, BF16),
        pltpu.VMEM(full, BF16),
        pltpu.VMEM((4, 512, 256), BF16),
        pltpu.VMEM((2, 4, 144, 256), BF16),
        pltpu.VMEM((4, 144, 256), F32),
        pltpu.VMEM((2, 4, 144, 256), BF16),
        pltpu.VMEM((16, 512), F32),
        pltpu.VMEM((16, 512), F32),
        pltpu.VMEM((2, 512, 512), BF16),
        pltpu.VMEM((2, 16, SLAB, 512), BF16),
        pltpu.VMEM((2, 16, HALF, 512), BF16),
        pltpu.VMEM((2, 2, 4, HALF, 512), BF16),
        pltpu.VMEM((2, 4, HALF, 512), BF16),
        pltpu.VMEM((2, 3, HALF, 512), BF16),
        pltpu.VMEM((2, HALF, 512), F32),
        pltpu.VMEM((SLAB, 512), F32),
        dma((11,)), dma((2, 4)), dma((2, 4)), dma((3,)), dma((2, 2, 4, 16)), dma((2, 2, 4, 16)), dma((2, 2)),
    ]
    return pl.pallas_call(
        backward_kernel,
        out_shape=[sds((2, 512, 512), BF16)]
        + [sds((32, 512), F32)] * 4
        + [sds((32, 2048), F32), sds((128, 512), F32), sds((8, 512), F32)],
        in_specs=[vm, pl.BlockSpec(memory_space=pltpu.SMEM)] + [hbm] * len(saved),
        out_specs=[vm] * 8,
        scratch_shapes=scratch,
        compiler_params=pltpu.CompilerParams(
            collective_id=1, has_side_effects=True, vmem_limit_bytes=VMEM_LIMIT
        ),
        name="backward",
    )(cotangent, lengths, *saved)


def fast_local(inputs, cotangent, doc_lengths, feature_proj, *weights):
    gain_rows = make_gain_rows(weights[6][0], weights[7][0])
    outs = forward_call(inputs, doc_lengths, weights[:6], gain_rows, feature_proj)
    gin, *grads = backward_call(cotangent, doc_lengths, outs[1:])
    return (
        (outs[0][None, :, None], gin[None, :, None])
        + tuple(g[None] for g in grads[:6])
        + (grads[6][0:1, 0:32], grads[6][1:2, 0:32])
    )


HIGH_PRECISION = lax.Precision.HIGHEST


def prefix(shard, axis, join, neutral):
    place = lax.axis_index(axis)
    gathered = jax.tree.map(
        lambda a, kind: lax.all_gather(a.astype(kind), axis),
        shard,
        (jnp.bfloat16, jnp.bfloat16, jnp.bfloat16),
    )
    state = jax.tree.map(lambda a, e: jnp.zeros_like(a) + jnp.asarray(e, a.dtype), shard, neutral)

    def prefix_one(lap, state):
        return join(
            state,
            jax.tree.map(
                lambda a, own: lax.dynamic_index_in_dim(a, lap, 0, False).astype(own.dtype),
                gathered,
                shard,
            ),
        )

    return lax.fori_loop(0, place, prefix_one, state)


def entering(shard, axis, join, neutral):
    count = lax.axis_size(axis)
    place = lax.axis_index(axis)
    ahead = count - 1 - place
    gathered = jax.tree.map(
        lambda a, kind: lax.all_gather(a.astype(kind), axis),
        shard,
        jax.tree.map(lambda a: jnp.bfloat16 if a.dtype == jnp.float32 else a.dtype, shard),
    )
    state = jax.tree.map(lambda a, e: jnp.zeros_like(a) + jnp.asarray(e, a.dtype), shard, neutral)

    def entering_one(lap, state):
        source = count - 1 - lap
        return join(
            state,
            jax.tree.map(
                lambda a, own: lax.dynamic_index_in_dim(a, source, 0, False).astype(own.dtype),
                gathered,
                shard,
            ),
        )

    return lax.fori_loop(0, ahead, entering_one, state)


def as_sent(shard):

    def short(part):
        return part.astype(jnp.bfloat16) if part.dtype == jnp.float32 else part

    return jax.tree.map(short, shard)


def passed_along(block, axis, distance):
    devices = range(lax.axis_size(axis))
    route = [(i - distance, i) for i in devices if i - distance in devices]
    return lax.ppermute(block, axis, route)


def matmul(left, right):
    return jnp.dot(left, right, preferred_element_type=jnp.float32)


def norm_rows(values):
    centre = values - jnp.mean(values, axis=-1, keepdims=True)
    return centre * lax.rsqrt(jnp.mean(centre * centre, axis=-1, keepdims=True) + 1e-05)


def lift(values, projection):
    heads, depth, feats = projection.shape
    scaled = values.reshape(values.shape[0], heads, depth) * depth ** (-0.25)
    raised = jnp.einsum("nhd,hdm->nhm", scaled, projection, precision=HIGH_PRECISION)
    return jnp.exp(raised - 0.5 * jnp.sum(scaled * scaled, axis=-1, keepdims=True)) * feats ** (
        -0.5
    )


def doc_masks(lengths, first_row, row_count):
    doc_ends = jnp.cumsum(lengths, dtype=jnp.int32)
    starts = doc_ends - lengths
    positions = first_row + jnp.arange(row_count, dtype=jnp.int32)
    begun_at = starts[None, :] <= positions[:, None]
    doc_ids = jnp.sum(begun_at.astype(jnp.int32), axis=1)
    order_idx = jnp.arange(row_count, dtype=jnp.int32)
    same_doc = (
        (doc_ids[:, None] == doc_ids[None, :]) & (order_idx[None, :] <= order_idx[:, None])
    ).astype(jnp.float32)
    inside = (starts >= first_row) & (starts < first_row + row_count)
    mask_per_head = (jnp.sum((begun_at & inside[None, :]).astype(jnp.int32), axis=1) == 0).astype(
        jnp.float32
    )
    tail_mask = (jnp.sum((~begun_at & inside[None, :]).astype(jnp.int32), axis=1) == 0).astype(
        jnp.float32
    )
    kept_flag = (jnp.sum(inside.astype(jnp.int32)) == 0).astype(jnp.float32)
    return (same_doc, mask_per_head, tail_mask, kept_flag)


def attend(query_features, feats_k, value_heads, incoming_state, norm_in, same_doc, mask_per_head):
    scores = (
        jnp.einsum("thm,shm->hts", query_features, feats_k, precision=HIGH_PRECISION)
        * same_doc[None]
    )
    attention_numerator = jnp.einsum("hts,shd->thd", scores, value_heads, precision=HIGH_PRECISION)
    attention_numerator = attention_numerator + mask_per_head[:, None, None] * jnp.einsum(
        "kec,ecz->kez", query_features, incoming_state, precision=HIGH_PRECISION
    )
    denominator = jnp.sum(scores, axis=2).T + mask_per_head[:, None] * jnp.einsum(
        "thm,hm->th", query_features, norm_in, precision=HIGH_PRECISION
    )
    return (attention_numerator / denominator[:, :, None]).reshape(query_features.shape[0], -1)


def tail_sums(feats_k, value_heads, tail_mask):
    weighted_values = feats_k * tail_mask[:, None, None]
    return (
        jnp.einsum("zlu,zlv->luv", weighted_values, value_heads, precision=HIGH_PRECISION),
        jnp.sum(weighted_values, axis=0),
    )


def combine_carry(earlier, later_part):
    return (
        earlier[0] * later_part[0],
        later_part[1] + later_part[0] * earlier[1],
        later_part[2] + later_part[0] * earlier[2],
    )


def run_forward(layer_in, weights, projection, lengths, first_row):
    w_query, w_key, w_value, w_out, w_up, w_down, gain_attn, gain_ffn = weights
    row_count = layer_in.shape[0]
    same_doc, mask_per_head, tail_mask, kept_flag = doc_masks(lengths, first_row, row_count)
    h_attn = (norm_rows(layer_in) * gain_attn.astype(jnp.float32)).astype(jnp.bfloat16)
    query_features = lift(matmul(h_attn, w_query), projection)
    feats_k = lift(matmul(h_attn, w_key), projection)
    value_heads = matmul(h_attn, w_value).reshape(row_count, projection.shape[0], -1)
    state_tail, norm_tail = tail_sums(feats_k, value_heads, tail_mask)
    identity = (jnp.ones((), jnp.float32), jnp.zeros_like(state_tail), jnp.zeros_like(norm_tail))
    _, incoming_state, norm_in = prefix(
        (kept_flag, state_tail, norm_tail), "seq", combine_carry, identity
    )
    mixed_heads = attend(
        query_features, feats_k, value_heads, incoming_state, norm_in, same_doc, mask_per_head
    ).astype(jnp.bfloat16)
    branch = layer_in + matmul(mixed_heads, w_out)
    h_ffn = (norm_rows(branch) * gain_ffn.astype(jnp.float32)).astype(jnp.bfloat16)
    hidden = jax.nn.gelu(matmul(h_ffn, w_up)).astype(jnp.bfloat16)
    return (branch + matmul(hidden, w_down), incoming_state, norm_in)


def run_backward(
    layer_in, incoming_state, norm_in, grad_out, weights, projection, lengths, first_row
):
    w_query, w_key, w_value, w_out, w_up, w_down, gain_attn, gain_ffn = weights
    row_count = layer_in.shape[0]
    same_doc, mask_per_head, tail_mask, kept_flag = doc_masks(lengths, first_row, row_count)
    gain_a = gain_attn.astype(jnp.float32)
    gain_f = gain_ffn.astype(jnp.float32)
    normed_a, norm_a_back = jax.vjp(norm_rows, layer_in)
    h_attn = (normed_a * gain_a).astype(jnp.bfloat16)
    query_features, lift_q_back = jax.vjp(lambda z: lift(z, projection), matmul(h_attn, w_query))
    feats_k, lift_k_back = jax.vjp(lambda z: lift(z, projection), matmul(h_attn, w_key))
    value_heads = matmul(h_attn, w_value).reshape(row_count, projection.shape[0], -1)
    attended, attend_back = jax.vjp(
        lambda a, b, c, d, e: attend(a, b, c, d, e, same_doc, mask_per_head),
        query_features,
        feats_k,
        value_heads,
        incoming_state,
        norm_in,
    )
    mixed_heads = attended.astype(jnp.bfloat16)
    branch = layer_in + matmul(mixed_heads, w_out)
    normed_f, norm_f_back = jax.vjp(norm_rows, branch)
    h_ffn = (normed_f * gain_f).astype(jnp.bfloat16)
    activated, gelu_back = jax.vjp(jax.nn.gelu, matmul(h_ffn, w_up))
    hidden = activated.astype(jnp.bfloat16)
    grad_low = grad_out.astype(jnp.bfloat16)
    grad_wdown = matmul(hidden.T, grad_low)
    grad_pre = gelu_back(matmul(grad_low, w_down.T))[0].astype(jnp.bfloat16)
    grad_wup = matmul(h_ffn.T, grad_pre)
    grad_hffn = matmul(grad_pre, w_up.T)
    grad_gain_f = jnp.sum(grad_hffn * normed_f, axis=0)
    ffn_terms = (grad_wup, grad_wdown, grad_gain_f)
    grad_branch = grad_out + norm_f_back(grad_hffn * gain_f)[0]
    grad_blow = grad_branch.astype(jnp.bfloat16)
    grad_wout = matmul(mixed_heads.T, grad_blow)
    grad_fq, grad_fk, grad_vals, grad_state, grad_norm = attend_back(matmul(grad_blow, w_out.T))
    identity = (jnp.ones((), jnp.float32), jnp.zeros_like(grad_state), jnp.zeros_like(grad_norm))
    _, carry_state, carry_norm = entering(
        (kept_flag, grad_state, grad_norm), "seq", combine_carry, identity
    )
    _, tail_back = jax.vjp(lambda a, b: tail_sums(a, b, tail_mask), feats_k, value_heads)
    more_k, more_v = tail_back((carry_state, carry_norm))
    grad_q = lift_q_back(grad_fq)[0].astype(jnp.bfloat16)
    grad_k = lift_k_back(grad_fk + more_k)[0].astype(jnp.bfloat16)
    grad_v = (grad_vals + more_v).reshape(row_count, -1).astype(jnp.bfloat16)
    grad_hattn = matmul(grad_q, w_query.T) + matmul(grad_k, w_key.T) + matmul(grad_v, w_value.T)
    grad_gain_a = jnp.sum(grad_hattn * normed_a, axis=0)
    grad_in = grad_branch + norm_a_back(grad_hattn * gain_a)[0]
    attn_grads = (
        matmul(h_attn.T, grad_q),
        matmul(h_attn.T, grad_k),
        matmul(h_attn.T, grad_v),
        grad_wout,
        grad_gain_a,
    )
    return (grad_in, attn_grads, ffn_terms)


def local(
    inputs,
    cotangent,
    doc_lengths,
    feature_proj,
    w_query,
    w_key,
    w_value,
    w_out,
    w_up,
    w_down,
    gain_attn,
    gain_ffn,
):
    section_idx = lax.axis_index("section")
    seq_idx = lax.axis_index("seq")
    micro_count, _, row_count, feat_width = inputs.shape
    first_row = seq_idx * row_count
    projection = feature_proj[0]
    lengths_all = doc_lengths[:, 0, :]
    masters = (
        w_query[0],
        w_key[0],
        w_value[0],
        w_out[0],
        w_up[0],
        w_down[0],
        gain_attn[0],
        gain_ffn[0],
    )
    lowered = tuple((master.astype(jnp.bfloat16) for master in masters))
    gathered = jax.tree.map(
        lambda part, own: part.astype(own.dtype),
        lax.all_gather(as_sent(lowered), ("dp", "seq"), axis=0, tiled=True),
        lowered,
    )
    batch_range = jnp.arange(micro_count, dtype=jnp.int32)
    received = jnp.zeros((row_count, feat_width), jnp.bfloat16)
    outputs = jnp.zeros((micro_count, row_count, feat_width), jnp.float32)
    kept_inputs, kept_states, kept_norms = ([], [], [])
    for step_no in range(micro_count + 1):
        batch_no = step_no - section_idx
        is_valid = ((batch_no >= 0) & (batch_no < micro_count)).astype(jnp.float32)
        batch_idx = jnp.clip(batch_no, 0, micro_count - 1)
        own_input = inputs[min(step_no, micro_count - 1), 0].astype(jnp.float32)
        layer_in = jnp.where(section_idx == 0, own_input, received.astype(jnp.float32))
        lengths = lax.dynamic_index_in_dim(lengths_all, batch_idx, 0, keepdims=False)
        layer_out, incoming_state, norm_in = run_forward(
            layer_in, gathered, projection, lengths, first_row
        )
        sent_out = layer_out.astype(jnp.bfloat16)
        chosen = (batch_range == batch_idx).astype(jnp.float32) * is_valid
        outputs = outputs + chosen[:, None, None] * sent_out.astype(jnp.float32)[None]
        kept_inputs.append(layer_in)
        kept_states.append(incoming_state)
        kept_norms.append(norm_in)
        if step_no < micro_count:
            received = passed_along(sent_out, "section", 1)
    weights_back = jax.tree.map(
        lambda part, own: part.astype(own.dtype),
        lax.all_gather(as_sent(lowered), ("dp", "seq"), axis=0, tiled=True),
        lowered,
    )
    stacked_inputs = jnp.stack(kept_inputs)
    stacked_states = jnp.stack(kept_states)
    stacked_norms = jnp.stack(kept_norms)
    grad_recv = jnp.zeros((row_count, feat_width), jnp.bfloat16)
    grad_inputs = jnp.zeros((micro_count, row_count, feat_width), jnp.float32)
    totals = tuple((jnp.zeros(part.shape, jnp.float32) for part in weights_back))
    for step_no in range(micro_count + 1):
        batch_no = step_no - 1 + section_idx
        is_valid = ((batch_no >= 0) & (batch_no < micro_count)).astype(jnp.float32)
        batch_idx = jnp.clip(batch_no, 0, micro_count - 1)
        slot_idx = jnp.clip(step_no - 1 + 2 * section_idx, 0, micro_count)
        layer_in = lax.dynamic_index_in_dim(stacked_inputs, slot_idx, 0, keepdims=False)
        incoming_state = lax.dynamic_index_in_dim(stacked_states, slot_idx, 0, keepdims=False)
        norm_in = lax.dynamic_index_in_dim(stacked_norms, slot_idx, 0, keepdims=False)
        own_grad = cotangent[min(step_no, micro_count - 1), 0].astype(jnp.float32)
        grad_out = jnp.where(section_idx == 1, own_grad, grad_recv.astype(jnp.float32))
        lengths = lax.dynamic_index_in_dim(lengths_all, batch_idx, 0, keepdims=False)
        grad_in, attn_grads, ffn_terms = run_backward(
            layer_in,
            incoming_state,
            norm_in,
            grad_out,
            weights_back,
            projection,
            lengths,
            first_row,
        )
        grads = (
            attn_grads[0],
            attn_grads[1],
            attn_grads[2],
            attn_grads[3],
            ffn_terms[0],
            ffn_terms[1],
            attn_grads[4],
            ffn_terms[2],
        )
        totals = tuple(
            (total_part + is_valid * grad_part for total_part, grad_part in zip(totals, grads))
        )
        sent_back = grad_in.astype(jnp.bfloat16)
        chosen = (batch_range == batch_idx).astype(jnp.float32) * is_valid
        grad_inputs = grad_inputs + chosen[:, None, None] * sent_back.astype(jnp.float32)[None]
        if step_no < micro_count:
            grad_recv = passed_along(sent_back, "section", -1)
    shares = lax.psum_scatter(totals, ("dp", "seq"), scatter_dimension=0, tiled=True)
    activations = outputs.astype(jnp.bfloat16)[None, :, None]
    input_grad = grad_inputs.astype(jnp.bfloat16)[None, :, None]
    return (activations, input_grad) + tuple((share_part[None] for share_part in shares))


def solution(mesh):
    in_specs = (
        P(None, "dp", "seq", None),
        P(None, "dp", "seq", None),
        P(None, "dp", None),
        P("section", None, None, None),
        P("section", ("dp", "seq"), None),
        P("section", ("dp", "seq"), None),
        P("section", ("dp", "seq"), None),
        P("section", ("dp", "seq"), None),
        P("section", ("dp", "seq"), None),
        P("section", ("dp", "seq"), None),
        P("section", ("dp", "seq")),
        P("section", ("dp", "seq")),
    )
    out_specs = (
        P("section", None, "dp", "seq", None),
        P("section", None, "dp", "seq", None),
        P("section", ("dp", "seq"), None),
        P("section", ("dp", "seq"), None),
        P("section", ("dp", "seq"), None),
        P("section", ("dp", "seq"), None),
        P("section", ("dp", "seq"), None),
        P("section", ("dp", "seq"), None),
        P("section", ("dp", "seq")),
        P("section", ("dp", "seq")),
    )
    fits = mesh.shape["section"] == 2 and mesh.shape["dp"] == 4 and mesh.shape["seq"] == 4
    body = fast_local if fits else local
    return jax.shard_map(body, mesh=mesh, in_specs=in_specs, out_specs=out_specs, check_vma=False)
```

```python
import functools

import jax
import jax.numpy as jnp
from jax import lax
from jax.experimental import pallas as pl
from jax.experimental.pallas import tpu as pltpu
from jax.sharding import PartitionSpec as P

MESH = pl.DeviceIdType.MESH
F32 = jnp.float32
BF16 = jnp.bfloat16
VMEM_LIMIT = 63 << 20

ROW_Q, ROW_K, ROW_V, ROW_O, ROW_UP, ROW_DOWN, SLAB = 32, 64, 96, 128, 160, 288, 416
PORTIONS = ((0, 64), (128, 144))


def dot(a, b):
    return lax.dot_general(a, b, (((1,), (0,)), ((), ())), preferred_element_type=F32)


def dot_nt(a, b):
    return lax.dot_general(a, b, (((1,), (1,)), ((), ())), preferred_element_type=F32)


def dot_tn(a, b):
    return lax.dot_general(a, b, (((0,), (0,)), ((), ())), preferred_element_type=F32)


def remote(src, dst, ssem, rsem, dev):
    return pltpu.make_async_remote_copy(
        src_ref=src, dst_ref=dst, send_sem=ssem, recv_sem=rsem, device_id=dev, device_id_type=MESH
    )


class Place:
    def __init__(self):
        self.c = lax.axis_index("section")
        self.d = lax.axis_index("dp")
        self.z = lax.axis_index("seq")
        self.o = 1 - self.c
        self.xn = self.d + 1 - 2 * lax.rem(self.d, 2)
        self.yn = lax.rem(self.d + 2, 4)
        self.first = self.xn + self.c * (self.yn - self.xn)
        self.second = self.yn + self.c * (self.xn - self.yn)
        self.diag = 3 - self.d
        self.me = self.d * 4 + self.z

    def at(self, d, z):
        return (self.c, d, z)

    def sibling(self):
        return (self.o, self.d, self.z)

    def peers(self):
        out = [self.sibling(), self.at(self.xn, self.z), self.at(self.yn, self.z)]
        return out + [self.at(self.d, lax.rem(self.z + k, 4)) for k in (1, 2, 3)]

    def greet(self):
        for dev in self.peers():
            pl.semaphore_signal(pltpu.get_barrier_semaphore(), inc=1, device_id=dev, device_id_type=MESH)

    def meet(self):
        pl.semaphore_wait(pltpu.get_barrier_semaphore(), len(self.peers()))


def weight(G, l, row, n=32):
    return G[l, :, row : row + n, :].reshape(16 * n, 512)


class Gather:
    def __init__(self, pc, G, l, por, ssem, rsem, dsend, drecv):
        base, self.n = PORTIONS[por]
        self.pc, self.G, self.l, self.por = pc, G, l, por
        self.sems = ssem, rsem, dsend, drecv
        self.start = pl.multiple_of(base + pc.c * self.n, 16)
        self.other = pl.multiple_of(base + pc.o * self.n, 16)

    def ref(self, g):
        return self.G.at[self.l, g, pl.ds(self.start, self.n)]

    def link(self, g, i, dev):
        ssem, rsem, _, _ = self.sems
        return remote(self.ref(g), self.ref(g), ssem.at[self.l, self.por, i], rsem.at[self.l, self.por, g], dev)

    def sib(self, g):
        _, _, dsend, drecv = self.sems
        return remote(
            self.ref(g), self.ref(g), dsend.at[self.l, self.por, g], drecv.at[self.l, self.por, g], self.pc.sibling()
        )

    def arrive(self, g):
        self.link(g, 0, self.pc.sibling()).wait_recv()

    def own(self):
        pc = self.pc
        for k in (2, 1, 3):
            self.link(pc.me, k, pc.at(pc.d, lax.rem(pc.z + k, 4))).start()
        self.link(pc.me, 4, pc.at(pc.first, pc.z)).start()
        self.link(pc.me, 8, pc.at(pc.second, pc.z)).start()

    def column(self, k):
        pc = self.pc

        def step():
            g = pc.d * 4 + lax.rem(pc.z + k, 4)
            self.arrive(g)
            self.link(g, 4 + k, pc.at(pc.first, pc.z)).start()
            self.link(g, 8 + k, pc.at(pc.second, pc.z)).start()
            self.sib(g).start()

        if not isinstance(k, int):
            pl.when(k > 0)(step)
        elif k > 0:
            step()

    def across(self, k):
        pc = self.pc
        g = pc.first * 4 + lax.rem(pc.z + k, 4)
        self.arrive(g)
        self.link(g, 12 + k, pc.at(pc.second, pc.z)).start()
        self.sib(g).start()

    def far(self, k):
        pc = self.pc
        zz = lax.rem(pc.z + k, 4)
        for dp in (pc.second, pc.diag):
            g = dp * 4 + zz
            self.arrive(g)
            self.sib(g).start()

    def finish(self):
        _, _, dsend, drecv = self.sems
        pc = self.pc

        def wait(g):
            ref = self.G.at[self.l, g, pl.ds(self.other, self.n)]
            remote(ref, ref, dsend.at[self.l, self.por, g], drecv.at[self.l, self.por, g], pc.sibling()).wait_recv()

        def step(i, _):
            wait(lax.rem(pc.me + 1 + i, 16))
            return 0

        lax.fori_loop(0, 15, step, 0)

    def drain(self):
        pc = self.pc

        def step(i, _):
            self.link(pc.me, 1 + i, pc.at(pc.first, pc.z)).wait_send()
            self.sib(lax.rem(pc.me + 1 + i, 16)).wait_send()
            return 0

        lax.fori_loop(0, 15, step, 0)


def last_start(lengths, c, first_row, pos):
    starts = []
    at = 0
    for i in range(3):
        at = at + lengths[c, 0, i]
        starts.append(at - first_row)
    out = jnp.full(pos.shape, -first_row, jnp.int32)
    for s in starts:
        out = jnp.where(pos >= s, s, out)
    return out, starts


def norm(x):
    c = x - jnp.mean(x, axis=-1, keepdims=True)
    rstd = lax.rsqrt(jnp.mean(c * c, axis=-1, keepdims=True) + 1e-05)
    return c * rstd, rstd


def lane_low(shape):
    return lax.rem(lax.broadcasted_iota(jnp.int32, shape, 1), 128) < 64


def lift_pair(w, proj):
    hi = w.astype(BF16)
    low = (w - hi.astype(F32)).astype(BF16)
    sq = (w * w).astype(BF16)
    e = dot(jnp.concatenate([hi, sq, low, hi], axis=1), proj)
    return (jnp.exp(e) * 0.0625).astype(BF16)


def forward_kernel(
    inputs, lengths, wq_in, wk_in, wv_in, wo_in, wup_in, wdown_in, gains_in, proj,
    act, G_out, fq_out, fk_out, v_out, att_out, rden_out, branch_out, w_out, x_out, sin_out, pb_out,
    G, px, pk, mask, xbuf, hbuf, qbuf, kbuf, fq, fk, vext, att, rden, branch, wqk, xin, sin, tail, sbuf,
    gains, ybuf, hf, acc,
    ssem, rsem, dsend, drecv, osem, osem2, psem, csend, crecv, asem, wsem,
):
    pc = Place()
    c, z = pc.c, pc.z
    pc.greet()
    G[c, pc.me, 0:ROW_Q, :] = gains_in[...]
    for ref, row in ((wq_in, ROW_Q), (wk_in, ROW_K), (wv_in, ROW_V), (wo_in, ROW_O)):
        G[c, pc.me, row : row + 32, :] = ref[0].astype(BF16)
    for j in range(4):
        row = ROW_UP + 32 * j
        G[c, pc.me, row : row + 32, :] = wup_in[0, :, 512 * j : 512 * j + 512].astype(BF16)
    G[c, pc.me, ROW_DOWN:SLAB, :] = wdown_in[0].astype(BF16)
    hi = proj[0].astype(BF16)
    px[c, 0] = hi
    px[c, 1] = (proj[0] - hi.astype(F32)).astype(BF16)
    pc.meet()
    halves = {}
    for por, (base, n) in enumerate(PORTIONS):
        for half, at in ((0, pc.o), (1, c)):
            ref = G.at[c, pc.me, pl.ds(pl.multiple_of(base + at * n, 16), n)]
            halves[por, half] = remote(ref, ref, osem2.at[0, por, half], osem2.at[1, por, half], pc.sibling())
            halves[por, half].start()
    psend = remote(px.at[c], px.at[c], psem.at[0], psem.at[1], pc.sibling())
    psend.start()
    moves = {
        (l, por): Gather(pc, G, l, por, ssem, rsem, dsend, drecv) for l in (0, 1) for por in range(2)
    }

    def four(step):
        for k in range(4):
            step(k)

    for por in (0, 1):
        for half in (0, 1):
            halves[por, half].wait()
    moves[0, 0].own()

    first_row = z * 512
    rows = lax.broadcasted_iota(jnp.int32, (512, 512), 0)
    cols = lax.broadcasted_iota(jnp.int32, (512, 512), 1)
    begin, starts = last_start(lengths, c, first_row, rows)
    mask[...] = ((cols <= rows) & (cols >= begin)).astype(F32)
    prow = lax.broadcasted_iota(jnp.int32, (512, 1), 0)
    begin_col, _ = last_start(lengths, c, first_row, prow)
    head_mask = (begin_col < 0).astype(F32)
    lane = lax.broadcasted_iota(jnp.int32, (1, 512), 1)
    inner = [jnp.where((s < 512) & (s >= 0), s, 0) for s in starts]
    cut = jnp.maximum(jnp.maximum(inner[0], inner[1]), inner[2])
    tail_mask = (lane >= cut).astype(F32)

    moves[0, 1].own()
    psend.wait()
    pk[...] = jnp.zeros_like(pk)
    for l in (0, 1):
        for p in range(4):
            for h in (0, 1):
                at = slice(64 * h, 64 * h + 64)
                to = slice(256 * h, 256 * h + 256)
                pk[l, p, at, to] = px[l, 0, 2 * p + h]
                pk[l, p, 128 + 64 * h : 192 + 64 * h, to] = jnp.full((64, 256), -0.5, BF16)
                pk[l, p, 256 + 64 * h : 320 + 64 * h, to] = px[l, 0, 2 * p + h]
                pk[l, p, 384 + 64 * h : 448 + 64 * h, to] = px[l, 1, 2 * p + h]
    keep = pltpu.make_async_copy(pk.at[:, :, 0:256, :], pb_out, osem)
    keep.start()
    vext[:, :, :, 128:] = jnp.ones((2, 4, 512, 128), BF16)

    @pl.when(z == 0)
    def _():
        sin[...] = jnp.zeros_like(sin)

    xbuf[...] = inputs[c, 0].astype(F32)
    four(moves[0, 0].column)
    moves[1, 0].own()
    four(moves[0, 0].across)
    moves[1, 1].own()
    four(moves[0, 1].column)
    four(moves[0, 0].far)
    four(moves[0, 1].across)
    moves[0, 0].finish()
    below = (c, pc.d, jnp.minimum(z + 1, 3))
    low = lane_low((512, 128))
    row_low = lax.broadcasted_iota(jnp.int32, (144, 256), 0)
    tail_is_first = (row_low < 64) | ((row_low >= 128) & (row_low < 136))
    low256 = lane_low((256, 128))

    def chain(l, p):
        return remote(sbuf.at[l, p], sin.at[l, p], csend.at[l, p], crecv.at[l, p], below)

    saved = (
        (G, G_out), (fq, fq_out), (fk, fk_out), (vext, v_out), (att, att_out), (rden, rden_out),
        (branch, branch_out), (wqk, w_out), (xin, x_out), (sin, sin_out),
    )

    def save(l, *refs):
        for i, (src, dst) in enumerate(saved):
            if any(src is ref for ref in refs):
                pltpu.make_async_copy(src.at[l], dst.at[l], wsem.at[l, i]).start()

    def give_own(l):
        return pltpu.make_async_copy(ybuf.at[l], act.at[c], asem.at[0])

    def give_far(l):
        return remote(ybuf.at[l], act.at[c], asem.at[1], asem.at[2], pc.sibling())

    def give(l):
        pl.when(c == l)(lambda: give_own(l).start())
        pl.when(c != l)(lambda: give_far(l).start())

    def layer(l, during):
        gains[...] = jnp.sum(G[l, :, 0:16, :].astype(F32), axis=0)

        def norm_tile(i, _):
            at = pl.ds(pl.multiple_of(i * 128, 128), 128)
            x = xbuf[at, :]
            xin[l, at, :] = x.astype(BF16)
            hbuf[at, :] = (norm(x)[0] * gains[0:1, :]).astype(BF16)
            return 0

        lax.fori_loop(0, 4, norm_tile, 0)
        scale = 64 ** (-0.25)
        kbuf[...] = dot(hbuf[...], weight(G, l, ROW_K)) * scale
        qbuf[...] = dot(hbuf[...], weight(G, l, ROW_V))

        def pass_on(p):
            chain(l, p).wait_recv()
            sbuf[l, p] = (tail[p] + sin[l, p].astype(F32)).astype(BF16)
            chain(l, p).start()

        def key_pair(p, _):
            if "key" in during:
                during["key"](p)
            at = pl.ds(pl.multiple_of(p * 128, 128), 128)
            w = kbuf[:, at]
            wqk[l, 1, p] = w.astype(BF16)
            f = lift_pair(w, pk[l, p])
            fk[l, p] = f
            v = qbuf[:, at]
            vext[l, p, :, 0:128] = v.astype(BF16)
            vt = jnp.concatenate([v.T * tail_mask, jnp.broadcast_to(tail_mask, (16, 512))], axis=0).astype(BF16)
            t = jnp.where(tail_is_first, dot(vt, f[:, 0:256]), dot(vt, f[:, 256:512]))
            tail[p] = t

            @pl.when(z == 0)
            def _():
                sbuf[l, p] = t.astype(BF16)
                chain(l, p).start()

            @pl.when((z == 1) & (p >= 2))
            def _():
                pass_on(p - 2)

            return 0

        lax.fori_loop(0, 4, key_pair, 0)
        save(l, fk, vext, xin)
        qbuf[...] = dot(hbuf[...], weight(G, l, ROW_Q)) * scale

        def query_pair(p, _):
            if "query" in during:
                during["query"](p)
            at = pl.ds(pl.multiple_of(p * 128, 128), 128)
            w = qbuf[:, at]
            wqk[l, 0, p] = w.astype(BF16)
            fq[l, p] = lift_pair(w, pk[l, p])

            @pl.when((z == 1) & (p < 2))
            def _():
                pass_on(p + 2)

            @pl.when((z == 2) & (p >= 1))
            def _():
                pass_on(p - 1)

            return 0

        lax.fori_loop(0, 4, query_pair, 0)
        save(l, fq, wqk)

        def attend_pair(p, _):
            if "attend" in during:
                during["attend"](p)
            at = pl.ds(pl.multiple_of(p * 128, 128), 128)

            @pl.when((z == 2) & (p == 0))
            def _():
                pass_on(3)

            @pl.when(z == 3)
            def _():
                chain(l, p).wait_recv()

            for t in (0, 1):
                n = 256 * (t + 1)
                tr = slice(256 * t, 256 * t + 256)
                res = []
                for h in (0, 1):
                    fl = slice(256 * h, 256 * h + 256)
                    fqh = fq[l, p, tr, fl]
                    a = (dot_nt(fqh, fk[l, p, 0:n, fl]) * mask[tr, 0:n]).astype(BF16)
                    zrow = sin[l, p, 128:144, :].astype(F32)[8 * h : 8 * h + 1, :]
                    st = jnp.concatenate(
                        [sin[l, p, 0:128, :], jnp.broadcast_to(zrow, (128, 256)).astype(BF16)], axis=0
                    )
                    res.append(dot(a, vext[l, p, 0:n, :]) + head_mask[tr, :] * dot_nt(fqh, st))
                num = jnp.where(low256, res[0][:, 0:128], res[1][:, 0:128])
                den = jnp.where(low256, res[0][:, 128:256], res[1][:, 128:256])
                r = 1.0 / den
                att[l, tr, at] = num * r
                rden[l, tr, at] = r
            return 0

        lax.fori_loop(0, 4, attend_pair, 0)
        save(l, att, rden, sin)

        if "branch" in during:
            during["branch"]()

        def branch_tile(i, _):
            at = pl.ds(pl.multiple_of(i * 256, 256), 256)
            b = xbuf[at, :] + dot(att[l, at, :].astype(BF16), weight(G, l, ROW_O))
            branch[l, at, :] = b
            hf[at, :] = (norm(b)[0] * gains[1:2, :]).astype(BF16)
            acc[at, :] = b
            return 0

        save(l, G)
        lax.fori_loop(0, 2, branch_tile, 0)
        save(l, branch)

        def ffn_tile(j, _):
            if "ffn" in during:
                during["ffn"](j)
            up = G[l, :, pl.ds(pl.multiple_of(ROW_UP + 32 * j, 32), 32), :].reshape(512, 512)
            down = G[l, pl.ds(4 * j, 4), ROW_DOWN:SLAB, :].reshape(512, 512)
            for i in (0, 1):
                at = slice(256 * i, 256 * i + 256)
                pre = dot(hf[at, :], up)
                hid = jax.nn.gelu(pre).astype(BF16)
                acc[at, :] += dot(hid, down)
            return 0

        lax.fori_loop(0, 4, ffn_tile, 0)
        y = acc[...].astype(BF16)
        ybuf[l] = y
        xbuf[...] = y.astype(F32)
        give(l)

    def before_branch(l):
        if l == 0:
            four(moves[0, 1].far)
        moves[l, 1].finish()

    layer(0, {"key": moves[1, 0].column, "query": moves[1, 1].column, "attend": moves[1, 0].across,
              "branch": lambda: before_branch(0), "ffn": moves[1, 1].across})
    four(moves[1, 0].far)
    moves[1, 0].finish()
    layer(1, {"query": moves[1, 1].far, "branch": lambda: before_branch(1)})
    give_own(0).wait()
    give_far(0).wait()
    keep.wait()
    for l in (0, 1):
        for i, (src, dst) in enumerate(saved):
            pltpu.make_async_copy(src.at[l], dst.at[l], wsem.at[l, i]).wait()

    @pl.when(z < 3)
    def _():
        for l in (0, 1):
            for p in range(4):
                chain(l, p).wait_send()

    for move in moves.values():
        move.drain()


def forward_call(inputs, lengths, weights, gain_rows, proj):
    sds = jax.ShapeDtypeStruct
    dma = pltpu.SemaphoreType.DMA
    vm = pl.BlockSpec(memory_space=pltpu.VMEM)
    hbm = pl.BlockSpec(memory_space=pl.ANY)
    saved = [
        sds((2, 16, SLAB, 512), BF16), sds((2, 4, 512, 512), BF16), sds((2, 4, 512, 512), BF16),
        sds((2, 4, 512, 256), BF16), sds((2, 512, 512), F32), sds((2, 512, 512), F32), sds((2, 512, 512), F32),
        sds((2, 2, 4, 512, 128), BF16), sds((2, 512, 512), BF16), sds((2, 4, 144, 256), BF16),
        sds((2, 4, 256, 512), BF16),
    ]
    scratch = [
        pltpu.VMEM((2, 16, SLAB, 512), BF16),
        pltpu.VMEM((2, 2, 8, 64, 256), BF16),
        pltpu.VMEM((2, 4, 512, 512), BF16),
        pltpu.VMEM((512, 512), F32),
        pltpu.VMEM((512, 512), F32),
        pltpu.VMEM((512, 512), BF16),
        pltpu.VMEM((512, 512), F32),
        pltpu.VMEM((512, 512), F32),
        pltpu.VMEM((2, 4, 512, 512), BF16),
        pltpu.VMEM((2, 4, 512, 512), BF16),
        pltpu.VMEM((2, 4, 512, 256), BF16),
        pltpu.VMEM((2, 512, 512), F32),
        pltpu.VMEM((2, 512, 512), F32),
        pltpu.VMEM((2, 512, 512), F32),
        pltpu.VMEM((2, 2, 4, 512, 128), BF16),
        pltpu.VMEM((2, 512, 512), BF16),
        pltpu.VMEM((2, 4, 144, 256), BF16),
        pltpu.VMEM((4, 144, 256), F32),
        pltpu.VMEM((2, 4, 144, 256), BF16),
        pltpu.VMEM((16, 512), F32),
        pltpu.VMEM((2, 512, 512), BF16),
        pltpu.VMEM((512, 512), BF16),
        pltpu.VMEM((512, 512), F32),
        dma((2, 2, 16)), dma((2, 2, 16)), dma((2, 2, 16)), dma((2, 2, 16)), dma, dma((2, 2, 2)), dma((2,)),
        dma((2, 4)), dma((2, 4)), dma((3,)), dma((2, 10)),
    ]
    return pl.pallas_call(
        forward_kernel,
        out_shape=[sds((2, 512, 512), BF16)] + saved,
        in_specs=[vm, pl.BlockSpec(memory_space=pltpu.SMEM)] + [vm] * 8,
        out_specs=[vm] + [hbm] * len(saved),
        scratch_shapes=scratch,
        compiler_params=pltpu.CompilerParams(
            collective_id=0, has_side_effects=True, vmem_limit_bytes=VMEM_LIMIT
        ),
        name="forward",
    )(inputs, lengths, *weights, gain_rows, proj)


def make_gain_rows(gain_attn, gain_ffn):
    g = lax.axis_index("dp") * 4 + lax.axis_index("seq")
    lane = lax.broadcasted_iota(jnp.int32, (1, 512), 1)
    mine = lane // 32 == g

    def gain_row(gain):
        return jnp.where(mine, jnp.tile(gain[None, :].astype(BF16), (1, 16)), jnp.zeros((), BF16))

    return jnp.concatenate([gain_row(gain_attn), gain_row(gain_ffn), jnp.zeros((30, 512), BF16)], axis=0)


def gelu_parts(x):
    k = 0.7978845608028654
    x2 = x * x
    t = jnp.tanh(k * x * (1.0 + 0.044715 * x2))
    half = 0.5 * (1.0 + t)
    return x * half, half + 0.5 * x * (1.0 - t * t) * k * (1.0 + 0.134145 * x2)


def norm_back(y, rstd, dy):
    m1 = jnp.mean(dy, axis=-1, keepdims=True)
    m2 = jnp.mean(dy * y, axis=-1, keepdims=True)
    return rstd * (dy - m1 - y * m2)


HALF = (SLAB - ROW_Q) // 2
SUM_PORTIONS = ((ROW_O, 144), (ROW_Q, 48))


class Sums:
    def __init__(self, pc, slabs, bufs, sems, l, por):
        base, self.n = SUM_PORTIONS[por]
        self.pc, self.slabs, self.l, self.por = pc, slabs, l, por
        self.sb, self.r1, self.r2, self.r3, self.keep = bufs
        self.sems = sems
        self.mine = pl.multiple_of(base + pc.c * self.n, 16)
        self.other = pl.multiple_of(base + pc.o * self.n, 16)
        self.at = pl.ds(sum(2 * n for _, n in SUM_PORTIONS[:por]) // 2, self.n)

    def copy(self, i, j, src, dst, dev):
        ssem, rsem = self.sems
        return remote(src, dst, ssem.at[self.l, self.por, i, j], rsem.at[self.l, self.por, i, j], dev)

    def to_sibling(self, g):
        src = self.slabs.at[self.l, g, pl.ds(self.other, self.n)]
        return self.copy(0, g, src, self.sb.at[self.l, g, self.at], self.pc.sibling())

    def to_second(self, j, zz, g):
        src, dst = self.sb.at[self.l, g, self.at], self.r1.at[self.l, j, zz, self.at]
        return self.copy(1, 4 * j + zz, src, dst, self.pc.at(self.pc.second, self.pc.z))

    def to_first(self, zz, g):
        src, dst = self.sb.at[self.l, g, self.at], self.r2.at[self.l, zz, self.at]
        return self.copy(2, zz, src, dst, self.pc.at(self.pc.first, self.pc.z))

    def along(self, k, g):
        src, dst = self.sb.at[self.l, g, self.at], self.r3.at[self.l, 3 - k, self.at]
        return self.copy(3, 3 - k, src, dst, self.pc.at(self.pc.d, lax.rem(self.pc.z + k, 4)))

    def begin(self):
        pc = self.pc
        for col in (pc.diag, pc.second, pc.first, pc.d):
            for k in (1, 2, 3, 0):
                self.to_sibling(col * 4 + lax.rem(pc.z + k, 4)).start()

    def pair(self, g):
        self.to_sibling(g).wait_recv()
        own = self.slabs[self.l, g, pl.ds(self.mine, self.n), :]
        return own.astype(F32) + self.sb[self.l, g, self.at, :].astype(F32)

    def stage1(self, j, i):
        pc = self.pc
        zz = lax.rem(pc.z + 1 + i, 4)
        g = (pc.diag if j == 0 else pc.second) * 4 + zz
        self.sb[self.l, g, self.at, :] = self.pair(g).astype(BF16)
        self.to_second(j, zz, g).start()

    def stage2(self, i):
        pc = self.pc
        zz = lax.rem(pc.z + 1 + i, 4)
        g = pc.first * 4 + zz
        s = self.pair(g)
        self.to_second(0, zz, g).wait_recv()
        self.sb[self.l, g, self.at, :] = (s + self.r1[self.l, 0, zz, self.at, :].astype(F32)).astype(BF16)
        self.to_first(zz, g).start()

    def stage3(self, k):
        pc = self.pc
        zz = lax.rem(pc.z + k, 4)
        g = pc.d * 4 + zz
        s = self.pair(g)
        self.to_second(1, zz, g).wait_recv()
        s = s + self.r1[self.l, 1, zz, self.at, :].astype(F32)
        self.to_first(zz, g).wait_recv()
        s = s + self.r2[self.l, zz, self.at, :].astype(F32)
        if k:
            self.sb[self.l, g, self.at, :] = s.astype(BF16)
            self.along(k, g).start()
        else:
            self.keep[self.l, self.at, :] = s

    def stage4(self, l):
        s = self.keep[l, self.at, :]
        for i in range(3):
            s = s + self.r3[l, i, self.at, :].astype(F32)
        return s

    def arrive(self):
        for k in (1, 2, 3):
            self.along(k, self.pc.me).wait_recv()

    def drain(self):
        for i in range(16):
            self.to_sibling(i).wait_send()
        for j in (0, 1):
            for zz in range(4):
                self.to_second(j, zz, 0).wait_send()
        for zz in range(4):
            self.to_first(zz, 0).wait_send()
        for k in (1, 2, 3):
            self.along(k, 0).wait_send()


def backward_kernel(
    cotangent, lengths, wq_in, wk_in, wv_in, wup_in, G_in, fq_in, fk_in, v_in, att_in, rden_in, branch_in, w_in, x_in, sin_in, pb_in,
    gin, gq_out, gk_out, gv_out, go_out, gup_out, gdown_out, gg_out,
    G, fq, fk, vext, att, rden, branch, wqk, xin, sin, pb,
    mask, mask_t, gbuf, gbr, hbuf, hT, gb, dh, gq, gk, gv, le, rin, rtail, rbuf, gains, xout, slabs,
    sb, r1, r2, r3, keep, total,
    lsem, csend, crecv, asem, ssem, rsem, fsem,
):
    pc = Place()
    c, z = pc.c, pc.z
    top, attn, ffn = pl.ds(0, 16), pl.ds(ROW_Q, ROW_UP - ROW_Q), pl.ds(ROW_UP, SLAB - ROW_UP)
    loads = {
        "branch": (lambda l: branch_in.at[l], branch), "top": (lambda l: G_in.at[l, :, top], G.at[:, top]),
        "ffn": (lambda l: G_in.at[l, :, ffn], G.at[:, ffn]), "att": (lambda l: att_in.at[l], att),
        "attn": (lambda l: G_in.at[l, :, attn], G.at[:, attn]), "rden": (lambda l: rden_in.at[l], rden),
        "fq": (lambda l: fq_in.at[l], fq), "sin": (lambda l: sin_in.at[l], sin), "fk": (lambda l: fk_in.at[l], fk),
        "vext": (lambda l: v_in.at[l], vext), "pb": (lambda l: pb_in.at[l], pb), "wqk": (lambda l: w_in.at[l], wqk),
        "xin": (lambda l: x_in.at[l], xin),
    }

    def load(l, name):
        src, dst = loads[name]
        return pltpu.make_async_copy(src(l), dst, lsem.at[list(loads).index(name)])

    def needs(l, *names):
        for name in names:
            load(l, name).wait()

    def done(l, *names):
        if l == 1:
            for name in names:
                load(0, name).start()

    pc.greet()
    for name in loads:
        load(1, name).start()

    first_row = z * 512
    rows = lax.broadcasted_iota(jnp.int32, (512, 512), 0)
    cols = lax.broadcasted_iota(jnp.int32, (512, 512), 1)
    begin, starts = last_start(lengths, c, first_row, rows)
    mask[...] = ((cols <= rows) & (cols >= begin)).astype(F32).astype(BF16)
    begin, _ = last_start(lengths, c, first_row, cols)
    mask_t[...] = ((rows <= cols) & (rows >= begin)).astype(F32).astype(BF16)
    prow = lax.broadcasted_iota(jnp.int32, (512, 1), 0)
    begin_col, _ = last_start(lengths, c, first_row, prow)
    head_col = (begin_col < 0).astype(F32)
    lane = lax.broadcasted_iota(jnp.int32, (1, 512), 1)
    begin_row, _ = last_start(lengths, c, first_row, lane)
    head_row = (begin_row < 0).astype(F32)
    inner = [jnp.where((s < 512) & (s >= 0), s, 0) for s in starts]
    cut = jnp.maximum(jnp.maximum(inner[0], inner[1]), inner[2])
    tail_col = (prow >= cut).astype(F32)

    @pl.when(z == 3)
    def _():
        rin[...] = jnp.zeros_like(rin)

    gbuf[...] = cotangent[c, 0].astype(F32)
    pc.meet()
    above = (c, pc.d, jnp.maximum(z - 1, 0))
    row_low = lax.broadcasted_iota(jnp.int32, (144, 256), 0)
    tail_is_first = (row_low < 64) | ((row_low >= 128) & (row_low < 136))
    low = lane_low((512, 128))
    ones_i = lax.broadcasted_iota(jnp.int32, (256, 128), 0)
    ones_j = lax.broadcasted_iota(jnp.int32, (256, 128), 1)
    head_ones = (lax.rem(ones_i, 128) // 64 == ones_j // 64).astype(BF16)
    scale = 64 ** (-0.25)

    def chain(l, p):
        return remote(rbuf.at[l, p], rin.at[l, p], csend.at[l, p], crecv.at[l, p], above)

    sums = {(l, por): Sums(pc, slabs, (sb, r1, r2, r3, keep), (ssem, rsem), l, por) for l in (0, 1) for por in (0, 1)}

    def put(l, row, n, value):
        slabs[l, :, row : row + n, :] = value.astype(BF16).reshape(16, n, 512)

    def layer(l, during):
        def at_point(name, *args):
            if name in during:
                during[name](*args)

        needs(l, "branch", "top")
        gains[...] = jnp.sum(G[:, 0:16, :].astype(F32), axis=0)

        def norm_tile(i, _):
            at = pl.ds(pl.multiple_of(i * 128, 128), 128)
            hbuf[at, :] = (norm(branch[at, :])[0] * gains[1:2, :]).astype(BF16)
            gb[at, :] = gbuf[at, :].astype(BF16)
            return 0

        lax.fori_loop(0, 4, norm_tile, 0)
        hT[...] = hbuf[...].T
        dh[...] = jnp.zeros_like(dh)

        def ffn_tile(j, _):
            at_point("ffn", j)
            up_at = pl.ds(pl.multiple_of(ROW_UP + 32 * j, 32), 32)
            up = G[:, up_at, :].reshape(512, 512)
            down = G[pl.ds(4 * j, 4), ROW_DOWN:SLAB, :].reshape(512, 512)
            for i in (0, 1):
                at = slice(256 * i, 256 * i + 256)
                hid, slope = gelu_parts(dot(hbuf[at, :], up))
                gq[at, :] = hid.astype(BF16)
                gk[at, :] = (slope * dot_nt(gb[at, :], down)).astype(BF16)
            slabs[l, pl.ds(4 * j, 4), ROW_DOWN:SLAB, :] = dot_tn(gq[...], gb[...]).astype(BF16).reshape(4, 128, 512)
            g = gk[...]
            slabs[l, :, up_at, :] = dot(hT[...], g).astype(BF16).reshape(16, 32, 512)
            dh[...] += dot_nt(g, up)
            return 0

        needs(l, "ffn")
        lax.fori_loop(0, 4, ffn_tile, 0)
        done(l, "top", "ffn")
        needs(l, "att")

        def branch_tile(i, _):
            at_point("branch", i)
            at = pl.ds(pl.multiple_of(i * 128, 128), 128)
            y, rstd = norm(branch[at, :])
            d = dh[at, :]
            g = gbuf[at, :] + norm_back(y, rstd, d * gains[1:2, :])
            gbr[at, :] = g
            gb[at, :] = g.astype(BF16)
            hbuf[at, :] = att[at, :].astype(BF16)
            return 0

        lax.fori_loop(0, 4, branch_tile, 0)
        done(l, "branch")
        put(l, ROW_O, 32, dot_tn(hbuf[...], gb[...]))
        sums[l, 0].begin()
        at_point("middle")
        needs(l, "attn", "rden", "fq")
        dh[...] = dot_nt(gb[...], G[:, ROW_O : ROW_O + 32, :].reshape(512, 512))

        def pass_on(p):
            chain(l, p).wait_recv()
            rbuf[l, p] = (rtail[p] + rin[l, p].astype(F32)).astype(BF16)
            chain(l, p).start()

        def tail_pair(p, _):
            at_point("tail", p)
            at = pl.ds(pl.multiple_of(p * 128, 128), 128)
            g = dh[:, at]
            r = rden[:, at]
            t = g * att[:, at]
            hi = t.astype(BF16)
            lo = (t - hi.astype(F32)).astype(BF16)
            dden = -dot(jnp.concatenate([hi, lo], axis=1), head_ones) * r
            dnum = g * r
            le[p] = jnp.concatenate([dnum, dden * (1.0 / 64.0)], axis=1).astype(BF16)
            dt = (dden.T) * head_row
            lhs = jnp.concatenate([dnum.T * head_row, dt[0:8], dt[64:72]], axis=0).astype(BF16)
            tl = jnp.where(tail_is_first, dot(lhs, fq[p, :, 0:256]), dot(lhs, fq[p, :, 256:512]))
            rtail[p] = tl

            @pl.when(z == 3)
            def _():
                rbuf[l, p] = tl.astype(BF16)
                chain(l, p).start()

            @pl.when((z == 2) & (p >= 3))
            def _():
                pass_on(p - 3)

            return 0

        lax.fori_loop(0, 4, tail_pair, 0)
        done(l, "att", "rden")
        needs(l, "sin", "fk", "vext", "pb", "wqk")

        def attend_pair(p, _):
            at_point("attend", p)
            at = pl.ds(pl.multiple_of(p * 128, 128), 128)

            @pl.when((z == 2) & (p < 3))
            def _():
                pass_on(p + 1)

            ve = vext[p]
            lep = le[p]
            dq, dk, dv = [], [], []
            for h in (0, 1):
                if h == 1:
                    @pl.when(z == 1)
                    def _():
                        pass_on(p)

                fl = slice(256 * h, 256 * h + 256)
                keep = lane_low((512, 256)) if h == 0 else jnp.logical_not(lane_low((512, 256)))
                leh = jnp.where(keep, lep, jnp.zeros((), BF16))
                fqh, fkh = fq[p, :, fl], fk[p, :, fl]
                zrow = sin[p, 128:144, :].astype(F32)[8 * h : 8 * h + 1, :]
                st = jnp.concatenate([sin[p, 0:128, :], jnp.broadcast_to(zrow, (128, 256)).astype(BF16)], axis=0)
                dqh = head_col * dot(leh, st)
                da0 = dot_nt(leh[0:256], ve[0:256]).astype(BF16) * mask[0:256, 0:256]
                da1 = dot_nt(leh[256:512], ve).astype(BF16) * mask[256:512, :]
                dqh = dqh + jnp.concatenate([dot(da0, fkh[0:256]), dot(da1, fkh)], axis=0)
                at0 = dot_nt(fkh[0:256], fqh).astype(BF16) * mask_t[0:256, :]
                at1 = dot_nt(fkh[256:512], fqh[256:512]).astype(BF16) * mask_t[256:512, 256:512]
                dvh = jnp.concatenate([dot(at0, lep[:, 0:128]), dot(at1, lep[256:512, 0:128])], axis=0)
                dt0 = dot_nt(ve[0:256], leh).astype(BF16) * mask_t[0:256, :]
                dt1 = dot_nt(ve[256:512], leh[256:512]).astype(BF16) * mask_t[256:512, 256:512]
                dkh = jnp.concatenate([dot(dt0, fqh), dot(dt1, fqh[256:512])], axis=0)
                dq.append((dqh * fqh.astype(F32)).astype(BF16))
                dk.append(dkh)
                dv.append(dvh)

            @pl.when(z == 0)
            def _():
                chain(l, p).wait_recv()

            for h in (0, 1):
                fkh = fk[p, :, 256 * h : 256 * h + 256]
                rrow = rin[l, p, 128:144, :].astype(F32)[8 * h : 8 * h + 1, :] * (1.0 / 128.0)
                rows_h = lax.broadcasted_iota(jnp.int32, (128, 256), 0) // 64 == h
                rt = jnp.where(rows_h, rin[l, p, 0:128, :], jnp.zeros((), BF16))
                rte = jnp.concatenate([rt, jnp.broadcast_to(rrow, (128, 256)).astype(BF16)], axis=0)
                dv[h] = dv[h] + tail_col * dot_nt(fkh, rin[l, p, 0:128, :])
                dk[h] = ((dk[h] + tail_col * dot(ve, rte)) * fkh.astype(F32)).astype(BF16)
            gv[:, at] = jnp.where(low, dv[0], dv[1]).astype(BF16)
            for k, e, out in ((0, dq, gq), (1, dk, gk)):
                gw = dot_nt(jnp.concatenate(e, axis=1), pb[p])
                gw = gw[:, 0:128] + 2.0 * wqk[k, p].astype(F32) * gw[:, 128:256]
                out[:, at] = (gw * scale).astype(BF16)
            return 0

        lax.fori_loop(0, 4, attend_pair, 0)
        done(l, "fq", "sin", "fk", "vext", "pb", "wqk")
        needs(l, "xin")

        def norm_tile2(i, _):
            at_point("norm", i)
            at = pl.ds(pl.multiple_of(i * 128, 128), 128)
            hbuf[at, :] = (norm(xin[at, :].astype(F32))[0] * gains[0:1, :]).astype(BF16)
            return 0

        lax.fori_loop(0, 4, norm_tile2, 0)
        hT[...] = hbuf[...].T
        for row, g in ((ROW_Q, gq), (ROW_K, gk), (ROW_V, gv)):
            put(l, row, 32, dot(hT[...], g[...]))
        sums[l, 1].begin()
        dh[...] = dot_nt(gq[...], G[:, ROW_Q : ROW_Q + 32, :].reshape(512, 512))
        dh[...] += dot_nt(gk[...], G[:, ROW_K : ROW_K + 32, :].reshape(512, 512))
        dh[...] += dot_nt(gv[...], G[:, ROW_V : ROW_V + 32, :].reshape(512, 512))

        done(l, "attn")
        at_point("late")

        def out_tile(i, _):
            at_point("out", i)
            at = pl.ds(pl.multiple_of(i * 128, 128), 128)
            y, rstd = norm(xin[at, :].astype(F32))
            d = dh[at, :]
            g = (gbr[at, :] + norm_back(y, rstd, d * gains[0:1, :])).astype(BF16)
            xout[l, at, :] = g
            gbuf[at, :] = g.astype(F32)
            return 0

        lax.fori_loop(0, 4, out_tile, 0)
        done(l, "xin")

    def four(step, *args):
        for i in range(4):
            step(*args, i)

    def along_z(m):
        for k in (1, 2, 3, 0):
            m.stage3(k)

    layer(1, {"tail": lambda p: sums[1, 0].stage1(0, p), "attend": lambda p: sums[1, 0].stage1(1, p),
              "norm": sums[1, 0].stage2})
    along_z(sums[1, 0])
    layer(0, {"ffn": lambda p: (sums[1, 1].stage1(0, p), sums[1, 1].stage1(1, p)), "branch": sums[1, 1].stage2,
              "middle": lambda: along_z(sums[1, 1]),
              "tail": lambda p: sums[0, 0].stage1(0, p), "attend": lambda p: sums[0, 0].stage1(1, p),
              "norm": sums[0, 0].stage2, "out": lambda i: (sums[0, 1].stage1(0, i), sums[0, 1].stage1(1, i))})
    own_act = pltpu.make_async_copy(xout.at[c], gin.at[c], asem.at[0])
    own_act.start()
    far_act = remote(xout.at[pc.o], gin.at[c], asem.at[1], asem.at[2], pc.sibling())
    far_act.start()
    own_act.wait()
    far_act.wait()

    along_z(sums[0, 0])
    four(sums[0, 1].stage2)
    along_z(sums[0, 1])
    for m in sums.values():
        m.arrive()
    for por in (0, 1):
        m = sums[0, por]
        gbr[m.at, :] = m.stage4(pc.o)
    parts = []
    for por in (0, 1):
        m = sums[0, por]
        part = remote(gbr.at[m.at], total.at[pl.ds(m.mine, m.n)], fsem.at[0, por], fsem.at[1, por], pc.sibling())
        part.start()
        parts.append(part)
    for por in (0, 1):
        m = sums[0, por]
        total[pl.ds(m.mine, m.n), :] = m.stage4(c)
    for part in parts:
        part.wait()
    for ref, row in ((gq_out, ROW_Q), (gk_out, ROW_K), (gv_out, ROW_V), (go_out, ROW_O)):
        ref[...] = total[row : row + 32, :]
    for j in range(4):
        gup_out[:, 512 * j : 512 * j + 512] = total[ROW_UP + 32 * j : ROW_UP + 32 * j + 32, :]
    gdown_out[...] = total[ROW_DOWN:SLAB, :]
    ga = jnp.zeros((32, 512), F32)
    for ref, row in ((wq_in, ROW_Q), (wk_in, ROW_K), (wv_in, ROW_V)):
        ga = ga + ref[0].astype(BF16).astype(F32) * total[row : row + 32, :]
    gf = jnp.zeros((32, 512), F32)
    for j in range(4):
        up = wup_in[0, :, 512 * j : 512 * j + 512].astype(BF16).astype(F32)
        gf = gf + up * total[ROW_UP + 32 * j : ROW_UP + 32 * j + 32, :]
    gg_out[0] = jnp.broadcast_to(jnp.sum(ga, axis=1, keepdims=True), (32, 128))
    gg_out[1] = jnp.broadcast_to(jnp.sum(gf, axis=1, keepdims=True), (32, 128))
    for m in sums.values():
        m.drain()

    @pl.when(z > 0)
    def _():
        for l in (0, 1):
            for p in range(4):
                chain(l, p).wait_send()


def backward_call(cotangent, lengths, weights, saved):
    sds = jax.ShapeDtypeStruct
    dma = pltpu.SemaphoreType.DMA
    vm = pl.BlockSpec(memory_space=pltpu.VMEM)
    hbm = pl.BlockSpec(memory_space=pl.ANY)
    bufs = [pltpu.VMEM(a.shape[1:], a.dtype) for a in saved]
    full = (512, 512)
    scratch = bufs + [
        pltpu.VMEM(full, BF16),
        pltpu.VMEM(full, BF16),
        pltpu.VMEM(full, F32),
        pltpu.VMEM(full, F32),
        pltpu.VMEM(full, BF16),
        pltpu.VMEM(full, BF16),
        pltpu.VMEM(full, BF16),
        pltpu.VMEM(full, F32),
        pltpu.VMEM(full, BF16),
        pltpu.VMEM(full, BF16),
        pltpu.VMEM(full, BF16),
        pltpu.VMEM((4, 512, 256), BF16),
        pltpu.VMEM((2, 4, 144, 256), BF16),
        pltpu.VMEM((4, 144, 256), F32),
        pltpu.VMEM((2, 4, 144, 256), BF16),
        pltpu.VMEM((16, 512), F32),
        pltpu.VMEM((2, 512, 512), BF16),
        pltpu.VMEM((2, 16, SLAB, 512), BF16),
        pltpu.VMEM((2, 16, HALF, 512), BF16),
        pltpu.VMEM((2, 2, 4, HALF, 512), BF16),
        pltpu.VMEM((2, 4, HALF, 512), BF16),
        pltpu.VMEM((2, 3, HALF, 512), BF16),
        pltpu.VMEM((2, HALF, 512), F32),
        pltpu.VMEM((SLAB, 512), F32),
        dma((13,)), dma((2, 4)), dma((2, 4)), dma((3,)), dma((2, 2, 4, 16)), dma((2, 2, 4, 16)), dma((2, 2)),
    ]
    return pl.pallas_call(
        backward_kernel,
        out_shape=[sds((2, 512, 512), BF16)]
        + [sds((32, 512), F32)] * 4
        + [sds((32, 2048), F32), sds((128, 512), F32), sds((2, 32, 128), F32)],
        in_specs=[vm, pl.BlockSpec(memory_space=pltpu.SMEM)] + [vm] * 4 + [hbm] * len(saved),
        out_specs=[vm] * 8,
        scratch_shapes=scratch,
        compiler_params=pltpu.CompilerParams(
            collective_id=1, has_side_effects=True, vmem_limit_bytes=VMEM_LIMIT
        ),
        name="backward",
    )(cotangent, lengths, *weights, *saved)


def fast_local(inputs, cotangent, doc_lengths, feature_proj, *weights):
    gain_rows = make_gain_rows(weights[6][0], weights[7][0])
    outs = forward_call(inputs, doc_lengths, weights[:6], gain_rows, feature_proj)
    w_query, w_key, w_value, _, w_up = weights[:5]
    gin, *grads = backward_call(cotangent, doc_lengths, (w_query, w_key, w_value, w_up), outs[1:])

    def by_gain(sums, gain):
        return sums[None, :, 0] / gain.astype(BF16).astype(F32)

    return (
        (outs[0][None, :, None], gin[None, :, None])
        + tuple(g[None] for g in grads[:6])
        + (by_gain(grads[6][0], weights[6]), by_gain(grads[6][1], weights[7]))
    )


HIGH_PRECISION = lax.Precision.HIGHEST


def prefix(shard, axis, join, neutral):
    place = lax.axis_index(axis)
    gathered = jax.tree.map(
        lambda a, kind: lax.all_gather(a.astype(kind), axis),
        shard,
        (jnp.bfloat16, jnp.bfloat16, jnp.bfloat16),
    )
    state = jax.tree.map(lambda a, e: jnp.zeros_like(a) + jnp.asarray(e, a.dtype), shard, neutral)

    def prefix_one(lap, state):
        return join(
            state,
            jax.tree.map(
                lambda a, own: lax.dynamic_index_in_dim(a, lap, 0, False).astype(own.dtype),
                gathered,
                shard,
            ),
        )

    return lax.fori_loop(0, place, prefix_one, state)


def entering(shard, axis, join, neutral):
    count = lax.axis_size(axis)
    place = lax.axis_index(axis)
    ahead = count - 1 - place
    gathered = jax.tree.map(
        lambda a, kind: lax.all_gather(a.astype(kind), axis),
        shard,
        jax.tree.map(lambda a: jnp.bfloat16 if a.dtype == jnp.float32 else a.dtype, shard),
    )
    state = jax.tree.map(lambda a, e: jnp.zeros_like(a) + jnp.asarray(e, a.dtype), shard, neutral)

    def entering_one(lap, state):
        source = count - 1 - lap
        return join(
            state,
            jax.tree.map(
                lambda a, own: lax.dynamic_index_in_dim(a, source, 0, False).astype(own.dtype),
                gathered,
                shard,
            ),
        )

    return lax.fori_loop(0, ahead, entering_one, state)


def as_sent(shard):

    def short(part):
        return part.astype(jnp.bfloat16) if part.dtype == jnp.float32 else part

    return jax.tree.map(short, shard)


def passed_along(block, axis, distance):
    devices = range(lax.axis_size(axis))
    route = [(i - distance, i) for i in devices if i - distance in devices]
    return lax.ppermute(block, axis, route)


def matmul(left, right):
    return jnp.dot(left, right, preferred_element_type=jnp.float32)


def norm_rows(values):
    centre = values - jnp.mean(values, axis=-1, keepdims=True)
    return centre * lax.rsqrt(jnp.mean(centre * centre, axis=-1, keepdims=True) + 1e-05)


def lift(values, projection):
    heads, depth, feats = projection.shape
    scaled = values.reshape(values.shape[0], heads, depth) * depth ** (-0.25)
    raised = jnp.einsum("nhd,hdm->nhm", scaled, projection, precision=HIGH_PRECISION)
    return jnp.exp(raised - 0.5 * jnp.sum(scaled * scaled, axis=-1, keepdims=True)) * feats ** (
        -0.5
    )


def doc_masks(lengths, first_row, row_count):
    doc_ends = jnp.cumsum(lengths, dtype=jnp.int32)
    starts = doc_ends - lengths
    positions = first_row + jnp.arange(row_count, dtype=jnp.int32)
    begun_at = starts[None, :] <= positions[:, None]
    doc_ids = jnp.sum(begun_at.astype(jnp.int32), axis=1)
    order_idx = jnp.arange(row_count, dtype=jnp.int32)
    same_doc = (
        (doc_ids[:, None] == doc_ids[None, :]) & (order_idx[None, :] <= order_idx[:, None])
    ).astype(jnp.float32)
    inside = (starts >= first_row) & (starts < first_row + row_count)
    mask_per_head = (jnp.sum((begun_at & inside[None, :]).astype(jnp.int32), axis=1) == 0).astype(
        jnp.float32
    )
    tail_mask = (jnp.sum((~begun_at & inside[None, :]).astype(jnp.int32), axis=1) == 0).astype(
        jnp.float32
    )
    kept_flag = (jnp.sum(inside.astype(jnp.int32)) == 0).astype(jnp.float32)
    return (same_doc, mask_per_head, tail_mask, kept_flag)


def attend(query_features, feats_k, value_heads, incoming_state, norm_in, same_doc, mask_per_head):
    scores = (
        jnp.einsum("thm,shm->hts", query_features, feats_k, precision=HIGH_PRECISION)
        * same_doc[None]
    )
    attention_numerator = jnp.einsum("hts,shd->thd", scores, value_heads, precision=HIGH_PRECISION)
    attention_numerator = attention_numerator + mask_per_head[:, None, None] * jnp.einsum(
        "kec,ecz->kez", query_features, incoming_state, precision=HIGH_PRECISION
    )
    denominator = jnp.sum(scores, axis=2).T + mask_per_head[:, None] * jnp.einsum(
        "thm,hm->th", query_features, norm_in, precision=HIGH_PRECISION
    )
    return (attention_numerator / denominator[:, :, None]).reshape(query_features.shape[0], -1)


def tail_sums(feats_k, value_heads, tail_mask):
    weighted_values = feats_k * tail_mask[:, None, None]
    return (
        jnp.einsum("zlu,zlv->luv", weighted_values, value_heads, precision=HIGH_PRECISION),
        jnp.sum(weighted_values, axis=0),
    )


def combine_carry(earlier, later_part):
    return (
        earlier[0] * later_part[0],
        later_part[1] + later_part[0] * earlier[1],
        later_part[2] + later_part[0] * earlier[2],
    )


def run_forward(layer_in, weights, projection, lengths, first_row):
    w_query, w_key, w_value, w_out, w_up, w_down, gain_attn, gain_ffn = weights
    row_count = layer_in.shape[0]
    same_doc, mask_per_head, tail_mask, kept_flag = doc_masks(lengths, first_row, row_count)
    h_attn = (norm_rows(layer_in) * gain_attn.astype(jnp.float32)).astype(jnp.bfloat16)
    query_features = lift(matmul(h_attn, w_query), projection)
    feats_k = lift(matmul(h_attn, w_key), projection)
    value_heads = matmul(h_attn, w_value).reshape(row_count, projection.shape[0], -1)
    state_tail, norm_tail = tail_sums(feats_k, value_heads, tail_mask)
    identity = (jnp.ones((), jnp.float32), jnp.zeros_like(state_tail), jnp.zeros_like(norm_tail))
    _, incoming_state, norm_in = prefix(
        (kept_flag, state_tail, norm_tail), "seq", combine_carry, identity
    )
    mixed_heads = attend(
        query_features, feats_k, value_heads, incoming_state, norm_in, same_doc, mask_per_head
    ).astype(jnp.bfloat16)
    branch = layer_in + matmul(mixed_heads, w_out)
    h_ffn = (norm_rows(branch) * gain_ffn.astype(jnp.float32)).astype(jnp.bfloat16)
    hidden = jax.nn.gelu(matmul(h_ffn, w_up)).astype(jnp.bfloat16)
    return (branch + matmul(hidden, w_down), incoming_state, norm_in)


def run_backward(
    layer_in, incoming_state, norm_in, grad_out, weights, projection, lengths, first_row
):
    w_query, w_key, w_value, w_out, w_up, w_down, gain_attn, gain_ffn = weights
    row_count = layer_in.shape[0]
    same_doc, mask_per_head, tail_mask, kept_flag = doc_masks(lengths, first_row, row_count)
    gain_a = gain_attn.astype(jnp.float32)
    gain_f = gain_ffn.astype(jnp.float32)
    normed_a, norm_a_back = jax.vjp(norm_rows, layer_in)
    h_attn = (normed_a * gain_a).astype(jnp.bfloat16)
    query_features, lift_q_back = jax.vjp(lambda z: lift(z, projection), matmul(h_attn, w_query))
    feats_k, lift_k_back = jax.vjp(lambda z: lift(z, projection), matmul(h_attn, w_key))
    value_heads = matmul(h_attn, w_value).reshape(row_count, projection.shape[0], -1)
    attended, attend_back = jax.vjp(
        lambda a, b, c, d, e: attend(a, b, c, d, e, same_doc, mask_per_head),
        query_features,
        feats_k,
        value_heads,
        incoming_state,
        norm_in,
    )
    mixed_heads = attended.astype(jnp.bfloat16)
    branch = layer_in + matmul(mixed_heads, w_out)
    normed_f, norm_f_back = jax.vjp(norm_rows, branch)
    h_ffn = (normed_f * gain_f).astype(jnp.bfloat16)
    activated, gelu_back = jax.vjp(jax.nn.gelu, matmul(h_ffn, w_up))
    hidden = activated.astype(jnp.bfloat16)
    grad_low = grad_out.astype(jnp.bfloat16)
    grad_wdown = matmul(hidden.T, grad_low)
    grad_pre = gelu_back(matmul(grad_low, w_down.T))[0].astype(jnp.bfloat16)
    grad_wup = matmul(h_ffn.T, grad_pre)
    grad_hffn = matmul(grad_pre, w_up.T)
    grad_gain_f = jnp.sum(grad_hffn * normed_f, axis=0)
    ffn_terms = (grad_wup, grad_wdown, grad_gain_f)
    grad_branch = grad_out + norm_f_back(grad_hffn * gain_f)[0]
    grad_blow = grad_branch.astype(jnp.bfloat16)
    grad_wout = matmul(mixed_heads.T, grad_blow)
    grad_fq, grad_fk, grad_vals, grad_state, grad_norm = attend_back(matmul(grad_blow, w_out.T))
    identity = (jnp.ones((), jnp.float32), jnp.zeros_like(grad_state), jnp.zeros_like(grad_norm))
    _, carry_state, carry_norm = entering(
        (kept_flag, grad_state, grad_norm), "seq", combine_carry, identity
    )
    _, tail_back = jax.vjp(lambda a, b: tail_sums(a, b, tail_mask), feats_k, value_heads)
    more_k, more_v = tail_back((carry_state, carry_norm))
    grad_q = lift_q_back(grad_fq)[0].astype(jnp.bfloat16)
    grad_k = lift_k_back(grad_fk + more_k)[0].astype(jnp.bfloat16)
    grad_v = (grad_vals + more_v).reshape(row_count, -1).astype(jnp.bfloat16)
    grad_hattn = matmul(grad_q, w_query.T) + matmul(grad_k, w_key.T) + matmul(grad_v, w_value.T)
    grad_gain_a = jnp.sum(grad_hattn * normed_a, axis=0)
    grad_in = grad_branch + norm_a_back(grad_hattn * gain_a)[0]
    attn_grads = (
        matmul(h_attn.T, grad_q),
        matmul(h_attn.T, grad_k),
        matmul(h_attn.T, grad_v),
        grad_wout,
        grad_gain_a,
    )
    return (grad_in, attn_grads, ffn_terms)


def local(
    inputs,
    cotangent,
    doc_lengths,
    feature_proj,
    w_query,
    w_key,
    w_value,
    w_out,
    w_up,
    w_down,
    gain_attn,
    gain_ffn,
):
    section_idx = lax.axis_index("section")
    seq_idx = lax.axis_index("seq")
    micro_count, _, row_count, feat_width = inputs.shape
    first_row = seq_idx * row_count
    projection = feature_proj[0]
    lengths_all = doc_lengths[:, 0, :]
    masters = (
        w_query[0],
        w_key[0],
        w_value[0],
        w_out[0],
        w_up[0],
        w_down[0],
        gain_attn[0],
        gain_ffn[0],
    )
    lowered = tuple((master.astype(jnp.bfloat16) for master in masters))
    gathered = jax.tree.map(
        lambda part, own: part.astype(own.dtype),
        lax.all_gather(as_sent(lowered), ("dp", "seq"), axis=0, tiled=True),
        lowered,
    )
    batch_range = jnp.arange(micro_count, dtype=jnp.int32)
    received = jnp.zeros((row_count, feat_width), jnp.bfloat16)
    outputs = jnp.zeros((micro_count, row_count, feat_width), jnp.float32)
    kept_inputs, kept_states, kept_norms = ([], [], [])
    for step_no in range(micro_count + 1):
        batch_no = step_no - section_idx
        is_valid = ((batch_no >= 0) & (batch_no < micro_count)).astype(jnp.float32)
        batch_idx = jnp.clip(batch_no, 0, micro_count - 1)
        own_input = inputs[min(step_no, micro_count - 1), 0].astype(jnp.float32)
        layer_in = jnp.where(section_idx == 0, own_input, received.astype(jnp.float32))
        lengths = lax.dynamic_index_in_dim(lengths_all, batch_idx, 0, keepdims=False)
        layer_out, incoming_state, norm_in = run_forward(
            layer_in, gathered, projection, lengths, first_row
        )
        sent_out = layer_out.astype(jnp.bfloat16)
        chosen = (batch_range == batch_idx).astype(jnp.float32) * is_valid
        outputs = outputs + chosen[:, None, None] * sent_out.astype(jnp.float32)[None]
        kept_inputs.append(layer_in)
        kept_states.append(incoming_state)
        kept_norms.append(norm_in)
        if step_no < micro_count:
            received = passed_along(sent_out, "section", 1)
    weights_back = jax.tree.map(
        lambda part, own: part.astype(own.dtype),
        lax.all_gather(as_sent(lowered), ("dp", "seq"), axis=0, tiled=True),
        lowered,
    )
    stacked_inputs = jnp.stack(kept_inputs)
    stacked_states = jnp.stack(kept_states)
    stacked_norms = jnp.stack(kept_norms)
    grad_recv = jnp.zeros((row_count, feat_width), jnp.bfloat16)
    grad_inputs = jnp.zeros((micro_count, row_count, feat_width), jnp.float32)
    totals = tuple((jnp.zeros(part.shape, jnp.float32) for part in weights_back))
    for step_no in range(micro_count + 1):
        batch_no = step_no - 1 + section_idx
        is_valid = ((batch_no >= 0) & (batch_no < micro_count)).astype(jnp.float32)
        batch_idx = jnp.clip(batch_no, 0, micro_count - 1)
        slot_idx = jnp.clip(step_no - 1 + 2 * section_idx, 0, micro_count)
        layer_in = lax.dynamic_index_in_dim(stacked_inputs, slot_idx, 0, keepdims=False)
        incoming_state = lax.dynamic_index_in_dim(stacked_states, slot_idx, 0, keepdims=False)
        norm_in = lax.dynamic_index_in_dim(stacked_norms, slot_idx, 0, keepdims=False)
        own_grad = cotangent[min(step_no, micro_count - 1), 0].astype(jnp.float32)
        grad_out = jnp.where(section_idx == 1, own_grad, grad_recv.astype(jnp.float32))
        lengths = lax.dynamic_index_in_dim(lengths_all, batch_idx, 0, keepdims=False)
        grad_in, attn_grads, ffn_terms = run_backward(
            layer_in,
            incoming_state,
            norm_in,
            grad_out,
            weights_back,
            projection,
            lengths,
            first_row,
        )
        grads = (
            attn_grads[0],
            attn_grads[1],
            attn_grads[2],
            attn_grads[3],
            ffn_terms[0],
            ffn_terms[1],
            attn_grads[4],
            ffn_terms[2],
        )
        totals = tuple(
            (total_part + is_valid * grad_part for total_part, grad_part in zip(totals, grads))
        )
        sent_back = grad_in.astype(jnp.bfloat16)
        chosen = (batch_range == batch_idx).astype(jnp.float32) * is_valid
        grad_inputs = grad_inputs + chosen[:, None, None] * sent_back.astype(jnp.float32)[None]
        if step_no < micro_count:
            grad_recv = passed_along(sent_back, "section", -1)
    shares = lax.psum_scatter(totals, ("dp", "seq"), scatter_dimension=0, tiled=True)
    activations = outputs.astype(jnp.bfloat16)[None, :, None]
    input_grad = grad_inputs.astype(jnp.bfloat16)[None, :, None]
    return (activations, input_grad) + tuple((share_part[None] for share_part in shares))


def solution(mesh):
    in_specs = (
        P(None, "dp", "seq", None),
        P(None, "dp", "seq", None),
        P(None, "dp", None),
        P("section", None, None, None),
        P("section", ("dp", "seq"), None),
        P("section", ("dp", "seq"), None),
        P("section", ("dp", "seq"), None),
        P("section", ("dp", "seq"), None),
        P("section", ("dp", "seq"), None),
        P("section", ("dp", "seq"), None),
        P("section", ("dp", "seq")),
        P("section", ("dp", "seq")),
    )
    out_specs = (
        P("section", None, "dp", "seq", None),
        P("section", None, "dp", "seq", None),
        P("section", ("dp", "seq"), None),
        P("section", ("dp", "seq"), None),
        P("section", ("dp", "seq"), None),
        P("section", ("dp", "seq"), None),
        P("section", ("dp", "seq"), None),
        P("section", ("dp", "seq"), None),
        P("section", ("dp", "seq")),
        P("section", ("dp", "seq")),
    )
    fits = mesh.shape["section"] == 2 and mesh.shape["dp"] == 4 and mesh.shape["seq"] == 4
    body = fast_local if fits else local
    return jax.shard_map(body, mesh=mesh, in_specs=in_specs, out_specs=out_specs, check_vma=False)
```

```python
import functools

import jax
import jax.numpy as jnp
from jax import lax
from jax.experimental import pallas as pl
from jax.experimental.pallas import tpu as pltpu
from jax.sharding import PartitionSpec as P

MESH = pl.DeviceIdType.MESH
F32 = jnp.float32
BF16 = jnp.bfloat16
VMEM_LIMIT = 63 << 20

ROW_Q, ROW_K, ROW_V, ROW_O, ROW_UP, ROW_DOWN, SLAB = 32, 64, 96, 128, 160, 288, 416
PORTIONS = ((0, 64), (128, 144))


def dot(a, b):
    return lax.dot_general(a, b, (((1,), (0,)), ((), ())), preferred_element_type=F32)


def dot_nt(a, b):
    return lax.dot_general(a, b, (((1,), (1,)), ((), ())), preferred_element_type=F32)


def dot_tn(a, b):
    return lax.dot_general(a, b, (((0,), (0,)), ((), ())), preferred_element_type=F32)


def remote(src, dst, ssem, rsem, dev):
    return pltpu.make_async_remote_copy(
        src_ref=src, dst_ref=dst, send_sem=ssem, recv_sem=rsem, device_id=dev, device_id_type=MESH
    )


class Place:
    def __init__(self):
        self.c = lax.axis_index("section")
        self.d = lax.axis_index("dp")
        self.z = lax.axis_index("seq")
        self.o = 1 - self.c
        self.xn = self.d + 1 - 2 * lax.rem(self.d, 2)
        self.yn = lax.rem(self.d + 2, 4)
        self.first = self.xn + self.c * (self.yn - self.xn)
        self.second = self.yn + self.c * (self.xn - self.yn)
        self.diag = 3 - self.d
        self.me = self.d * 4 + self.z

    def at(self, d, z):
        return (self.c, d, z)

    def sibling(self):
        return (self.o, self.d, self.z)

    def peers(self):
        out = [self.sibling(), self.at(self.xn, self.z), self.at(self.yn, self.z)]
        return out + [self.at(self.d, lax.rem(self.z + k, 4)) for k in (1, 2, 3)]

    def greet(self):
        for dev in self.peers():
            pl.semaphore_signal(pltpu.get_barrier_semaphore(), inc=1, device_id=dev, device_id_type=MESH)

    def meet(self):
        pl.semaphore_wait(pltpu.get_barrier_semaphore(), len(self.peers()))


def weight(G, l, row, n=32):
    return G[l, :, row : row + n, :].reshape(16 * n, 512)


class Gather:
    def __init__(self, pc, G, l, por, ssem, rsem, dsend, drecv):
        base, self.n = PORTIONS[por]
        self.pc, self.G, self.l, self.por = pc, G, l, por
        self.sems = ssem, rsem, dsend, drecv
        self.start = pl.multiple_of(base + pc.c * self.n, 16)
        self.other = pl.multiple_of(base + pc.o * self.n, 16)

    def ref(self, g):
        return self.G.at[self.l, g, pl.ds(self.start, self.n)]

    def link(self, g, i, dev):
        ssem, rsem, _, _ = self.sems
        return remote(self.ref(g), self.ref(g), ssem.at[self.l, self.por, i], rsem.at[self.l, self.por, g], dev)

    def sib(self, g):
        _, _, dsend, drecv = self.sems
        return remote(
            self.ref(g), self.ref(g), dsend.at[self.l, self.por, g], drecv.at[self.l, self.por, g], self.pc.sibling()
        )

    def arrive(self, g):
        self.link(g, 0, self.pc.sibling()).wait_recv()

    def own(self):
        pc = self.pc
        for k in (2, 1, 3):
            self.link(pc.me, k, pc.at(pc.d, lax.rem(pc.z + k, 4))).start()
        self.link(pc.me, 4, pc.at(pc.first, pc.z)).start()
        self.link(pc.me, 8, pc.at(pc.second, pc.z)).start()

    def column(self, k):
        pc = self.pc

        def step():
            g = pc.d * 4 + lax.rem(pc.z + k, 4)
            self.arrive(g)
            self.link(g, 4 + k, pc.at(pc.first, pc.z)).start()
            self.link(g, 8 + k, pc.at(pc.second, pc.z)).start()
            self.sib(g).start()

        if not isinstance(k, int):
            pl.when(k > 0)(step)
        elif k > 0:
            step()

    def across(self, k):
        pc = self.pc
        g = pc.first * 4 + lax.rem(pc.z + k, 4)
        self.arrive(g)
        self.link(g, 12 + k, pc.at(pc.second, pc.z)).start()
        self.sib(g).start()

    def far(self, k):
        pc = self.pc
        zz = lax.rem(pc.z + k, 4)
        for dp in (pc.second, pc.diag):
            g = dp * 4 + zz
            self.arrive(g)
            self.sib(g).start()

    def finish(self):
        _, _, dsend, drecv = self.sems
        pc = self.pc

        def wait(g):
            ref = self.G.at[self.l, g, pl.ds(self.other, self.n)]
            remote(ref, ref, dsend.at[self.l, self.por, g], drecv.at[self.l, self.por, g], pc.sibling()).wait_recv()

        def step(i, _):
            wait(lax.rem(pc.me + 1 + i, 16))
            return 0

        lax.fori_loop(0, 15, step, 0)

    def drain(self):
        pc = self.pc

        def step(i, _):
            self.link(pc.me, 1 + i, pc.at(pc.first, pc.z)).wait_send()
            self.sib(lax.rem(pc.me + 1 + i, 16)).wait_send()
            return 0

        lax.fori_loop(0, 15, step, 0)


def last_start(lengths, c, first_row, pos):
    starts = []
    at = 0
    for i in range(3):
        at = at + lengths[c, 0, i]
        starts.append(at - first_row)
    out = jnp.full(pos.shape, -first_row, jnp.int32)
    for s in starts:
        out = jnp.where(pos >= s, s, out)
    return out, starts


def norm(x):
    c = x - jnp.mean(x, axis=-1, keepdims=True)
    rstd = lax.rsqrt(jnp.mean(c * c, axis=-1, keepdims=True) + 1e-05)
    return c * rstd, rstd


def lane_low(shape):
    return lax.rem(lax.broadcasted_iota(jnp.int32, shape, 1), 128) < 64


def lift_pair(w, proj):
    hi = w.astype(BF16)
    low = (w - hi.astype(F32)).astype(BF16)
    sq = (w * w).astype(BF16)
    e = dot(jnp.concatenate([hi, sq, low, hi], axis=1), proj)
    return (jnp.exp(e) * 0.0625).astype(BF16)


def forward_kernel(
    inputs, lengths, wq_in, wk_in, wv_in, wo_in, wup_in, wdown_in, ga_in, gf_in, proj,
    act, G_out, fq_out, fk_out, v_out, att_out, rden_out, branch_out, w_out, x_out, sin_out, pb_out,
    G, px, pk, mask, xbuf, hbuf, qbuf, kbuf, fq, fk, vext, att, rden, branch, wqk, xin, sin, tail, sbuf,
    gains, ybuf, hf, acc,
    ssem, rsem, dsend, drecv, osem, osem2, psem, csend, crecv, asem, wsem,
):
    pc = Place()
    c, z = pc.c, pc.z
    pc.greet()
    gains[...] = jnp.zeros_like(gains)
    gains[0:1, 0:32] = ga_in[...]
    gains[1:2, 0:32] = gf_in[...]
    placed = pltpu.roll(gains[0:8, :], 32 * pc.me, 1)
    G[c, pc.me, 0:16, :] = jnp.concatenate([placed, jnp.zeros((8, 512), F32)], axis=0).astype(BF16)
    G[c, pc.me, 16:ROW_Q, :] = jnp.zeros((ROW_Q - 16, 512), BF16)
    for ref, row in ((wq_in, ROW_Q), (wk_in, ROW_K), (wv_in, ROW_V), (wo_in, ROW_O)):
        G[c, pc.me, row : row + 32, :] = ref[0].astype(BF16)
    for j in range(4):
        row = ROW_UP + 32 * j
        G[c, pc.me, row : row + 32, :] = wup_in[0, :, 512 * j : 512 * j + 512].astype(BF16)
    G[c, pc.me, ROW_DOWN:SLAB, :] = wdown_in[0].astype(BF16)
    hi = proj[0].astype(BF16)
    px[c, 0] = hi
    px[c, 1] = (proj[0] - hi.astype(F32)).astype(BF16)
    pc.meet()
    halves = {}
    for por, (base, n) in enumerate(PORTIONS):
        for half, at in ((0, pc.o), (1, c)):
            ref = G.at[c, pc.me, pl.ds(pl.multiple_of(base + at * n, 16), n)]
            halves[por, half] = remote(ref, ref, osem2.at[0, por, half], osem2.at[1, por, half], pc.sibling())
            halves[por, half].start()
    psend = remote(px.at[c], px.at[c], psem.at[0], psem.at[1], pc.sibling())
    psend.start()
    moves = {
        (l, por): Gather(pc, G, l, por, ssem, rsem, dsend, drecv) for l in (0, 1) for por in range(2)
    }

    def four(step):
        for k in range(4):
            step(k)

    for por in (0, 1):
        for half in (0, 1):
            halves[por, half].wait()
    moves[0, 0].own()

    first_row = z * 512
    rows = lax.broadcasted_iota(jnp.int32, (512, 512), 0)
    cols = lax.broadcasted_iota(jnp.int32, (512, 512), 1)
    begin, starts = last_start(lengths, c, first_row, rows)
    mask[...] = ((cols <= rows) & (cols >= begin)).astype(F32)
    prow = lax.broadcasted_iota(jnp.int32, (512, 1), 0)
    begin_col, _ = last_start(lengths, c, first_row, prow)
    head_mask = (begin_col < 0).astype(F32)
    lane = lax.broadcasted_iota(jnp.int32, (1, 512), 1)
    inner = [jnp.where((s < 512) & (s >= 0), s, 0) for s in starts]
    cut = jnp.maximum(jnp.maximum(inner[0], inner[1]), inner[2])
    tail_mask = (lane >= cut).astype(F32)

    moves[0, 1].own()
    psend.wait()
    pk[...] = jnp.zeros_like(pk)
    for l in (0, 1):
        for p in range(4):
            for h in (0, 1):
                at = slice(64 * h, 64 * h + 64)
                to = slice(256 * h, 256 * h + 256)
                pk[l, p, at, to] = px[l, 0, 2 * p + h]
                pk[l, p, 128 + 64 * h : 192 + 64 * h, to] = jnp.full((64, 256), -0.5, BF16)
                pk[l, p, 256 + 64 * h : 320 + 64 * h, to] = px[l, 0, 2 * p + h]
                pk[l, p, 384 + 64 * h : 448 + 64 * h, to] = px[l, 1, 2 * p + h]
    keep = pltpu.make_async_copy(pk.at[:, :, 0:256, :], pb_out, osem)
    keep.start()
    vext[:, :, :, 128:] = jnp.ones((2, 4, 512, 128), BF16)

    @pl.when(z == 0)
    def _():
        sin[...] = jnp.zeros_like(sin)

    xbuf[...] = inputs[c, 0].astype(F32)
    four(moves[0, 0].column)
    moves[1, 0].own()
    four(moves[0, 0].across)
    moves[1, 1].own()
    four(moves[0, 1].column)
    four(moves[0, 0].far)
    four(moves[0, 1].across)
    moves[0, 0].finish()
    below = (c, pc.d, jnp.minimum(z + 1, 3))
    low = lane_low((512, 128))
    row_low = lax.broadcasted_iota(jnp.int32, (144, 256), 0)
    tail_is_first = (row_low < 64) | ((row_low >= 128) & (row_low < 136))
    low256 = lane_low((256, 128))

    def chain(l, p):
        return remote(sbuf.at[l, p], sin.at[l, p], csend.at[l, p], crecv.at[l, p], below)

    saved = (
        (G, G_out), (fq, fq_out), (fk, fk_out), (vext, v_out), (att, att_out), (rden, rden_out),
        (branch, branch_out), (wqk, w_out), (xin, x_out), (sin, sin_out),
    )

    def save(l, *refs):
        for i, (src, dst) in enumerate(saved):
            if any(src is ref for ref in refs):
                pltpu.make_async_copy(src.at[l], dst.at[l], wsem.at[l, i]).start()

    def give_own(l):
        return pltpu.make_async_copy(ybuf.at[l], act.at[c], asem.at[0])

    def give_far(l):
        return remote(ybuf.at[l], act.at[c], asem.at[1], asem.at[2], pc.sibling())

    def give(l):
        pl.when(c == l)(lambda: give_own(l).start())
        pl.when(c != l)(lambda: give_far(l).start())

    def layer(l, during):
        gains[...] = jnp.sum(G[l, :, 0:16, :].astype(F32), axis=0)

        def norm_tile(i, _):
            at = pl.ds(pl.multiple_of(i * 128, 128), 128)
            x = xbuf[at, :]
            xin[l, at, :] = x.astype(BF16)
            hbuf[at, :] = (norm(x)[0] * gains[0:1, :]).astype(BF16)
            return 0

        lax.fori_loop(0, 4, norm_tile, 0)
        scale = 64 ** (-0.25)
        kbuf[...] = dot(hbuf[...], weight(G, l, ROW_K)) * scale
        qbuf[...] = dot(hbuf[...], weight(G, l, ROW_V))

        def pass_on(p):
            chain(l, p).wait_recv()
            sbuf[l, p] = (tail[p] + sin[l, p].astype(F32)).astype(BF16)
            chain(l, p).start()

        def key_pair(p, _):
            if "key" in during:
                during["key"](p)
            at = pl.ds(pl.multiple_of(p * 128, 128), 128)
            w = kbuf[:, at]
            wqk[l, 1, p] = w.astype(BF16)
            f = lift_pair(w, pk[l, p])
            fk[l, p] = f
            v = qbuf[:, at]
            vext[l, p, :, 0:128] = v.astype(BF16)
            vt = jnp.concatenate([v.T * tail_mask, jnp.broadcast_to(tail_mask, (16, 512))], axis=0).astype(BF16)
            t = jnp.where(tail_is_first, dot(vt, f[:, 0:256]), dot(vt, f[:, 256:512]))
            tail[p] = t

            @pl.when(z == 0)
            def _():
                sbuf[l, p] = t.astype(BF16)
                chain(l, p).start()

            @pl.when((z == 1) & (p >= 2))
            def _():
                pass_on(p - 2)

            return 0

        lax.fori_loop(0, 4, key_pair, 0)
        save(l, fk, vext, xin)
        qbuf[...] = dot(hbuf[...], weight(G, l, ROW_Q)) * scale

        def query_pair(p, _):
            if "query" in during:
                during["query"](p)
            at = pl.ds(pl.multiple_of(p * 128, 128), 128)
            w = qbuf[:, at]
            wqk[l, 0, p] = w.astype(BF16)
            fq[l, p] = lift_pair(w, pk[l, p])

            @pl.when((z == 1) & (p < 2))
            def _():
                pass_on(p + 2)

            @pl.when((z == 2) & (p >= 1))
            def _():
                pass_on(p - 1)

            return 0

        lax.fori_loop(0, 4, query_pair, 0)
        save(l, fq, wqk)

        def attend_pair(p, _):
            if "attend" in during:
                during["attend"](p)
            at = pl.ds(pl.multiple_of(p * 128, 128), 128)

            @pl.when((z == 2) & (p == 0))
            def _():
                pass_on(3)

            @pl.when(z == 3)
            def _():
                chain(l, p).wait_recv()

            for t in (0, 1):
                n = 256 * (t + 1)
                tr = slice(256 * t, 256 * t + 256)
                res = []
                for h in (0, 1):
                    fl = slice(256 * h, 256 * h + 256)
                    fqh = fq[l, p, tr, fl]
                    a = (dot_nt(fqh, fk[l, p, 0:n, fl]) * mask[tr, 0:n]).astype(BF16)
                    zrow = sin[l, p, 128:144, :].astype(F32)[8 * h : 8 * h + 1, :]
                    st = jnp.concatenate(
                        [sin[l, p, 0:128, :], jnp.broadcast_to(zrow, (128, 256)).astype(BF16)], axis=0
                    )
                    res.append(dot(a, vext[l, p, 0:n, :]) + head_mask[tr, :] * dot_nt(fqh, st))
                num = jnp.where(low256, res[0][:, 0:128], res[1][:, 0:128])
                den = jnp.where(low256, res[0][:, 128:256], res[1][:, 128:256])
                r = 1.0 / den
                att[l, tr, at] = num * r
                rden[l, tr, at] = r
            return 0

        lax.fori_loop(0, 4, attend_pair, 0)
        save(l, att, rden, sin)

        if "branch" in during:
            during["branch"]()

        def branch_tile(i, _):
            at = pl.ds(pl.multiple_of(i * 256, 256), 256)
            b = xbuf[at, :] + dot(att[l, at, :].astype(BF16), weight(G, l, ROW_O))
            branch[l, at, :] = b
            hf[at, :] = (norm(b)[0] * gains[1:2, :]).astype(BF16)
            acc[at, :] = b
            return 0

        save(l, G)
        lax.fori_loop(0, 2, branch_tile, 0)
        save(l, branch)

        def ffn_tile(j, _):
            if "ffn" in during:
                during["ffn"](j)
            up = G[l, :, pl.ds(pl.multiple_of(ROW_UP + 32 * j, 32), 32), :].reshape(512, 512)
            down = G[l, pl.ds(4 * j, 4), ROW_DOWN:SLAB, :].reshape(512, 512)
            for i in (0, 1):
                at = slice(256 * i, 256 * i + 256)
                pre = dot(hf[at, :], up)
                hid = jax.nn.gelu(pre).astype(BF16)
                acc[at, :] += dot(hid, down)
            return 0

        lax.fori_loop(0, 4, ffn_tile, 0)
        y = acc[...].astype(BF16)
        ybuf[l] = y
        xbuf[...] = y.astype(F32)
        give(l)

    def before_branch(l):
        if l == 0:
            four(moves[0, 1].far)
        moves[l, 1].finish()

    layer(0, {"key": moves[1, 0].column, "query": moves[1, 1].column, "attend": moves[1, 0].across,
              "branch": lambda: before_branch(0), "ffn": moves[1, 1].across})
    four(moves[1, 0].far)
    moves[1, 0].finish()
    layer(1, {"query": moves[1, 1].far, "branch": lambda: before_branch(1)})
    give_own(0).wait()
    give_far(0).wait()
    keep.wait()
    for l in (0, 1):
        for i, (src, dst) in enumerate(saved):
            pltpu.make_async_copy(src.at[l], dst.at[l], wsem.at[l, i]).wait()

    @pl.when(z < 3)
    def _():
        for l in (0, 1):
            for p in range(4):
                chain(l, p).wait_send()

    for move in moves.values():
        move.drain()


def forward_call(inputs, lengths, weights, proj):
    sds = jax.ShapeDtypeStruct
    dma = pltpu.SemaphoreType.DMA
    vm = pl.BlockSpec(memory_space=pltpu.VMEM)
    hbm = pl.BlockSpec(memory_space=pl.ANY)
    saved = [
        sds((2, 16, SLAB, 512), BF16), sds((2, 4, 512, 512), BF16), sds((2, 4, 512, 512), BF16),
        sds((2, 4, 512, 256), BF16), sds((2, 512, 512), F32), sds((2, 512, 512), F32), sds((2, 512, 512), F32),
        sds((2, 2, 4, 512, 128), BF16), sds((2, 512, 512), BF16), sds((2, 4, 144, 256), BF16),
        sds((2, 4, 256, 512), BF16),
    ]
    scratch = [
        pltpu.VMEM((2, 16, SLAB, 512), BF16),
        pltpu.VMEM((2, 2, 8, 64, 256), BF16),
        pltpu.VMEM((2, 4, 512, 512), BF16),
        pltpu.VMEM((512, 512), F32),
        pltpu.VMEM((512, 512), F32),
        pltpu.VMEM((512, 512), BF16),
        pltpu.VMEM((512, 512), F32),
        pltpu.VMEM((512, 512), F32),
        pltpu.VMEM((2, 4, 512, 512), BF16),
        pltpu.VMEM((2, 4, 512, 512), BF16),
        pltpu.VMEM((2, 4, 512, 256), BF16),
        pltpu.VMEM((2, 512, 512), F32),
        pltpu.VMEM((2, 512, 512), F32),
        pltpu.VMEM((2, 512, 512), F32),
        pltpu.VMEM((2, 2, 4, 512, 128), BF16),
        pltpu.VMEM((2, 512, 512), BF16),
        pltpu.VMEM((2, 4, 144, 256), BF16),
        pltpu.VMEM((4, 144, 256), F32),
        pltpu.VMEM((2, 4, 144, 256), BF16),
        pltpu.VMEM((16, 512), F32),
        pltpu.VMEM((2, 512, 512), BF16),
        pltpu.VMEM((512, 512), BF16),
        pltpu.VMEM((512, 512), F32),
        dma((2, 2, 16)), dma((2, 2, 16)), dma((2, 2, 16)), dma((2, 2, 16)), dma, dma((2, 2, 2)), dma((2,)),
        dma((2, 4)), dma((2, 4)), dma((3,)), dma((2, 10)),
    ]
    return pl.pallas_call(
        forward_kernel,
        out_shape=[sds((2, 512, 512), BF16)] + saved,
        in_specs=[vm, pl.BlockSpec(memory_space=pltpu.SMEM)] + [vm] * 9,
        out_specs=[vm] + [hbm] * len(saved),
        scratch_shapes=scratch,
        compiler_params=pltpu.CompilerParams(
            collective_id=0, has_side_effects=True, vmem_limit_bytes=VMEM_LIMIT
        ),
        name="forward",
    )(inputs, lengths, *weights, proj)


def gelu_parts(x):
    k = 0.7978845608028654
    x2 = x * x
    t = jnp.tanh(k * x * (1.0 + 0.044715 * x2))
    half = 0.5 * (1.0 + t)
    return x * half, half + 0.5 * x * (1.0 - t * t) * k * (1.0 + 0.134145 * x2)


def norm_back(y, rstd, dy):
    m1 = jnp.mean(dy, axis=-1, keepdims=True)
    m2 = jnp.mean(dy * y, axis=-1, keepdims=True)
    return rstd * (dy - m1 - y * m2)


HALF = (SLAB - ROW_Q) // 2
SUM_PORTIONS = ((ROW_O, 144), (ROW_Q, 48))


class Sums:
    def __init__(self, pc, slabs, bufs, sems, l, por):
        base, self.n = SUM_PORTIONS[por]
        self.pc, self.slabs, self.l, self.por = pc, slabs, l, por
        self.sb, self.r1, self.r2, self.r3, self.keep = bufs
        self.sems = sems
        self.mine = pl.multiple_of(base + pc.c * self.n, 16)
        self.other = pl.multiple_of(base + pc.o * self.n, 16)
        self.at = pl.ds(sum(2 * n for _, n in SUM_PORTIONS[:por]) // 2, self.n)

    def copy(self, i, j, src, dst, dev):
        ssem, rsem = self.sems
        return remote(src, dst, ssem.at[self.l, self.por, i, j], rsem.at[self.l, self.por, i, j], dev)

    def to_sibling(self, g):
        src = self.slabs.at[self.l, g, pl.ds(self.other, self.n)]
        return self.copy(0, g, src, self.sb.at[self.l, g, self.at], self.pc.sibling())

    def to_second(self, j, zz, g):
        src, dst = self.sb.at[self.l, g, self.at], self.r1.at[self.l, j, zz, self.at]
        return self.copy(1, 4 * j + zz, src, dst, self.pc.at(self.pc.second, self.pc.z))

    def to_first(self, zz, g):
        src, dst = self.sb.at[self.l, g, self.at], self.r2.at[self.l, zz, self.at]
        return self.copy(2, zz, src, dst, self.pc.at(self.pc.first, self.pc.z))

    def along(self, k, g):
        src, dst = self.sb.at[self.l, g, self.at], self.r3.at[self.l, 3 - k, self.at]
        return self.copy(3, 3 - k, src, dst, self.pc.at(self.pc.d, lax.rem(self.pc.z + k, 4)))

    def begin(self):
        pc = self.pc
        for k in (1, 2, 3, 0):
            for col in (pc.diag, pc.second, pc.first, pc.d):
                self.to_sibling(col * 4 + lax.rem(pc.z + k, 4)).start()

    def pair(self, g):
        self.to_sibling(g).wait_recv()
        own = self.slabs[self.l, g, pl.ds(self.mine, self.n), :]
        return own.astype(F32) + self.sb[self.l, g, self.at, :].astype(F32)

    def stage1(self, j, i):
        pc = self.pc
        zz = lax.rem(pc.z + 1 + i, 4)
        g = (pc.diag if j == 0 else pc.second) * 4 + zz
        self.sb[self.l, g, self.at, :] = self.pair(g).astype(BF16)
        self.to_second(j, zz, g).start()

    def stage2(self, i):
        pc = self.pc
        zz = lax.rem(pc.z + 1 + i, 4)
        g = pc.first * 4 + zz
        s = self.pair(g)
        self.to_second(0, zz, g).wait_recv()
        self.sb[self.l, g, self.at, :] = (s + self.r1[self.l, 0, zz, self.at, :].astype(F32)).astype(BF16)
        self.to_first(zz, g).start()

    def stage3(self, k):
        pc = self.pc
        zz = lax.rem(pc.z + k, 4)
        g = pc.d * 4 + zz
        s = self.pair(g)
        self.to_second(1, zz, g).wait_recv()
        s = s + self.r1[self.l, 1, zz, self.at, :].astype(F32)
        self.to_first(zz, g).wait_recv()
        s = s + self.r2[self.l, zz, self.at, :].astype(F32)
        if k:
            self.sb[self.l, g, self.at, :] = s.astype(BF16)
            self.along(k, g).start()
        else:
            self.keep[self.l, self.at, :] = s

    def stage4(self, l):
        s = self.keep[l, self.at, :]
        for i in range(3):
            s = s + self.r3[l, i, self.at, :].astype(F32)
        return s

    def arrive(self):
        for k in (1, 2, 3):
            self.along(k, self.pc.me).wait_recv()

    def drain(self):
        for i in range(16):
            self.to_sibling(i).wait_send()
        for j in (0, 1):
            for zz in range(4):
                self.to_second(j, zz, 0).wait_send()
        for zz in range(4):
            self.to_first(zz, 0).wait_send()
        for k in (1, 2, 3):
            self.along(k, 0).wait_send()


def backward_kernel(
    cotangent, lengths, wq_in, wk_in, wv_in, wup_in, G_in, fq_in, fk_in, v_in, att_in, rden_in, branch_in, w_in, x_in, sin_in, pb_in,
    gin, gq_out, gk_out, gv_out, go_out, gup_out, gdown_out, gg_out,
    G, fq, fk, vext, att, rden, branch, wqk, xin, sin, pb,
    mask, mask_t, gbuf, gbr, hbuf, hT, gb, dh, gq, gk, gv, le, rin, rtail, rbuf, gains, xout, slabs,
    sb, r1, r2, r3, keep, total,
    lsem, csend, crecv, asem, ssem, rsem, fsem,
):
    pc = Place()
    c, z = pc.c, pc.z
    top, attn, ffn = pl.ds(0, 16), pl.ds(ROW_Q, ROW_UP - ROW_Q), pl.ds(ROW_UP, SLAB - ROW_UP)
    loads = {
        "branch": (lambda l: branch_in.at[l], branch), "top": (lambda l: G_in.at[l, :, top], G.at[:, top]),
        "ffn": (lambda l: G_in.at[l, :, ffn], G.at[:, ffn]), "att": (lambda l: att_in.at[l], att),
        "attn": (lambda l: G_in.at[l, :, attn], G.at[:, attn]), "rden": (lambda l: rden_in.at[l], rden),
        "fq": (lambda l: fq_in.at[l], fq), "sin": (lambda l: sin_in.at[l], sin), "fk": (lambda l: fk_in.at[l], fk),
        "vext": (lambda l: v_in.at[l], vext), "pb": (lambda l: pb_in.at[l], pb), "wqk": (lambda l: w_in.at[l], wqk),
        "xin": (lambda l: x_in.at[l], xin),
    }

    def load(l, name):
        src, dst = loads[name]
        return pltpu.make_async_copy(src(l), dst, lsem.at[list(loads).index(name)])

    def needs(l, *names):
        for name in names:
            load(l, name).wait()

    def done(l, *names):
        if l == 1:
            for name in names:
                load(0, name).start()

    pc.greet()
    for name in loads:
        load(1, name).start()

    first_row = z * 512
    rows = lax.broadcasted_iota(jnp.int32, (512, 512), 0)
    cols = lax.broadcasted_iota(jnp.int32, (512, 512), 1)
    begin, starts = last_start(lengths, c, first_row, rows)
    mask[...] = ((cols <= rows) & (cols >= begin)).astype(F32).astype(BF16)
    begin, _ = last_start(lengths, c, first_row, cols)
    mask_t[...] = ((rows <= cols) & (rows >= begin)).astype(F32).astype(BF16)
    prow = lax.broadcasted_iota(jnp.int32, (512, 1), 0)
    begin_col, _ = last_start(lengths, c, first_row, prow)
    head_col = (begin_col < 0).astype(F32)
    lane = lax.broadcasted_iota(jnp.int32, (1, 512), 1)
    begin_row, _ = last_start(lengths, c, first_row, lane)
    head_row = (begin_row < 0).astype(F32)
    inner = [jnp.where((s < 512) & (s >= 0), s, 0) for s in starts]
    cut = jnp.maximum(jnp.maximum(inner[0], inner[1]), inner[2])
    tail_col = (prow >= cut).astype(F32)

    @pl.when(z == 3)
    def _():
        rin[...] = jnp.zeros_like(rin)

    gbuf[...] = cotangent[c, 0].astype(F32)
    pc.meet()
    above = (c, pc.d, jnp.maximum(z - 1, 0))
    row_low = lax.broadcasted_iota(jnp.int32, (144, 256), 0)
    tail_is_first = (row_low < 64) | ((row_low >= 128) & (row_low < 136))
    low = lane_low((512, 128))
    ones_i = lax.broadcasted_iota(jnp.int32, (256, 128), 0)
    ones_j = lax.broadcasted_iota(jnp.int32, (256, 128), 1)
    head_ones = (lax.rem(ones_i, 128) // 64 == ones_j // 64).astype(BF16)
    scale = 64 ** (-0.25)

    def chain(l, p):
        return remote(rbuf.at[l, p], rin.at[l, p], csend.at[l, p], crecv.at[l, p], above)

    sums = {(l, por): Sums(pc, slabs, (sb, r1, r2, r3, keep), (ssem, rsem), l, por) for l in (0, 1) for por in (0, 1)}

    def put(l, row, n, value):
        slabs[l, :, row : row + n, :] = value.astype(BF16).reshape(16, n, 512)

    def layer(l, during):
        def at_point(name, *args):
            if name in during:
                during[name](*args)

        needs(l, "branch", "top")
        gains[...] = jnp.sum(G[:, 0:16, :].astype(F32), axis=0)

        def norm_tile(i, _):
            at = pl.ds(pl.multiple_of(i * 128, 128), 128)
            hbuf[at, :] = (norm(branch[at, :])[0] * gains[1:2, :]).astype(BF16)
            gb[at, :] = gbuf[at, :].astype(BF16)
            return 0

        lax.fori_loop(0, 4, norm_tile, 0)
        hT[...] = hbuf[...].T
        dh[...] = jnp.zeros_like(dh)

        def ffn_tile(j, _):
            at_point("ffn", j)
            up_at = pl.ds(pl.multiple_of(ROW_UP + 32 * j, 32), 32)
            up = G[:, up_at, :].reshape(512, 512)
            down = G[pl.ds(4 * j, 4), ROW_DOWN:SLAB, :].reshape(512, 512)
            for i in (0, 1):
                at = slice(256 * i, 256 * i + 256)
                hid, slope = gelu_parts(dot(hbuf[at, :], up))
                gq[at, :] = hid.astype(BF16)
                gk[at, :] = (slope * dot_nt(gb[at, :], down)).astype(BF16)
            slabs[l, pl.ds(4 * j, 4), ROW_DOWN:SLAB, :] = dot_tn(gq[...], gb[...]).astype(BF16).reshape(4, 128, 512)
            g = gk[...]
            slabs[l, :, up_at, :] = dot(hT[...], g).astype(BF16).reshape(16, 32, 512)
            dh[...] += dot_nt(g, up)
            return 0

        needs(l, "ffn")
        lax.fori_loop(0, 4, ffn_tile, 0)
        done(l, "top", "ffn")
        needs(l, "att")

        def branch_tile(i, _):
            at_point("branch", i)
            at = pl.ds(pl.multiple_of(i * 128, 128), 128)
            y, rstd = norm(branch[at, :])
            d = dh[at, :]
            g = gbuf[at, :] + norm_back(y, rstd, d * gains[1:2, :])
            gbr[at, :] = g
            gb[at, :] = g.astype(BF16)
            hbuf[at, :] = att[at, :].astype(BF16)
            return 0

        lax.fori_loop(0, 4, branch_tile, 0)
        done(l, "branch")
        put(l, ROW_O, 32, dot_tn(hbuf[...], gb[...]))
        sums[l, 0].begin()
        at_point("middle")
        needs(l, "attn", "rden", "fq")
        dh[...] = dot_nt(gb[...], G[:, ROW_O : ROW_O + 32, :].reshape(512, 512))

        def pass_on(p):
            chain(l, p).wait_recv()
            rbuf[l, p] = (rtail[p] + rin[l, p].astype(F32)).astype(BF16)
            chain(l, p).start()

        def tail_pair(p, _):
            at_point("tail", p)
            at = pl.ds(pl.multiple_of(p * 128, 128), 128)
            g = dh[:, at]
            r = rden[:, at]
            t = g * att[:, at]
            hi = t.astype(BF16)
            lo = (t - hi.astype(F32)).astype(BF16)
            dden = -dot(jnp.concatenate([hi, lo], axis=1), head_ones) * r
            dnum = g * r
            le[p] = jnp.concatenate([dnum, dden * (1.0 / 64.0)], axis=1).astype(BF16)
            dt = (dden.T) * head_row
            lhs = jnp.concatenate([dnum.T * head_row, dt[0:8], dt[64:72]], axis=0).astype(BF16)
            tl = jnp.where(tail_is_first, dot(lhs, fq[p, :, 0:256]), dot(lhs, fq[p, :, 256:512]))
            rtail[p] = tl

            @pl.when(z == 3)
            def _():
                rbuf[l, p] = tl.astype(BF16)
                chain(l, p).start()

            return 0

        lax.fori_loop(0, 4, tail_pair, 0)
        done(l, "att", "rden")
        needs(l, "sin", "fk", "vext", "pb", "wqk")

        def of_head(h, value):
            keep = lane_low(value.shape) if h == 0 else jnp.logical_not(lane_low(value.shape))
            return jnp.where(keep, value, jnp.zeros((), BF16))

        def through_lift(p, k, e):
            gw = dot_nt(jnp.concatenate(e, axis=1), pb[p])
            gw = gw[:, 0:128] + 2.0 * wqk[k, p].astype(F32) * gw[:, 128:256]
            return (gw * scale).astype(BF16)

        def query_pair(p, _):
            at_point("query", p)
            at = pl.ds(pl.multiple_of(p * 128, 128), 128)

            @pl.when((z == 2) & (p >= 1))
            def _():
                pass_on(p - 1)

            ve = vext[p]
            lep = le[p]
            dq = []
            for h in (0, 1):
                fl = slice(256 * h, 256 * h + 256)
                leh = of_head(h, lep)
                fkh = fk[p, :, fl]
                zrow = sin[p, 128:144, :].astype(F32)[8 * h : 8 * h + 1, :]
                st = jnp.concatenate([sin[p, 0:128, :], jnp.broadcast_to(zrow, (128, 256)).astype(BF16)], axis=0)
                dqh = head_col * dot(leh, st)
                da0 = dot_nt(leh[0:256], ve[0:256]).astype(BF16) * mask[0:256, 0:256]
                da1 = dot_nt(leh[256:512], ve).astype(BF16) * mask[256:512, :]
                dqh = dqh + jnp.concatenate([dot(da0, fkh[0:256]), dot(da1, fkh)], axis=0)
                dq.append((dqh * fq[p, :, fl].astype(F32)).astype(BF16))
            gq[:, at] = through_lift(p, 0, dq)
            return 0

        lax.fori_loop(0, 4, query_pair, 0)

        def attend_pair(p, _):
            at_point("attend", p)
            at = pl.ds(pl.multiple_of(p * 128, 128), 128)

            @pl.when((z == 2) & (p == 0))
            def _():
                pass_on(3)

            ve = vext[p]
            lep = le[p]
            dk, dv = [], []
            for h in (0, 1):
                if h == 1:
                    @pl.when(z == 1)
                    def _():
                        pass_on(p)

                fl = slice(256 * h, 256 * h + 256)
                leh = of_head(h, lep)
                fqh, fkh = fq[p, :, fl], fk[p, :, fl]
                at0 = dot_nt(fkh[0:256], fqh).astype(BF16) * mask_t[0:256, :]
                at1 = dot_nt(fkh[256:512], fqh[256:512]).astype(BF16) * mask_t[256:512, 256:512]
                dv.append(jnp.concatenate([dot(at0, lep[:, 0:128]), dot(at1, lep[256:512, 0:128])], axis=0))
                dt0 = dot_nt(ve[0:256], leh).astype(BF16) * mask_t[0:256, :]
                dt1 = dot_nt(ve[256:512], leh[256:512]).astype(BF16) * mask_t[256:512, 256:512]
                dk.append(jnp.concatenate([dot(dt0, fqh), dot(dt1, fqh[256:512])], axis=0))

            @pl.when(z == 0)
            def _():
                chain(l, p).wait_recv()

            for h in (0, 1):
                fkh = fk[p, :, 256 * h : 256 * h + 256]
                rrow = rin[l, p, 128:144, :].astype(F32)[8 * h : 8 * h + 1, :] * (1.0 / 128.0)
                rows_h = lax.broadcasted_iota(jnp.int32, (128, 256), 0) // 64 == h
                rt = jnp.where(rows_h, rin[l, p, 0:128, :], jnp.zeros((), BF16))
                rte = jnp.concatenate([rt, jnp.broadcast_to(rrow, (128, 256)).astype(BF16)], axis=0)
                dv[h] = dv[h] + tail_col * dot_nt(fkh, rin[l, p, 0:128, :])
                dk[h] = ((dk[h] + tail_col * dot(ve, rte)) * fkh.astype(F32)).astype(BF16)
            gv[:, at] = jnp.where(low, dv[0], dv[1]).astype(BF16)
            gk[:, at] = through_lift(p, 1, dk)
            return 0

        lax.fori_loop(0, 4, attend_pair, 0)
        done(l, "fq", "sin", "fk", "vext", "pb", "wqk")
        needs(l, "xin")

        def norm_tile2(i, _):
            at_point("norm", i)
            at = pl.ds(pl.multiple_of(i * 128, 128), 128)
            hbuf[at, :] = (norm(xin[at, :].astype(F32))[0] * gains[0:1, :]).astype(BF16)
            return 0

        lax.fori_loop(0, 4, norm_tile2, 0)
        hT[...] = hbuf[...].T
        for row, g in ((ROW_Q, gq), (ROW_K, gk), (ROW_V, gv)):
            put(l, row, 32, dot(hT[...], g[...]))
        sums[l, 1].begin()
        dh[...] = dot_nt(gq[...], G[:, ROW_Q : ROW_Q + 32, :].reshape(512, 512))
        dh[...] += dot_nt(gk[...], G[:, ROW_K : ROW_K + 32, :].reshape(512, 512))
        dh[...] += dot_nt(gv[...], G[:, ROW_V : ROW_V + 32, :].reshape(512, 512))

        done(l, "attn")
        at_point("late")

        def out_tile(i, _):
            at_point("out", i)
            at = pl.ds(pl.multiple_of(i * 128, 128), 128)
            y, rstd = norm(xin[at, :].astype(F32))
            d = dh[at, :]
            g = (gbr[at, :] + norm_back(y, rstd, d * gains[0:1, :])).astype(BF16)
            xout[l, at, :] = g
            gbuf[at, :] = g.astype(F32)
            return 0

        lax.fori_loop(0, 4, out_tile, 0)
        done(l, "xin")

    def four(step, *args):
        for i in range(4):
            step(*args, i)

    def along_z(m):
        for k in (1, 2, 3, 0):
            m.stage3(k)

    def both(m):
        return lambda i: (m.stage1(0, i), m.stage1(1, i))

    def at_steps(**steps):
        def run(i):
            for name, step in steps.items():
                pl.when(i == int(name[1:]))(step)

        return run

    def larger(l, extra=lambda: None):
        m = sums[l, 0]
        return {
            "tail": both(m),
            "attend": at_steps(i1=lambda: m.stage2(0), i3=lambda: (m.stage2(1), extra())[0]),
            "norm": at_steps(i0=lambda: m.stage3(1), i3=lambda: m.stage2(2)),
            "late": lambda: m.stage3(2),
            "out": at_steps(i1=lambda: m.stage2(3)),
        }

    m1, m0 = sums[1, 0], sums[0, 0]
    layer(1, {"tail": both(m1), "attend": at_steps(i1=lambda: m1.stage2(0), i3=lambda: m1.stage2(1)),
              "norm": at_steps(i3=lambda: m1.stage2(2)), "out": at_steps(i1=lambda: m1.stage2(3), i3=lambda: m1.stage3(1))})
    early = at_steps(i0=lambda: m1.stage3(2), i1=lambda: m1.stage3(3), i2=lambda: m1.stage3(0))
    hooks = larger(0, lambda: four(sums[1, 1].stage2))
    late_steps = hooks["out"]
    hooks["out"] = lambda i: (both(sums[0, 1])(i), late_steps(i))
    layer(0, {"ffn": lambda i: (early(i), both(sums[1, 1])(i)), **hooks})
    own_act = pltpu.make_async_copy(xout.at[c], gin.at[c], asem.at[0])
    own_act.start()
    far_act = remote(xout.at[pc.o], gin.at[c], asem.at[1], asem.at[2], pc.sibling())
    far_act.start()
    own_act.wait()
    far_act.wait()

    along_z(sums[1, 1])
    sums[0, 0].stage3(3)
    sums[0, 0].stage3(0)
    four(sums[0, 1].stage2)
    along_z(sums[0, 1])
    for m in sums.values():
        m.arrive()
    for por in (0, 1):
        m = sums[0, por]
        gbr[m.at, :] = m.stage4(pc.o)
    parts = []
    for por in (0, 1):
        m = sums[0, por]
        part = remote(gbr.at[m.at], total.at[pl.ds(m.mine, m.n)], fsem.at[0, por], fsem.at[1, por], pc.sibling())
        part.start()
        parts.append(part)
    for por in (0, 1):
        m = sums[0, por]
        total[pl.ds(m.mine, m.n), :] = m.stage4(c)
    for part in parts:
        part.wait()
    for ref, row in ((gq_out, ROW_Q), (gk_out, ROW_K), (gv_out, ROW_V), (go_out, ROW_O)):
        ref[...] = total[row : row + 32, :]
    for j in range(4):
        gup_out[:, 512 * j : 512 * j + 512] = total[ROW_UP + 32 * j : ROW_UP + 32 * j + 32, :]
    gdown_out[...] = total[ROW_DOWN:SLAB, :]
    ga = jnp.zeros((32, 512), F32)
    for ref, row in ((wq_in, ROW_Q), (wk_in, ROW_K), (wv_in, ROW_V)):
        ga = ga + ref[0].astype(BF16).astype(F32) * total[row : row + 32, :]
    gf = jnp.zeros((32, 512), F32)
    for j in range(4):
        up = wup_in[0, :, 512 * j : 512 * j + 512].astype(BF16).astype(F32)
        gf = gf + up * total[ROW_UP + 32 * j : ROW_UP + 32 * j + 32, :]
    gg_out[0] = jnp.broadcast_to(jnp.sum(ga, axis=1, keepdims=True), (32, 128))
    gg_out[1] = jnp.broadcast_to(jnp.sum(gf, axis=1, keepdims=True), (32, 128))
    for m in sums.values():
        m.drain()

    @pl.when(z > 0)
    def _():
        for l in (0, 1):
            for p in range(4):
                chain(l, p).wait_send()


def backward_call(cotangent, lengths, weights, saved):
    sds = jax.ShapeDtypeStruct
    dma = pltpu.SemaphoreType.DMA
    vm = pl.BlockSpec(memory_space=pltpu.VMEM)
    hbm = pl.BlockSpec(memory_space=pl.ANY)
    bufs = [pltpu.VMEM(a.shape[1:], a.dtype) for a in saved]
    full = (512, 512)
    scratch = bufs + [
        pltpu.VMEM(full, BF16),
        pltpu.VMEM(full, BF16),
        pltpu.VMEM(full, F32),
        pltpu.VMEM(full, F32),
        pltpu.VMEM(full, BF16),
        pltpu.VMEM(full, BF16),
        pltpu.VMEM(full, BF16),
        pltpu.VMEM(full, F32),
        pltpu.VMEM(full, BF16),
        pltpu.VMEM(full, BF16),
        pltpu.VMEM(full, BF16),
        pltpu.VMEM((4, 512, 256), BF16),
        pltpu.VMEM((2, 4, 144, 256), BF16),
        pltpu.VMEM((4, 144, 256), F32),
        pltpu.VMEM((2, 4, 144, 256), BF16),
        pltpu.VMEM((16, 512), F32),
        pltpu.VMEM((2, 512, 512), BF16),
        pltpu.VMEM((2, 16, SLAB, 512), BF16),
        pltpu.VMEM((2, 16, HALF, 512), BF16),
        pltpu.VMEM((2, 2, 4, HALF, 512), BF16),
        pltpu.VMEM((2, 4, HALF, 512), BF16),
        pltpu.VMEM((2, 3, HALF, 512), BF16),
        pltpu.VMEM((2, HALF, 512), F32),
        pltpu.VMEM((SLAB, 512), F32),
        dma((13,)), dma((2, 4)), dma((2, 4)), dma((3,)), dma((2, 2, 4, 16)), dma((2, 2, 4, 16)), dma((2, 2)),
    ]
    return pl.pallas_call(
        backward_kernel,
        out_shape=[sds((2, 512, 512), BF16)]
        + [sds((32, 512), F32)] * 4
        + [sds((32, 2048), F32), sds((128, 512), F32), sds((2, 32, 128), F32)],
        in_specs=[vm, pl.BlockSpec(memory_space=pltpu.SMEM)] + [vm] * 4 + [hbm] * len(saved),
        out_specs=[vm] * 8,
        scratch_shapes=scratch,
        compiler_params=pltpu.CompilerParams(
            collective_id=1, has_side_effects=True, vmem_limit_bytes=VMEM_LIMIT
        ),
        name="backward",
    )(cotangent, lengths, *weights, *saved)


def finish_kernel(*refs):
    n = len(refs) // 2
    ins, outs, sems = refs[:n], refs[n : 2 * n - 1], refs[2 * n - 1 :]
    sums, ga, gf = ins[n - 3 :]
    copies = [pltpu.make_async_copy(src, dst, sems[0].at[i]) for i, (src, dst) in enumerate(zip(ins[: n - 3], outs))]
    for copy in copies:
        copy.start()
    for i, gain in ((0, ga), (1, gf)):
        outs[n - 3 + i][...] = sums[i].T[0:1, 0:32] / gain[...].astype(BF16).astype(F32)
    for copy in copies:
        copy.wait()


def finish_call(results, sums, gain_attn, gain_ffn):
    vm = pl.BlockSpec(memory_space=pltpu.VMEM)
    hbm = pl.BlockSpec(memory_space=pl.ANY)
    n = len(results)
    return pl.pallas_call(
        finish_kernel,
        out_shape=[jax.ShapeDtypeStruct(r.shape, r.dtype) for r in results + [gain_attn, gain_ffn]],
        in_specs=[hbm] * n + [vm] * 3,
        out_specs=[vm] * (n + 2),
        scratch_shapes=[pltpu.SemaphoreType.DMA((n,))],
        name="finish",
    )(*results, sums, gain_attn, gain_ffn)


def fast_local(inputs, cotangent, doc_lengths, feature_proj, *weights):
    act, *saved = forward_call(inputs, doc_lengths, weights, feature_proj)
    w_query, w_key, w_value, _, w_up = weights[:5]
    gin, *grads = backward_call(cotangent, doc_lengths, (w_query, w_key, w_value, w_up), saved)
    done = finish_call([act, gin] + grads[:6], grads[6], weights[6], weights[7])
    return (done[0][None, :, None], done[1][None, :, None]) + tuple(g[None] for g in done[2:8]) + tuple(done[8:])


HIGH_PRECISION = lax.Precision.HIGHEST


def prefix(shard, axis, join, neutral):
    place = lax.axis_index(axis)
    gathered = jax.tree.map(
        lambda a, kind: lax.all_gather(a.astype(kind), axis),
        shard,
        (jnp.bfloat16, jnp.bfloat16, jnp.bfloat16),
    )
    state = jax.tree.map(lambda a, e: jnp.zeros_like(a) + jnp.asarray(e, a.dtype), shard, neutral)

    def prefix_one(lap, state):
        return join(
            state,
            jax.tree.map(
                lambda a, own: lax.dynamic_index_in_dim(a, lap, 0, False).astype(own.dtype),
                gathered,
                shard,
            ),
        )

    return lax.fori_loop(0, place, prefix_one, state)


def entering(shard, axis, join, neutral):
    count = lax.axis_size(axis)
    place = lax.axis_index(axis)
    ahead = count - 1 - place
    gathered = jax.tree.map(
        lambda a, kind: lax.all_gather(a.astype(kind), axis),
        shard,
        jax.tree.map(lambda a: jnp.bfloat16 if a.dtype == jnp.float32 else a.dtype, shard),
    )
    state = jax.tree.map(lambda a, e: jnp.zeros_like(a) + jnp.asarray(e, a.dtype), shard, neutral)

    def entering_one(lap, state):
        source = count - 1 - lap
        return join(
            state,
            jax.tree.map(
                lambda a, own: lax.dynamic_index_in_dim(a, source, 0, False).astype(own.dtype),
                gathered,
                shard,
            ),
        )

    return lax.fori_loop(0, ahead, entering_one, state)


def as_sent(shard):

    def short(part):
        return part.astype(jnp.bfloat16) if part.dtype == jnp.float32 else part

    return jax.tree.map(short, shard)


def passed_along(block, axis, distance):
    devices = range(lax.axis_size(axis))
    route = [(i - distance, i) for i in devices if i - distance in devices]
    return lax.ppermute(block, axis, route)


def matmul(left, right):
    return jnp.dot(left, right, preferred_element_type=jnp.float32)


def norm_rows(values):
    centre = values - jnp.mean(values, axis=-1, keepdims=True)
    return centre * lax.rsqrt(jnp.mean(centre * centre, axis=-1, keepdims=True) + 1e-05)


def lift(values, projection):
    heads, depth, feats = projection.shape
    scaled = values.reshape(values.shape[0], heads, depth) * depth ** (-0.25)
    raised = jnp.einsum("nhd,hdm->nhm", scaled, projection, precision=HIGH_PRECISION)
    return jnp.exp(raised - 0.5 * jnp.sum(scaled * scaled, axis=-1, keepdims=True)) * feats ** (
        -0.5
    )


def doc_masks(lengths, first_row, row_count):
    doc_ends = jnp.cumsum(lengths, dtype=jnp.int32)
    starts = doc_ends - lengths
    positions = first_row + jnp.arange(row_count, dtype=jnp.int32)
    begun_at = starts[None, :] <= positions[:, None]
    doc_ids = jnp.sum(begun_at.astype(jnp.int32), axis=1)
    order_idx = jnp.arange(row_count, dtype=jnp.int32)
    same_doc = (
        (doc_ids[:, None] == doc_ids[None, :]) & (order_idx[None, :] <= order_idx[:, None])
    ).astype(jnp.float32)
    inside = (starts >= first_row) & (starts < first_row + row_count)
    mask_per_head = (jnp.sum((begun_at & inside[None, :]).astype(jnp.int32), axis=1) == 0).astype(
        jnp.float32
    )
    tail_mask = (jnp.sum((~begun_at & inside[None, :]).astype(jnp.int32), axis=1) == 0).astype(
        jnp.float32
    )
    kept_flag = (jnp.sum(inside.astype(jnp.int32)) == 0).astype(jnp.float32)
    return (same_doc, mask_per_head, tail_mask, kept_flag)


def attend(query_features, feats_k, value_heads, incoming_state, norm_in, same_doc, mask_per_head):
    scores = (
        jnp.einsum("thm,shm->hts", query_features, feats_k, precision=HIGH_PRECISION)
        * same_doc[None]
    )
    attention_numerator = jnp.einsum("hts,shd->thd", scores, value_heads, precision=HIGH_PRECISION)
    attention_numerator = attention_numerator + mask_per_head[:, None, None] * jnp.einsum(
        "kec,ecz->kez", query_features, incoming_state, precision=HIGH_PRECISION
    )
    denominator = jnp.sum(scores, axis=2).T + mask_per_head[:, None] * jnp.einsum(
        "thm,hm->th", query_features, norm_in, precision=HIGH_PRECISION
    )
    return (attention_numerator / denominator[:, :, None]).reshape(query_features.shape[0], -1)


def tail_sums(feats_k, value_heads, tail_mask):
    weighted_values = feats_k * tail_mask[:, None, None]
    return (
        jnp.einsum("zlu,zlv->luv", weighted_values, value_heads, precision=HIGH_PRECISION),
        jnp.sum(weighted_values, axis=0),
    )


def combine_carry(earlier, later_part):
    return (
        earlier[0] * later_part[0],
        later_part[1] + later_part[0] * earlier[1],
        later_part[2] + later_part[0] * earlier[2],
    )


def run_forward(layer_in, weights, projection, lengths, first_row):
    w_query, w_key, w_value, w_out, w_up, w_down, gain_attn, gain_ffn = weights
    row_count = layer_in.shape[0]
    same_doc, mask_per_head, tail_mask, kept_flag = doc_masks(lengths, first_row, row_count)
    h_attn = (norm_rows(layer_in) * gain_attn.astype(jnp.float32)).astype(jnp.bfloat16)
    query_features = lift(matmul(h_attn, w_query), projection)
    feats_k = lift(matmul(h_attn, w_key), projection)
    value_heads = matmul(h_attn, w_value).reshape(row_count, projection.shape[0], -1)
    state_tail, norm_tail = tail_sums(feats_k, value_heads, tail_mask)
    identity = (jnp.ones((), jnp.float32), jnp.zeros_like(state_tail), jnp.zeros_like(norm_tail))
    _, incoming_state, norm_in = prefix(
        (kept_flag, state_tail, norm_tail), "seq", combine_carry, identity
    )
    mixed_heads = attend(
        query_features, feats_k, value_heads, incoming_state, norm_in, same_doc, mask_per_head
    ).astype(jnp.bfloat16)
    branch = layer_in + matmul(mixed_heads, w_out)
    h_ffn = (norm_rows(branch) * gain_ffn.astype(jnp.float32)).astype(jnp.bfloat16)
    hidden = jax.nn.gelu(matmul(h_ffn, w_up)).astype(jnp.bfloat16)
    return (branch + matmul(hidden, w_down), incoming_state, norm_in)


def run_backward(
    layer_in, incoming_state, norm_in, grad_out, weights, projection, lengths, first_row
):
    w_query, w_key, w_value, w_out, w_up, w_down, gain_attn, gain_ffn = weights
    row_count = layer_in.shape[0]
    same_doc, mask_per_head, tail_mask, kept_flag = doc_masks(lengths, first_row, row_count)
    gain_a = gain_attn.astype(jnp.float32)
    gain_f = gain_ffn.astype(jnp.float32)
    normed_a, norm_a_back = jax.vjp(norm_rows, layer_in)
    h_attn = (normed_a * gain_a).astype(jnp.bfloat16)
    query_features, lift_q_back = jax.vjp(lambda z: lift(z, projection), matmul(h_attn, w_query))
    feats_k, lift_k_back = jax.vjp(lambda z: lift(z, projection), matmul(h_attn, w_key))
    value_heads = matmul(h_attn, w_value).reshape(row_count, projection.shape[0], -1)
    attended, attend_back = jax.vjp(
        lambda a, b, c, d, e: attend(a, b, c, d, e, same_doc, mask_per_head),
        query_features,
        feats_k,
        value_heads,
        incoming_state,
        norm_in,
    )
    mixed_heads = attended.astype(jnp.bfloat16)
    branch = layer_in + matmul(mixed_heads, w_out)
    normed_f, norm_f_back = jax.vjp(norm_rows, branch)
    h_ffn = (normed_f * gain_f).astype(jnp.bfloat16)
    activated, gelu_back = jax.vjp(jax.nn.gelu, matmul(h_ffn, w_up))
    hidden = activated.astype(jnp.bfloat16)
    grad_low = grad_out.astype(jnp.bfloat16)
    grad_wdown = matmul(hidden.T, grad_low)
    grad_pre = gelu_back(matmul(grad_low, w_down.T))[0].astype(jnp.bfloat16)
    grad_wup = matmul(h_ffn.T, grad_pre)
    grad_hffn = matmul(grad_pre, w_up.T)
    grad_gain_f = jnp.sum(grad_hffn * normed_f, axis=0)
    ffn_terms = (grad_wup, grad_wdown, grad_gain_f)
    grad_branch = grad_out + norm_f_back(grad_hffn * gain_f)[0]
    grad_blow = grad_branch.astype(jnp.bfloat16)
    grad_wout = matmul(mixed_heads.T, grad_blow)
    grad_fq, grad_fk, grad_vals, grad_state, grad_norm = attend_back(matmul(grad_blow, w_out.T))
    identity = (jnp.ones((), jnp.float32), jnp.zeros_like(grad_state), jnp.zeros_like(grad_norm))
    _, carry_state, carry_norm = entering(
        (kept_flag, grad_state, grad_norm), "seq", combine_carry, identity
    )
    _, tail_back = jax.vjp(lambda a, b: tail_sums(a, b, tail_mask), feats_k, value_heads)
    more_k, more_v = tail_back((carry_state, carry_norm))
    grad_q = lift_q_back(grad_fq)[0].astype(jnp.bfloat16)
    grad_k = lift_k_back(grad_fk + more_k)[0].astype(jnp.bfloat16)
    grad_v = (grad_vals + more_v).reshape(row_count, -1).astype(jnp.bfloat16)
    grad_hattn = matmul(grad_q, w_query.T) + matmul(grad_k, w_key.T) + matmul(grad_v, w_value.T)
    grad_gain_a = jnp.sum(grad_hattn * normed_a, axis=0)
    grad_in = grad_branch + norm_a_back(grad_hattn * gain_a)[0]
    attn_grads = (
        matmul(h_attn.T, grad_q),
        matmul(h_attn.T, grad_k),
        matmul(h_attn.T, grad_v),
        grad_wout,
        grad_gain_a,
    )
    return (grad_in, attn_grads, ffn_terms)


def local(
    inputs,
    cotangent,
    doc_lengths,
    feature_proj,
    w_query,
    w_key,
    w_value,
    w_out,
    w_up,
    w_down,
    gain_attn,
    gain_ffn,
):
    section_idx = lax.axis_index("section")
    seq_idx = lax.axis_index("seq")
    micro_count, _, row_count, feat_width = inputs.shape
    first_row = seq_idx * row_count
    projection = feature_proj[0]
    lengths_all = doc_lengths[:, 0, :]
    masters = (
        w_query[0],
        w_key[0],
        w_value[0],
        w_out[0],
        w_up[0],
        w_down[0],
        gain_attn[0],
        gain_ffn[0],
    )
    lowered = tuple((master.astype(jnp.bfloat16) for master in masters))
    gathered = jax.tree.map(
        lambda part, own: part.astype(own.dtype),
        lax.all_gather(as_sent(lowered), ("dp", "seq"), axis=0, tiled=True),
        lowered,
    )
    batch_range = jnp.arange(micro_count, dtype=jnp.int32)
    received = jnp.zeros((row_count, feat_width), jnp.bfloat16)
    outputs = jnp.zeros((micro_count, row_count, feat_width), jnp.float32)
    kept_inputs, kept_states, kept_norms = ([], [], [])
    for step_no in range(micro_count + 1):
        batch_no = step_no - section_idx
        is_valid = ((batch_no >= 0) & (batch_no < micro_count)).astype(jnp.float32)
        batch_idx = jnp.clip(batch_no, 0, micro_count - 1)
        own_input = inputs[min(step_no, micro_count - 1), 0].astype(jnp.float32)
        layer_in = jnp.where(section_idx == 0, own_input, received.astype(jnp.float32))
        lengths = lax.dynamic_index_in_dim(lengths_all, batch_idx, 0, keepdims=False)
        layer_out, incoming_state, norm_in = run_forward(
            layer_in, gathered, projection, lengths, first_row
        )
        sent_out = layer_out.astype(jnp.bfloat16)
        chosen = (batch_range == batch_idx).astype(jnp.float32) * is_valid
        outputs = outputs + chosen[:, None, None] * sent_out.astype(jnp.float32)[None]
        kept_inputs.append(layer_in)
        kept_states.append(incoming_state)
        kept_norms.append(norm_in)
        if step_no < micro_count:
            received = passed_along(sent_out, "section", 1)
    weights_back = jax.tree.map(
        lambda part, own: part.astype(own.dtype),
        lax.all_gather(as_sent(lowered), ("dp", "seq"), axis=0, tiled=True),
        lowered,
    )
    stacked_inputs = jnp.stack(kept_inputs)
    stacked_states = jnp.stack(kept_states)
    stacked_norms = jnp.stack(kept_norms)
    grad_recv = jnp.zeros((row_count, feat_width), jnp.bfloat16)
    grad_inputs = jnp.zeros((micro_count, row_count, feat_width), jnp.float32)
    totals = tuple((jnp.zeros(part.shape, jnp.float32) for part in weights_back))
    for step_no in range(micro_count + 1):
        batch_no = step_no - 1 + section_idx
        is_valid = ((batch_no >= 0) & (batch_no < micro_count)).astype(jnp.float32)
        batch_idx = jnp.clip(batch_no, 0, micro_count - 1)
        slot_idx = jnp.clip(step_no - 1 + 2 * section_idx, 0, micro_count)
        layer_in = lax.dynamic_index_in_dim(stacked_inputs, slot_idx, 0, keepdims=False)
        incoming_state = lax.dynamic_index_in_dim(stacked_states, slot_idx, 0, keepdims=False)
        norm_in = lax.dynamic_index_in_dim(stacked_norms, slot_idx, 0, keepdims=False)
        own_grad = cotangent[min(step_no, micro_count - 1), 0].astype(jnp.float32)
        grad_out = jnp.where(section_idx == 1, own_grad, grad_recv.astype(jnp.float32))
        lengths = lax.dynamic_index_in_dim(lengths_all, batch_idx, 0, keepdims=False)
        grad_in, attn_grads, ffn_terms = run_backward(
            layer_in,
            incoming_state,
            norm_in,
            grad_out,
            weights_back,
            projection,
            lengths,
            first_row,
        )
        grads = (
            attn_grads[0],
            attn_grads[1],
            attn_grads[2],
            attn_grads[3],
            ffn_terms[0],
            ffn_terms[1],
            attn_grads[4],
            ffn_terms[2],
        )
        totals = tuple(
            (total_part + is_valid * grad_part for total_part, grad_part in zip(totals, grads))
        )
        sent_back = grad_in.astype(jnp.bfloat16)
        chosen = (batch_range == batch_idx).astype(jnp.float32) * is_valid
        grad_inputs = grad_inputs + chosen[:, None, None] * sent_back.astype(jnp.float32)[None]
        if step_no < micro_count:
            grad_recv = passed_along(sent_back, "section", -1)
    shares = lax.psum_scatter(totals, ("dp", "seq"), scatter_dimension=0, tiled=True)
    activations = outputs.astype(jnp.bfloat16)[None, :, None]
    input_grad = grad_inputs.astype(jnp.bfloat16)[None, :, None]
    return (activations, input_grad) + tuple((share_part[None] for share_part in shares))


def solution(mesh):
    in_specs = (
        P(None, "dp", "seq", None),
        P(None, "dp", "seq", None),
        P(None, "dp", None),
        P("section", None, None, None),
        P("section", ("dp", "seq"), None),
        P("section", ("dp", "seq"), None),
        P("section", ("dp", "seq"), None),
        P("section", ("dp", "seq"), None),
        P("section", ("dp", "seq"), None),
        P("section", ("dp", "seq"), None),
        P("section", ("dp", "seq")),
        P("section", ("dp", "seq")),
    )
    out_specs = (
        P("section", None, "dp", "seq", None),
        P("section", None, "dp", "seq", None),
        P("section", ("dp", "seq"), None),
        P("section", ("dp", "seq"), None),
        P("section", ("dp", "seq"), None),
        P("section", ("dp", "seq"), None),
        P("section", ("dp", "seq"), None),
        P("section", ("dp", "seq"), None),
        P("section", ("dp", "seq")),
        P("section", ("dp", "seq")),
    )
    fits = mesh.shape["section"] == 2 and mesh.shape["dp"] == 4 and mesh.shape["seq"] == 4
    body = fast_local if fits else local
    return jax.shard_map(body, mesh=mesh, in_specs=in_specs, out_specs=out_specs, check_vma=False)
```

```python
import functools

import jax
import jax.numpy as jnp
from jax import lax
from jax.experimental import pallas as pl
from jax.experimental.pallas import tpu as pltpu
from jax.sharding import PartitionSpec as P

MESH = pl.DeviceIdType.MESH
F32 = jnp.float32
BF16 = jnp.bfloat16
VMEM_LIMIT = 63 << 20

ROW_Q, ROW_K, ROW_V, ROW_O, ROW_UP, ROW_DOWN, SLAB = 0, 32, 64, 96, 128, 256, 384
PORTIONS = ((0, 48), (96, 144))


def dot(a, b):
    return lax.dot_general(a, b, (((1,), (0,)), ((), ())), preferred_element_type=F32)


def dot_nt(a, b):
    return lax.dot_general(a, b, (((1,), (1,)), ((), ())), preferred_element_type=F32)


def dot_tn(a, b):
    return lax.dot_general(a, b, (((0,), (0,)), ((), ())), preferred_element_type=F32)


def remote(src, dst, ssem, rsem, dev):
    return pltpu.make_async_remote_copy(
        src_ref=src, dst_ref=dst, send_sem=ssem, recv_sem=rsem, device_id=dev, device_id_type=MESH
    )


class Place:
    def __init__(self):
        self.c = lax.axis_index("section")
        self.d = lax.axis_index("dp")
        self.z = lax.axis_index("seq")
        self.o = 1 - self.c
        self.xn = self.d + 1 - 2 * lax.rem(self.d, 2)
        self.yn = lax.rem(self.d + 2, 4)
        self.first = self.xn + self.c * (self.yn - self.xn)
        self.second = self.yn + self.c * (self.xn - self.yn)
        self.diag = 3 - self.d
        self.me = self.d * 4 + self.z

    def at(self, d, z):
        return (self.c, d, z)

    def sibling(self):
        return (self.o, self.d, self.z)

    def peers(self):
        out = [self.sibling(), self.at(self.xn, self.z), self.at(self.yn, self.z)]
        return out + [self.at(self.d, lax.rem(self.z + k, 4)) for k in (1, 2, 3)]

    def greet(self):
        for dev in self.peers():
            pl.semaphore_signal(pltpu.get_barrier_semaphore(), inc=1, device_id=dev, device_id_type=MESH)

    def meet(self):
        pl.semaphore_wait(pltpu.get_barrier_semaphore(), len(self.peers()))


def weight(G, l, row, n=32):
    return G[l, :, row : row + n, :].reshape(16 * n, 512)


class Gather:
    def __init__(self, pc, G, l, por, ssem, rsem, dsend, drecv, tiles=None):
        base, self.n = PORTIONS[por]
        self.pc, self.G, self.l, self.por = pc, G, l, por
        self.sems = ssem, rsem, dsend, drecv
        self.tiles = tiles
        self.start = pl.multiple_of(base + pc.c * self.n, 16)
        self.other = pl.multiple_of(base + pc.o * self.n, 16)

    def ref(self, g):
        return self.G.at[self.l, g, pl.ds(self.start, self.n)]

    def link(self, g, i, dev):
        ssem, rsem, _, _ = self.sems
        return remote(self.ref(g), self.ref(g), ssem.at[self.l, self.por, i], rsem.at[self.l, self.por, g], dev)

    def tile(self, g, i, dev):
        ref, tsend, trecv = self.tiles
        return remote(ref.at[g], ref.at[g], tsend.at[i], trecv.at[g], dev)

    def pass_to(self, g, i, dev):
        self.link(g, i, dev).start()
        if self.tiles:
            self.tile(g, i, dev).start()

    def sib(self, g):
        _, _, dsend, drecv = self.sems
        return remote(
            self.ref(g), self.ref(g), dsend.at[self.l, self.por, g], drecv.at[self.l, self.por, g], self.pc.sibling()
        )

    def arrive(self, g):
        self.link(g, 0, self.pc.sibling()).wait_recv()
        if self.tiles:
            self.tile(g, 0, self.pc.sibling()).wait_recv()

    def own(self):
        pc = self.pc
        for k in (2, 1, 3):
            self.pass_to(pc.me, k, pc.at(pc.d, lax.rem(pc.z + k, 4)))
        self.pass_to(pc.me, 4, pc.at(pc.first, pc.z))
        self.pass_to(pc.me, 8, pc.at(pc.second, pc.z))

    def column(self, k):
        pc = self.pc

        def step():
            g = pc.d * 4 + lax.rem(pc.z + k, 4)
            self.arrive(g)
            self.pass_to(g, 4 + k, pc.at(pc.first, pc.z))
            self.pass_to(g, 8 + k, pc.at(pc.second, pc.z))
            self.sib(g).start()

        if not isinstance(k, int):
            pl.when(k > 0)(step)
        elif k > 0:
            step()

    def across(self, k):
        pc = self.pc
        g = pc.first * 4 + lax.rem(pc.z + k, 4)
        self.arrive(g)
        self.pass_to(g, 12 + k, pc.at(pc.second, pc.z))
        self.sib(g).start()

    def far(self, k):
        pc = self.pc
        zz = lax.rem(pc.z + k, 4)
        for dp in (pc.second, pc.diag):
            g = dp * 4 + zz
            self.arrive(g)
            self.sib(g).start()

    def finish(self):
        _, _, dsend, drecv = self.sems
        pc = self.pc

        def wait(g):
            ref = self.G.at[self.l, g, pl.ds(self.other, self.n)]
            remote(ref, ref, dsend.at[self.l, self.por, g], drecv.at[self.l, self.por, g], pc.sibling()).wait_recv()

        def step(i, _):
            wait(lax.rem(pc.me + 1 + i, 16))
            return 0

        lax.fori_loop(0, 15, step, 0)

    def drain(self):
        pc = self.pc

        def step(i, _):
            self.link(pc.me, 1 + i, pc.at(pc.first, pc.z)).wait_send()
            if self.tiles:
                self.tile(pc.me, 1 + i, pc.at(pc.first, pc.z)).wait_send()
            self.sib(lax.rem(pc.me + 1 + i, 16)).wait_send()
            return 0

        lax.fori_loop(0, 15, step, 0)


def last_start(lengths, c, first_row, pos):
    starts = []
    at = 0
    for i in range(3):
        at = at + lengths[c, 0, i]
        starts.append(at - first_row)
    out = jnp.full(pos.shape, -first_row, jnp.int32)
    for s in starts:
        out = jnp.where(pos >= s, s, out)
    return out, starts


def norm(x):
    c = x - jnp.mean(x, axis=-1, keepdims=True)
    rstd = lax.rsqrt(jnp.mean(c * c, axis=-1, keepdims=True) + 1e-05)
    return c * rstd, rstd


def lane_low(shape):
    return lax.rem(lax.broadcasted_iota(jnp.int32, shape, 1), 128) < 64


def lift_pair(w, proj):
    hi = w.astype(BF16)
    low = (w - hi.astype(F32)).astype(BF16)
    sq = (w * w).astype(BF16)
    e = dot(jnp.concatenate([hi, sq, low, hi], axis=1), proj)
    return (jnp.exp(e) * 0.0625).astype(BF16)


def forward_kernel(
    inputs, lengths, wq_in, wk_in, wv_in, wo_in, wup_in, wdown_in, ga_in, gf_in, proj,
    act, G_out, fq_out, fk_out, v_out, att_out, rden_out, branch_out, w_out, x_out, sin_out, pb_out, gains_out,
    G, px, pk, mask, xbuf, hbuf, qbuf, kbuf, fq, fk, vext, att, rden, branch, wqk, xin, sin, tail, sbuf,
    gains, ybuf, hf, acc, tile_a, tile_b, tiles,
    ssem, rsem, dsend, drecv, osem, osem2, psem, csend, crecv, asem, wsem, gsend, grecv,
):
    pc = Place()
    c, z = pc.c, pc.z
    pc.greet()
    tile_a[...] = jnp.zeros_like(tile_a)
    tile_a[0:1, 0:32] = ga_in[...]
    tile_a[1:2, 0:32] = gf_in[...]
    placed = pltpu.roll(pltpu.roll(tile_a[...], 32 * z, 1), 2 * c, 0)
    tile_b[0] = placed.astype(BF16)
    for ref, row in ((wq_in, ROW_Q), (wk_in, ROW_K), (wv_in, ROW_V), (wo_in, ROW_O)):
        G[c, pc.me, row : row + 32, :] = ref[0].astype(BF16)
    for j in range(4):
        row = ROW_UP + 32 * j
        G[c, pc.me, row : row + 32, :] = wup_in[0, :, 512 * j : 512 * j + 512].astype(BF16)
    G[c, pc.me, ROW_DOWN:SLAB, :] = wdown_in[0].astype(BF16)
    hi = proj[0].astype(BF16)
    px[c, 0] = hi
    px[c, 1] = (proj[0] - hi.astype(F32)).astype(BF16)
    pc.meet()
    halves = {}
    for por, (base, n) in enumerate(PORTIONS):
        for half, at in ((0, pc.o), (1, c)):
            ref = G.at[c, pc.me, pl.ds(pl.multiple_of(base + at * n, 16), n)]
            halves[por, half] = remote(ref, ref, osem2.at[0, por, half], osem2.at[1, por, half], pc.sibling())
            halves[por, half].start()
    tsend = remote(tile_b.at[0], tile_b.at[1], psem.at[2], psem.at[3], pc.sibling())
    tsend.start()
    psend = remote(px.at[c], px.at[c], psem.at[0], psem.at[1], pc.sibling())
    psend.start()
    moves = {
        (l, por): Gather(
            pc, G, l, por, ssem, rsem, dsend, drecv, (tiles, gsend, grecv) if l == 0 and por == 0 else None
        )
        for l in (0, 1)
        for por in range(2)
    }

    def four(step):
        for k in range(4):
            step(k)

    for por in (0, 1):
        for half in (0, 1):
            halves[por, half].wait()
    tsend.wait()
    tiles[pc.me] = (tile_b[0].astype(F32) + tile_b[1].astype(F32)).astype(BF16)
    moves[0, 0].own()

    first_row = z * 512
    rows = lax.broadcasted_iota(jnp.int32, (512, 512), 0)
    cols = lax.broadcasted_iota(jnp.int32, (512, 512), 1)
    begin, starts = last_start(lengths, c, first_row, rows)
    mask[...] = ((cols <= rows) & (cols >= begin)).astype(F32)
    prow = lax.broadcasted_iota(jnp.int32, (512, 1), 0)
    begin_col, _ = last_start(lengths, c, first_row, prow)
    head_mask = (begin_col < 0).astype(F32)
    lane = lax.broadcasted_iota(jnp.int32, (1, 512), 1)
    inner = [jnp.where((s < 512) & (s >= 0), s, 0) for s in starts]
    cut = jnp.maximum(jnp.maximum(inner[0], inner[1]), inner[2])
    tail_mask = (lane >= cut).astype(F32)

    moves[0, 1].own()
    psend.wait()
    pk[...] = jnp.zeros_like(pk)
    for l in (0, 1):
        for p in range(4):
            for h in (0, 1):
                at = slice(64 * h, 64 * h + 64)
                to = slice(256 * h, 256 * h + 256)
                pk[l, p, at, to] = px[l, 0, 2 * p + h]
                pk[l, p, 128 + 64 * h : 192 + 64 * h, to] = jnp.full((64, 256), -0.5, BF16)
                pk[l, p, 256 + 64 * h : 320 + 64 * h, to] = px[l, 0, 2 * p + h]
                pk[l, p, 384 + 64 * h : 448 + 64 * h, to] = px[l, 1, 2 * p + h]
    keep = pltpu.make_async_copy(pk.at[:, :, 0:256, :], pb_out, osem)
    keep.start()
    vext[:, :, :, 128:] = jnp.ones((2, 4, 512, 128), BF16)

    @pl.when(z == 0)
    def _():
        sin[...] = jnp.zeros_like(sin)

    xbuf[...] = inputs[c, 0].astype(F32)
    four(moves[0, 0].column)
    moves[1, 0].own()
    four(moves[0, 0].across)
    moves[1, 1].own()
    four(moves[0, 1].column)
    four(moves[0, 0].far)
    four(moves[0, 1].across)
    moves[0, 0].finish()
    for dp in range(4):
        gains[:, 128 * dp : 128 * dp + 128] = jnp.sum(tiles[4 * dp : 4 * dp + 4].astype(F32), axis=0)
    gains_out[...] = gains[...]
    below = (c, pc.d, jnp.minimum(z + 1, 3))
    low = lane_low((512, 128))
    row_low = lax.broadcasted_iota(jnp.int32, (144, 256), 0)
    tail_is_first = (row_low < 64) | ((row_low >= 128) & (row_low < 136))
    low256 = lane_low((256, 128))

    def chain(l, p):
        return remote(sbuf.at[l, p], sin.at[l, p], csend.at[l, p], crecv.at[l, p], below)

    saved = (
        (G, G_out), (fq, fq_out), (fk, fk_out), (vext, v_out), (att, att_out), (rden, rden_out),
        (branch, branch_out), (wqk, w_out), (xin, x_out), (sin, sin_out),
    )

    def save(l, *refs):
        for i, (src, dst) in enumerate(saved):
            if any(src is ref for ref in refs):
                pltpu.make_async_copy(src.at[l], dst.at[l], wsem.at[l, i]).start()

    def give_own(l):
        return pltpu.make_async_copy(ybuf.at[l], act.at[c], asem.at[0])

    def give_far(l):
        return remote(ybuf.at[l], act.at[c], asem.at[1], asem.at[2], pc.sibling())

    def give(l):
        pl.when(c == l)(lambda: give_own(l).start())
        pl.when(c != l)(lambda: give_far(l).start())

    def layer(l, during):
        def norm_tile(i, _):
            at = pl.ds(pl.multiple_of(i * 128, 128), 128)
            x = xbuf[at, :]
            xin[l, at, :] = x.astype(BF16)
            hbuf[at, :] = (norm(x)[0] * gains[2 * l : 2 * l + 1, :]).astype(BF16)
            return 0

        lax.fori_loop(0, 4, norm_tile, 0)
        scale = 64 ** (-0.25)
        kbuf[...] = dot(hbuf[...], weight(G, l, ROW_K)) * scale
        qbuf[...] = dot(hbuf[...], weight(G, l, ROW_V))

        def pass_on(p):
            chain(l, p).wait_recv()
            sbuf[l, p] = (tail[p] + sin[l, p].astype(F32)).astype(BF16)
            chain(l, p).start()

        def key_pair(p, _):
            if "key" in during:
                during["key"](p)
            at = pl.ds(pl.multiple_of(p * 128, 128), 128)
            w = kbuf[:, at]
            wqk[l, 1, p] = w.astype(BF16)
            f = lift_pair(w, pk[l, p])
            fk[l, p] = f
            v = qbuf[:, at]
            vext[l, p, :, 0:128] = v.astype(BF16)
            vt = jnp.concatenate([v.T * tail_mask, jnp.broadcast_to(tail_mask, (16, 512))], axis=0).astype(BF16)
            t = jnp.where(tail_is_first, dot(vt, f[:, 0:256]), dot(vt, f[:, 256:512]))
            tail[p] = t

            @pl.when(z == 0)
            def _():
                sbuf[l, p] = t.astype(BF16)
                chain(l, p).start()

            @pl.when((z == 1) & (p >= 2))
            def _():
                pass_on(p - 2)

            return 0

        lax.fori_loop(0, 4, key_pair, 0)
        save(l, fk, vext, xin)
        qbuf[...] = dot(hbuf[...], weight(G, l, ROW_Q)) * scale

        def query_pair(p, _):
            if "query" in during:
                during["query"](p)
            at = pl.ds(pl.multiple_of(p * 128, 128), 128)
            w = qbuf[:, at]
            wqk[l, 0, p] = w.astype(BF16)
            fq[l, p] = lift_pair(w, pk[l, p])

            @pl.when((z == 1) & (p < 2))
            def _():
                pass_on(p + 2)

            @pl.when((z == 2) & (p >= 1))
            def _():
                pass_on(p - 1)

            return 0

        lax.fori_loop(0, 4, query_pair, 0)
        save(l, fq, wqk)

        def attend_pair(p, _):
            if "attend" in during:
                during["attend"](p)
            at = pl.ds(pl.multiple_of(p * 128, 128), 128)

            @pl.when((z == 2) & (p == 0))
            def _():
                pass_on(3)

            @pl.when(z == 3)
            def _():
                chain(l, p).wait_recv()

            for t in (0, 1):
                n = 256 * (t + 1)
                tr = slice(256 * t, 256 * t + 256)
                res = []
                for h in (0, 1):
                    fl = slice(256 * h, 256 * h + 256)
                    fqh = fq[l, p, tr, fl]
                    a = (dot_nt(fqh, fk[l, p, 0:n, fl]) * mask[tr, 0:n]).astype(BF16)
                    zrow = sin[l, p, 128:144, :].astype(F32)[8 * h : 8 * h + 1, :]
                    st = jnp.concatenate(
                        [sin[l, p, 0:128, :], jnp.broadcast_to(zrow, (128, 256)).astype(BF16)], axis=0
                    )
                    res.append(dot(a, vext[l, p, 0:n, :]) + head_mask[tr, :] * dot_nt(fqh, st))
                num = jnp.where(low256, res[0][:, 0:128], res[1][:, 0:128])
                den = jnp.where(low256, res[0][:, 128:256], res[1][:, 128:256])
                r = 1.0 / den
                att[l, tr, at] = num * r
                rden[l, tr, at] = r
            return 0

        lax.fori_loop(0, 4, attend_pair, 0)
        save(l, att, rden, sin)

        if "branch" in during:
            during["branch"]()

        def branch_tile(i, _):
            at = pl.ds(pl.multiple_of(i * 256, 256), 256)
            b = xbuf[at, :] + dot(att[l, at, :].astype(BF16), weight(G, l, ROW_O))
            branch[l, at, :] = b
            hf[at, :] = (norm(b)[0] * gains[2 * l + 1 : 2 * l + 2, :]).astype(BF16)
            acc[at, :] = b
            return 0

        save(l, G)
        lax.fori_loop(0, 2, branch_tile, 0)
        save(l, branch)

        def ffn_tile(j, _):
            if "ffn" in during:
                during["ffn"](j)
            up = G[l, :, pl.ds(pl.multiple_of(ROW_UP + 32 * j, 32), 32), :].reshape(512, 512)
            down = G[l, pl.ds(4 * j, 4), ROW_DOWN:SLAB, :].reshape(512, 512)
            for i in (0, 1):
                at = slice(256 * i, 256 * i + 256)
                pre = dot(hf[at, :], up)
                hid = jax.nn.gelu(pre).astype(BF16)
                acc[at, :] += dot(hid, down)
            return 0

        lax.fori_loop(0, 4, ffn_tile, 0)
        y = acc[...].astype(BF16)
        ybuf[l] = y
        xbuf[...] = y.astype(F32)
        give(l)

    def before_branch(l):
        if l == 0:
            four(moves[0, 1].far)
        moves[l, 1].finish()

    layer(0, {"key": moves[1, 0].column, "query": moves[1, 1].column, "attend": moves[1, 0].across,
              "branch": lambda: before_branch(0), "ffn": moves[1, 1].across})
    four(moves[1, 0].far)
    moves[1, 0].finish()
    layer(1, {"query": moves[1, 1].far, "branch": lambda: before_branch(1)})
    give_own(0).wait()
    give_far(0).wait()
    keep.wait()
    for l in (0, 1):
        for i, (src, dst) in enumerate(saved):
            pltpu.make_async_copy(src.at[l], dst.at[l], wsem.at[l, i]).wait()

    @pl.when(z < 3)
    def _():
        for l in (0, 1):
            for p in range(4):
                chain(l, p).wait_send()

    for move in moves.values():
        move.drain()


def forward_call(inputs, lengths, weights, proj):
    sds = jax.ShapeDtypeStruct
    dma = pltpu.SemaphoreType.DMA
    vm = pl.BlockSpec(memory_space=pltpu.VMEM)
    hbm = pl.BlockSpec(memory_space=pl.ANY)
    saved = [
        sds((2, 16, SLAB, 512), BF16), sds((2, 4, 512, 512), BF16), sds((2, 4, 512, 512), BF16),
        sds((2, 4, 512, 256), BF16), sds((2, 512, 512), F32), sds((2, 512, 512), F32), sds((2, 512, 512), F32),
        sds((2, 2, 4, 512, 128), BF16), sds((2, 512, 512), BF16), sds((2, 4, 144, 256), BF16),
        sds((2, 4, 256, 512), BF16), sds((16, 512), F32),
    ]
    scratch = [
        pltpu.VMEM((2, 16, SLAB, 512), BF16),
        pltpu.VMEM((2, 2, 8, 64, 256), BF16),
        pltpu.VMEM((2, 4, 512, 512), BF16),
        pltpu.VMEM((512, 512), F32),
        pltpu.VMEM((512, 512), F32),
        pltpu.VMEM((512, 512), BF16),
        pltpu.VMEM((512, 512), F32),
        pltpu.VMEM((512, 512), F32),
        pltpu.VMEM((2, 4, 512, 512), BF16),
        pltpu.VMEM((2, 4, 512, 512), BF16),
        pltpu.VMEM((2, 4, 512, 256), BF16),
        pltpu.VMEM((2, 512, 512), F32),
        pltpu.VMEM((2, 512, 512), F32),
        pltpu.VMEM((2, 512, 512), F32),
        pltpu.VMEM((2, 2, 4, 512, 128), BF16),
        pltpu.VMEM((2, 512, 512), BF16),
        pltpu.VMEM((2, 4, 144, 256), BF16),
        pltpu.VMEM((4, 144, 256), F32),
        pltpu.VMEM((2, 4, 144, 256), BF16),
        pltpu.VMEM((16, 512), F32),
        pltpu.VMEM((2, 512, 512), BF16),
        pltpu.VMEM((512, 512), BF16),
        pltpu.VMEM((512, 512), F32),
        pltpu.VMEM((16, 128), F32),
        pltpu.VMEM((2, 16, 128), BF16),
        pltpu.VMEM((16, 16, 128), BF16),
        dma((2, 2, 16)), dma((2, 2, 16)), dma((2, 2, 16)), dma((2, 2, 16)), dma, dma((2, 2, 2)), dma((4,)),
        dma((2, 4)), dma((2, 4)), dma((3,)), dma((2, 10)), dma((16,)), dma((16,)),
    ]
    return pl.pallas_call(
        forward_kernel,
        out_shape=[sds((2, 512, 512), BF16)] + saved,
        in_specs=[vm, pl.BlockSpec(memory_space=pltpu.SMEM)] + [vm] * 9,
        out_specs=[vm] + [hbm] * (len(saved) - 1) + [vm],
        scratch_shapes=scratch,
        compiler_params=pltpu.CompilerParams(
            collective_id=0, has_side_effects=True, vmem_limit_bytes=VMEM_LIMIT
        ),
        name="forward",
    )(inputs, lengths, *weights, proj)


def gelu_parts(x):
    k = 0.7978845608028654
    x2 = x * x
    t = jnp.tanh(k * x * (1.0 + 0.044715 * x2))
    half = 0.5 * (1.0 + t)
    return x * half, half + 0.5 * x * (1.0 - t * t) * k * (1.0 + 0.134145 * x2)


def norm_back(y, rstd, dy):
    m1 = jnp.mean(dy, axis=-1, keepdims=True)
    m2 = jnp.mean(dy * y, axis=-1, keepdims=True)
    return rstd * (dy - m1 - y * m2)


HALF = (SLAB - ROW_Q) // 2
SUM_PORTIONS = ((ROW_O, 144), (ROW_Q, 48))


class Sums:
    def __init__(self, pc, slabs, bufs, sems, l, por):
        base, self.n = SUM_PORTIONS[por]
        self.pc, self.slabs, self.l, self.por = pc, slabs, l, por
        self.sb, self.r1, self.r2, self.r3, self.keep = bufs
        self.sems = sems
        self.mine = pl.multiple_of(base + pc.c * self.n, 16)
        self.other = pl.multiple_of(base + pc.o * self.n, 16)
        self.at = pl.ds(sum(2 * n for _, n in SUM_PORTIONS[:por]) // 2, self.n)

    def copy(self, i, j, src, dst, dev):
        ssem, rsem = self.sems
        return remote(src, dst, ssem.at[self.l, self.por, i, j], rsem.at[self.l, self.por, i, j], dev)

    def to_sibling(self, g):
        src = self.slabs.at[self.l, g, pl.ds(self.other, self.n)]
        return self.copy(0, g, src, self.sb.at[self.l, g, self.at], self.pc.sibling())

    def to_second(self, j, zz, g):
        src, dst = self.sb.at[self.l, g, self.at], self.r1.at[self.l, j, zz, self.at]
        return self.copy(1, 4 * j + zz, src, dst, self.pc.at(self.pc.second, self.pc.z))

    def to_first(self, zz, g):
        src, dst = self.sb.at[self.l, g, self.at], self.r2.at[self.l, zz, self.at]
        return self.copy(2, zz, src, dst, self.pc.at(self.pc.first, self.pc.z))

    def along(self, k, g):
        src, dst = self.sb.at[self.l, g, self.at], self.r3.at[self.l, 3 - k, self.at]
        return self.copy(3, 3 - k, src, dst, self.pc.at(self.pc.d, lax.rem(self.pc.z + k, 4)))

    def begin(self):
        pc = self.pc
        for k in (1, 2, 3, 0):
            for col in (pc.diag, pc.second, pc.first, pc.d):
                self.to_sibling(col * 4 + lax.rem(pc.z + k, 4)).start()

    def pair(self, g):
        self.to_sibling(g).wait_recv()
        own = self.slabs[self.l, g, pl.ds(self.mine, self.n), :]
        return own.astype(F32) + self.sb[self.l, g, self.at, :].astype(F32)

    def stage1(self, j, i):
        pc = self.pc
        zz = lax.rem(pc.z + 1 + i, 4)
        g = (pc.diag if j == 0 else pc.second) * 4 + zz
        self.sb[self.l, g, self.at, :] = self.pair(g).astype(BF16)
        self.to_second(j, zz, g).start()

    def stage2(self, i):
        pc = self.pc
        zz = lax.rem(pc.z + 1 + i, 4)
        g = pc.first * 4 + zz
        s = self.pair(g)
        self.to_second(0, zz, g).wait_recv()
        self.sb[self.l, g, self.at, :] = (s + self.r1[self.l, 0, zz, self.at, :].astype(F32)).astype(BF16)
        self.to_first(zz, g).start()

    def stage3(self, k):
        pc = self.pc
        zz = lax.rem(pc.z + k, 4)
        g = pc.d * 4 + zz
        s = self.pair(g)
        self.to_second(1, zz, g).wait_recv()
        s = s + self.r1[self.l, 1, zz, self.at, :].astype(F32)
        self.to_first(zz, g).wait_recv()
        s = s + self.r2[self.l, zz, self.at, :].astype(F32)
        if k:
            self.sb[self.l, g, self.at, :] = s.astype(BF16)
            self.along(k, g).start()
        else:
            self.keep[self.l, self.at, :] = s

    def stage4(self, l):
        s = self.keep[l, self.at, :]
        for i in range(3):
            s = s + self.r3[l, i, self.at, :].astype(F32)
        return s

    def arrive(self):
        for k in (1, 2, 3):
            self.along(k, self.pc.me).wait_recv()

    def drain(self):
        for i in range(16):
            self.to_sibling(i).wait_send()
        for j in (0, 1):
            for zz in range(4):
                self.to_second(j, zz, 0).wait_send()
        for zz in range(4):
            self.to_first(zz, 0).wait_send()
        for k in (1, 2, 3):
            self.along(k, 0).wait_send()


def backward_kernel(
    cotangent, lengths, wq_in, wk_in, wv_in, wup_in, G_in, fq_in, fk_in, v_in, att_in, rden_in, branch_in, w_in, x_in, sin_in, pb_in, gains_in,
    gin, gq_out, gk_out, gv_out, go_out, gup_out, gdown_out, gg_out,
    G, fq, fk, vext, att, rden, branch, wqk, xin, sin, pb,
    mask, mask_t, gbuf, gbr, hbuf, hT, gb, dh, gq, gk, gv, le, rin, rtail, rbuf, gains, xout, slabs,
    sb, r1, r2, r3, keep, total,
    lsem, csend, crecv, asem, ssem, rsem, fsem,
):
    pc = Place()
    c, z = pc.c, pc.z
    attn, ffn = pl.ds(ROW_Q, ROW_UP - ROW_Q), pl.ds(ROW_UP, SLAB - ROW_UP)
    loads = {
        "branch": (lambda l: branch_in.at[l], branch),         "ffn": (lambda l: G_in.at[l, :, ffn], G.at[:, ffn]), "att": (lambda l: att_in.at[l], att),
        "attn": (lambda l: G_in.at[l, :, attn], G.at[:, attn]), "rden": (lambda l: rden_in.at[l], rden),
        "fq": (lambda l: fq_in.at[l], fq), "sin": (lambda l: sin_in.at[l], sin), "fk": (lambda l: fk_in.at[l], fk),
        "vext": (lambda l: v_in.at[l], vext), "pb": (lambda l: pb_in.at[l], pb), "wqk": (lambda l: w_in.at[l], wqk),
        "xin": (lambda l: x_in.at[l], xin),
    }

    def load(l, name):
        src, dst = loads[name]
        return pltpu.make_async_copy(src(l), dst, lsem.at[list(loads).index(name)])

    def needs(l, *names):
        for name in names:
            load(l, name).wait()

    def done(l, *names):
        if l == 1:
            for name in names:
                load(0, name).start()

    pc.greet()
    gains[...] = gains_in[...]
    for name in loads:
        load(1, name).start()

    first_row = z * 512
    rows = lax.broadcasted_iota(jnp.int32, (512, 512), 0)
    cols = lax.broadcasted_iota(jnp.int32, (512, 512), 1)
    begin, starts = last_start(lengths, c, first_row, rows)
    mask[...] = ((cols <= rows) & (cols >= begin)).astype(F32).astype(BF16)
    begin, _ = last_start(lengths, c, first_row, cols)
    mask_t[...] = ((rows <= cols) & (rows >= begin)).astype(F32).astype(BF16)
    prow = lax.broadcasted_iota(jnp.int32, (512, 1), 0)
    begin_col, _ = last_start(lengths, c, first_row, prow)
    head_col = (begin_col < 0).astype(F32)
    lane = lax.broadcasted_iota(jnp.int32, (1, 512), 1)
    begin_row, _ = last_start(lengths, c, first_row, lane)
    head_row = (begin_row < 0).astype(F32)
    inner = [jnp.where((s < 512) & (s >= 0), s, 0) for s in starts]
    cut = jnp.maximum(jnp.maximum(inner[0], inner[1]), inner[2])
    tail_col = (prow >= cut).astype(F32)

    @pl.when(z == 3)
    def _():
        rin[...] = jnp.zeros_like(rin)

    gbuf[...] = cotangent[c, 0].astype(F32)
    pc.meet()
    above = (c, pc.d, jnp.maximum(z - 1, 0))
    row_low = lax.broadcasted_iota(jnp.int32, (144, 256), 0)
    tail_is_first = (row_low < 64) | ((row_low >= 128) & (row_low < 136))
    low = lane_low((512, 128))
    ones_i = lax.broadcasted_iota(jnp.int32, (256, 128), 0)
    ones_j = lax.broadcasted_iota(jnp.int32, (256, 128), 1)
    head_ones = (lax.rem(ones_i, 128) // 64 == ones_j // 64).astype(BF16)
    scale = 64 ** (-0.25)

    def chain(l, p):
        return remote(rbuf.at[l, p], rin.at[l, p], csend.at[l, p], crecv.at[l, p], above)

    sums = {(l, por): Sums(pc, slabs, (sb, r1, r2, r3, keep), (ssem, rsem), l, por) for l in (0, 1) for por in (0, 1)}

    def put(l, row, n, value):
        slabs[l, :, row : row + n, :] = value.astype(BF16).reshape(16, n, 512)

    def layer(l, during):
        def at_point(name, *args):
            if name in during:
                during[name](*args)

        needs(l, "branch")

        def norm_tile(i, _):
            at = pl.ds(pl.multiple_of(i * 128, 128), 128)
            hbuf[at, :] = (norm(branch[at, :])[0] * gains[2 * l + 1 : 2 * l + 2, :]).astype(BF16)
            gb[at, :] = gbuf[at, :].astype(BF16)
            return 0

        lax.fori_loop(0, 4, norm_tile, 0)
        hT[...] = hbuf[...].T
        dh[...] = jnp.zeros_like(dh)

        def ffn_tile(j, _):
            at_point("ffn", j)
            up_at = pl.ds(pl.multiple_of(ROW_UP + 32 * j, 32), 32)
            up = G[:, up_at, :].reshape(512, 512)
            down = G[pl.ds(4 * j, 4), ROW_DOWN:SLAB, :].reshape(512, 512)
            for i in (0, 1):
                at = slice(256 * i, 256 * i + 256)
                hid, slope = gelu_parts(dot(hbuf[at, :], up))
                gq[at, :] = hid.astype(BF16)
                gk[at, :] = (slope * dot_nt(gb[at, :], down)).astype(BF16)
            slabs[l, pl.ds(4 * j, 4), ROW_DOWN:SLAB, :] = dot_tn(gq[...], gb[...]).astype(BF16).reshape(4, 128, 512)
            g = gk[...]
            slabs[l, :, up_at, :] = dot(hT[...], g).astype(BF16).reshape(16, 32, 512)
            dh[...] += dot_nt(g, up)
            return 0

        needs(l, "ffn")
        lax.fori_loop(0, 4, ffn_tile, 0)
        done(l, "ffn")
        needs(l, "att")

        def branch_tile(i, _):
            at_point("branch", i)
            at = pl.ds(pl.multiple_of(i * 128, 128), 128)
            y, rstd = norm(branch[at, :])
            d = dh[at, :]
            g = gbuf[at, :] + norm_back(y, rstd, d * gains[2 * l + 1 : 2 * l + 2, :])
            gbr[at, :] = g
            gb[at, :] = g.astype(BF16)
            hbuf[at, :] = att[at, :].astype(BF16)
            return 0

        lax.fori_loop(0, 4, branch_tile, 0)
        done(l, "branch")
        put(l, ROW_O, 32, dot_tn(hbuf[...], gb[...]))
        sums[l, 0].begin()
        at_point("middle")
        needs(l, "attn", "rden", "fq")
        dh[...] = dot_nt(gb[...], G[:, ROW_O : ROW_O + 32, :].reshape(512, 512))

        def pass_on(p):
            chain(l, p).wait_recv()
            rbuf[l, p] = (rtail[p] + rin[l, p].astype(F32)).astype(BF16)
            chain(l, p).start()

        def tail_pair(p, _):
            at_point("tail", p)
            at = pl.ds(pl.multiple_of(p * 128, 128), 128)
            g = dh[:, at]
            r = rden[:, at]
            t = g * att[:, at]
            hi = t.astype(BF16)
            lo = (t - hi.astype(F32)).astype(BF16)
            dden = -dot(jnp.concatenate([hi, lo], axis=1), head_ones) * r
            dnum = g * r
            le[p] = jnp.concatenate([dnum, dden * (1.0 / 64.0)], axis=1).astype(BF16)
            dt = (dden.T) * head_row
            lhs = jnp.concatenate([dnum.T * head_row, dt[0:8], dt[64:72]], axis=0).astype(BF16)
            tl = jnp.where(tail_is_first, dot(lhs, fq[p, :, 0:256]), dot(lhs, fq[p, :, 256:512]))
            rtail[p] = tl

            @pl.when(z == 3)
            def _():
                rbuf[l, p] = tl.astype(BF16)
                chain(l, p).start()

            return 0

        lax.fori_loop(0, 4, tail_pair, 0)
        done(l, "att", "rden")
        needs(l, "sin", "fk", "vext", "pb", "wqk")

        def of_head(h, value):
            keep = lane_low(value.shape) if h == 0 else jnp.logical_not(lane_low(value.shape))
            return jnp.where(keep, value, jnp.zeros((), BF16))

        def through_lift(p, k, e):
            gw = dot_nt(jnp.concatenate(e, axis=1), pb[p])
            gw = gw[:, 0:128] + 2.0 * wqk[k, p].astype(F32) * gw[:, 128:256]
            return (gw * scale).astype(BF16)

        def query_pair(p, _):
            at_point("query", p)
            at = pl.ds(pl.multiple_of(p * 128, 128), 128)

            @pl.when((z == 2) & (p >= 1))
            def _():
                pass_on(p - 1)

            ve = vext[p]
            lep = le[p]
            dq = []
            for h in (0, 1):
                fl = slice(256 * h, 256 * h + 256)
                leh = of_head(h, lep)
                fkh = fk[p, :, fl]
                zrow = sin[p, 128:144, :].astype(F32)[8 * h : 8 * h + 1, :]
                st = jnp.concatenate([sin[p, 0:128, :], jnp.broadcast_to(zrow, (128, 256)).astype(BF16)], axis=0)
                dqh = head_col * dot(leh, st)
                da0 = dot_nt(leh[0:256], ve[0:256]).astype(BF16) * mask[0:256, 0:256]
                da1 = dot_nt(leh[256:512], ve).astype(BF16) * mask[256:512, :]
                dqh = dqh + jnp.concatenate([dot(da0, fkh[0:256]), dot(da1, fkh)], axis=0)
                dq.append((dqh * fq[p, :, fl].astype(F32)).astype(BF16))
            gq[:, at] = through_lift(p, 0, dq)
            return 0

        lax.fori_loop(0, 4, query_pair, 0)

        def attend_pair(p, _):
            at_point("attend", p)
            at = pl.ds(pl.multiple_of(p * 128, 128), 128)

            @pl.when((z == 2) & (p == 0))
            def _():
                pass_on(3)

            ve = vext[p]
            lep = le[p]
            dk, dv = [], []
            for h in (0, 1):
                if h == 1:
                    @pl.when(z == 1)
                    def _():
                        pass_on(p)

                fl = slice(256 * h, 256 * h + 256)
                leh = of_head(h, lep)
                fqh, fkh = fq[p, :, fl], fk[p, :, fl]
                at0 = dot_nt(fkh[0:256], fqh).astype(BF16) * mask_t[0:256, :]
                at1 = dot_nt(fkh[256:512], fqh[256:512]).astype(BF16) * mask_t[256:512, 256:512]
                dv.append(jnp.concatenate([dot(at0, lep[:, 0:128]), dot(at1, lep[256:512, 0:128])], axis=0))
                dt0 = dot_nt(ve[0:256], leh).astype(BF16) * mask_t[0:256, :]
                dt1 = dot_nt(ve[256:512], leh[256:512]).astype(BF16) * mask_t[256:512, 256:512]
                dk.append(jnp.concatenate([dot(dt0, fqh), dot(dt1, fqh[256:512])], axis=0))

            @pl.when(z == 0)
            def _():
                chain(l, p).wait_recv()

            for h in (0, 1):
                fkh = fk[p, :, 256 * h : 256 * h + 256]
                rrow = rin[l, p, 128:144, :].astype(F32)[8 * h : 8 * h + 1, :] * (1.0 / 128.0)
                rows_h = lax.broadcasted_iota(jnp.int32, (128, 256), 0) // 64 == h
                rt = jnp.where(rows_h, rin[l, p, 0:128, :], jnp.zeros((), BF16))
                rte = jnp.concatenate([rt, jnp.broadcast_to(rrow, (128, 256)).astype(BF16)], axis=0)
                dv[h] = dv[h] + tail_col * dot_nt(fkh, rin[l, p, 0:128, :])
                dk[h] = ((dk[h] + tail_col * dot(ve, rte)) * fkh.astype(F32)).astype(BF16)
            gv[:, at] = jnp.where(low, dv[0], dv[1]).astype(BF16)
            gk[:, at] = through_lift(p, 1, dk)
            return 0

        lax.fori_loop(0, 4, attend_pair, 0)
        done(l, "fq", "sin", "fk", "vext", "pb", "wqk")
        needs(l, "xin")

        def norm_tile2(i, _):
            at_point("norm", i)
            at = pl.ds(pl.multiple_of(i * 128, 128), 128)
            hbuf[at, :] = (norm(xin[at, :].astype(F32))[0] * gains[2 * l : 2 * l + 1, :]).astype(BF16)
            return 0

        lax.fori_loop(0, 4, norm_tile2, 0)
        hT[...] = hbuf[...].T
        for row, g in ((ROW_Q, gq), (ROW_K, gk), (ROW_V, gv)):
            put(l, row, 32, dot(hT[...], g[...]))
        sums[l, 1].begin()
        dh[...] = dot_nt(gq[...], G[:, ROW_Q : ROW_Q + 32, :].reshape(512, 512))
        dh[...] += dot_nt(gk[...], G[:, ROW_K : ROW_K + 32, :].reshape(512, 512))
        dh[...] += dot_nt(gv[...], G[:, ROW_V : ROW_V + 32, :].reshape(512, 512))

        done(l, "attn")
        at_point("late")

        def out_tile(i, _):
            at_point("out", i)
            at = pl.ds(pl.multiple_of(i * 128, 128), 128)
            y, rstd = norm(xin[at, :].astype(F32))
            d = dh[at, :]
            g = (gbr[at, :] + norm_back(y, rstd, d * gains[2 * l : 2 * l + 1, :])).astype(BF16)
            xout[l, at, :] = g
            gbuf[at, :] = g.astype(F32)
            return 0

        lax.fori_loop(0, 4, out_tile, 0)
        done(l, "xin")

    def four(step, *args):
        for i in range(4):
            step(*args, i)

    def along_z(m):
        for k in (1, 2, 3, 0):
            m.stage3(k)

    def both(m):
        return lambda i: (m.stage1(0, i), m.stage1(1, i))

    def at_steps(**steps):
        def run(i):
            for name, step in steps.items():
                pl.when(i == int(name[1:]))(step)

        return run

    def larger(l, extra=lambda: None):
        m = sums[l, 0]
        return {
            "tail": both(m),
            "attend": at_steps(i1=lambda: m.stage2(0), i3=lambda: (m.stage2(1), extra())[0]),
            "norm": at_steps(i0=lambda: m.stage3(1), i3=lambda: m.stage2(2)),
            "late": lambda: m.stage3(2),
            "out": at_steps(i1=lambda: m.stage2(3)),
        }

    m1, m0 = sums[1, 0], sums[0, 0]
    layer(1, {"tail": both(m1), "attend": at_steps(i1=lambda: m1.stage2(0), i3=lambda: m1.stage2(1)),
              "norm": at_steps(i3=lambda: m1.stage2(2)), "out": at_steps(i1=lambda: m1.stage2(3), i3=lambda: m1.stage3(1))})
    early = at_steps(i0=lambda: m1.stage3(2), i1=lambda: m1.stage3(3), i2=lambda: m1.stage3(0))
    hooks = larger(0, lambda: four(sums[1, 1].stage2))
    late_steps = hooks["out"]
    hooks["out"] = lambda i: (both(sums[0, 1])(i), late_steps(i))
    layer(0, {"ffn": lambda i: (early(i), both(sums[1, 1])(i)), **hooks})
    own_act = pltpu.make_async_copy(xout.at[c], gin.at[c], asem.at[0])
    own_act.start()
    far_act = remote(xout.at[pc.o], gin.at[c], asem.at[1], asem.at[2], pc.sibling())
    far_act.start()
    own_act.wait()
    far_act.wait()

    along_z(sums[1, 1])
    sums[0, 0].stage3(3)
    sums[0, 0].stage3(0)
    four(sums[0, 1].stage2)
    along_z(sums[0, 1])
    for m in sums.values():
        m.arrive()
    for por in (0, 1):
        m = sums[0, por]
        gbr[m.at, :] = m.stage4(pc.o)
    parts = []
    for por in (0, 1):
        m = sums[0, por]
        part = remote(gbr.at[m.at], total.at[pl.ds(m.mine, m.n)], fsem.at[0, por], fsem.at[1, por], pc.sibling())
        part.start()
        parts.append(part)
    for por in (0, 1):
        m = sums[0, por]
        total[pl.ds(m.mine, m.n), :] = m.stage4(c)
    for part in parts:
        part.wait()
    for ref, row in ((gq_out, ROW_Q), (gk_out, ROW_K), (gv_out, ROW_V), (go_out, ROW_O)):
        ref[...] = total[row : row + 32, :]
    for j in range(4):
        gup_out[:, 512 * j : 512 * j + 512] = total[ROW_UP + 32 * j : ROW_UP + 32 * j + 32, :]
    gdown_out[...] = total[ROW_DOWN:SLAB, :]
    ga = jnp.zeros((32, 512), F32)
    for ref, row in ((wq_in, ROW_Q), (wk_in, ROW_K), (wv_in, ROW_V)):
        ga = ga + ref[0].astype(BF16).astype(F32) * total[row : row + 32, :]
    gf = jnp.zeros((32, 512), F32)
    for j in range(4):
        up = wup_in[0, :, 512 * j : 512 * j + 512].astype(BF16).astype(F32)
        gf = gf + up * total[ROW_UP + 32 * j : ROW_UP + 32 * j + 32, :]
    gg_out[0] = jnp.broadcast_to(jnp.sum(ga, axis=1, keepdims=True), (32, 128))
    gg_out[1] = jnp.broadcast_to(jnp.sum(gf, axis=1, keepdims=True), (32, 128))
    for m in sums.values():
        m.drain()

    @pl.when(z > 0)
    def _():
        for l in (0, 1):
            for p in range(4):
                chain(l, p).wait_send()


def backward_call(cotangent, lengths, weights, saved):
    sds = jax.ShapeDtypeStruct
    dma = pltpu.SemaphoreType.DMA
    vm = pl.BlockSpec(memory_space=pltpu.VMEM)
    hbm = pl.BlockSpec(memory_space=pl.ANY)
    bufs = [pltpu.VMEM(a.shape[1:], a.dtype) for a in saved[:-1]]
    full = (512, 512)
    scratch = bufs + [
        pltpu.VMEM(full, BF16),
        pltpu.VMEM(full, BF16),
        pltpu.VMEM(full, F32),
        pltpu.VMEM(full, F32),
        pltpu.VMEM(full, BF16),
        pltpu.VMEM(full, BF16),
        pltpu.VMEM(full, BF16),
        pltpu.VMEM(full, F32),
        pltpu.VMEM(full, BF16),
        pltpu.VMEM(full, BF16),
        pltpu.VMEM(full, BF16),
        pltpu.VMEM((4, 512, 256), BF16),
        pltpu.VMEM((2, 4, 144, 256), BF16),
        pltpu.VMEM((4, 144, 256), F32),
        pltpu.VMEM((2, 4, 144, 256), BF16),
        pltpu.VMEM((16, 512), F32),
        pltpu.VMEM((2, 512, 512), BF16),
        pltpu.VMEM((2, 16, SLAB, 512), BF16),
        pltpu.VMEM((2, 16, HALF, 512), BF16),
        pltpu.VMEM((2, 2, 4, HALF, 512), BF16),
        pltpu.VMEM((2, 4, HALF, 512), BF16),
        pltpu.VMEM((2, 3, HALF, 512), BF16),
        pltpu.VMEM((2, HALF, 512), F32),
        pltpu.VMEM((SLAB, 512), F32),
        dma((13,)), dma((2, 4)), dma((2, 4)), dma((3,)), dma((2, 2, 4, 16)), dma((2, 2, 4, 16)), dma((2, 2)),
    ]
    return pl.pallas_call(
        backward_kernel,
        out_shape=[sds((2, 512, 512), BF16)]
        + [sds((32, 512), F32)] * 4
        + [sds((32, 2048), F32), sds((128, 512), F32), sds((2, 32, 128), F32)],
        in_specs=[vm, pl.BlockSpec(memory_space=pltpu.SMEM)] + [vm] * 4 + [hbm] * (len(saved) - 1) + [vm],
        out_specs=[vm] * 8,
        scratch_shapes=scratch,
        compiler_params=pltpu.CompilerParams(
            collective_id=1, has_side_effects=True, vmem_limit_bytes=VMEM_LIMIT
        ),
        name="backward",
    )(cotangent, lengths, *weights, *saved)


def finish_kernel(*refs):
    n = len(refs) // 2
    ins, outs, sems = refs[:n], refs[n : 2 * n - 1], refs[2 * n - 1 :]
    sums, ga, gf = ins[n - 3 :]
    copies = [pltpu.make_async_copy(src, dst, sems[0].at[i]) for i, (src, dst) in enumerate(zip(ins[: n - 3], outs))]
    for copy in copies:
        copy.start()
    for i, gain in ((0, ga), (1, gf)):
        outs[n - 3 + i][...] = sums[i].T[0:1, 0:32] / gain[...].astype(BF16).astype(F32)
    for copy in copies:
        copy.wait()


def finish_call(results, sums, gain_attn, gain_ffn):
    vm = pl.BlockSpec(memory_space=pltpu.VMEM)
    hbm = pl.BlockSpec(memory_space=pl.ANY)
    n = len(results)
    return pl.pallas_call(
        finish_kernel,
        out_shape=[jax.ShapeDtypeStruct(r.shape, r.dtype) for r in results + [gain_attn, gain_ffn]],
        in_specs=[hbm] * n + [vm] * 3,
        out_specs=[vm] * (n + 2),
        scratch_shapes=[pltpu.SemaphoreType.DMA((n,))],
        name="finish",
    )(*results, sums, gain_attn, gain_ffn)


def fast_local(inputs, cotangent, doc_lengths, feature_proj, *weights):
    act, *saved = forward_call(inputs, doc_lengths, weights, feature_proj)
    w_query, w_key, w_value, _, w_up = weights[:5]
    gin, *grads = backward_call(cotangent, doc_lengths, (w_query, w_key, w_value, w_up), saved)
    done = finish_call([act, gin] + grads[:6], grads[6], weights[6], weights[7])
    return (done[0][None, :, None], done[1][None, :, None]) + tuple(g[None] for g in done[2:8]) + tuple(done[8:])


HIGH_PRECISION = lax.Precision.HIGHEST


def prefix(shard, axis, join, neutral):
    place = lax.axis_index(axis)
    gathered = jax.tree.map(
        lambda a, kind: lax.all_gather(a.astype(kind), axis),
        shard,
        (jnp.bfloat16, jnp.bfloat16, jnp.bfloat16),
    )
    state = jax.tree.map(lambda a, e: jnp.zeros_like(a) + jnp.asarray(e, a.dtype), shard, neutral)

    def prefix_one(lap, state):
        return join(
            state,
            jax.tree.map(
                lambda a, own: lax.dynamic_index_in_dim(a, lap, 0, False).astype(own.dtype),
                gathered,
                shard,
            ),
        )

    return lax.fori_loop(0, place, prefix_one, state)


def entering(shard, axis, join, neutral):
    count = lax.axis_size(axis)
    place = lax.axis_index(axis)
    ahead = count - 1 - place
    gathered = jax.tree.map(
        lambda a, kind: lax.all_gather(a.astype(kind), axis),
        shard,
        jax.tree.map(lambda a: jnp.bfloat16 if a.dtype == jnp.float32 else a.dtype, shard),
    )
    state = jax.tree.map(lambda a, e: jnp.zeros_like(a) + jnp.asarray(e, a.dtype), shard, neutral)

    def entering_one(lap, state):
        source = count - 1 - lap
        return join(
            state,
            jax.tree.map(
                lambda a, own: lax.dynamic_index_in_dim(a, source, 0, False).astype(own.dtype),
                gathered,
                shard,
            ),
        )

    return lax.fori_loop(0, ahead, entering_one, state)


def as_sent(shard):

    def short(part):
        return part.astype(jnp.bfloat16) if part.dtype == jnp.float32 else part

    return jax.tree.map(short, shard)


def passed_along(block, axis, distance):
    devices = range(lax.axis_size(axis))
    route = [(i - distance, i) for i in devices if i - distance in devices]
    return lax.ppermute(block, axis, route)


def matmul(left, right):
    return jnp.dot(left, right, preferred_element_type=jnp.float32)


def norm_rows(values):
    centre = values - jnp.mean(values, axis=-1, keepdims=True)
    return centre * lax.rsqrt(jnp.mean(centre * centre, axis=-1, keepdims=True) + 1e-05)


def lift(values, projection):
    heads, depth, feats = projection.shape
    scaled = values.reshape(values.shape[0], heads, depth) * depth ** (-0.25)
    raised = jnp.einsum("nhd,hdm->nhm", scaled, projection, precision=HIGH_PRECISION)
    return jnp.exp(raised - 0.5 * jnp.sum(scaled * scaled, axis=-1, keepdims=True)) * feats ** (
        -0.5
    )


def doc_masks(lengths, first_row, row_count):
    doc_ends = jnp.cumsum(lengths, dtype=jnp.int32)
    starts = doc_ends - lengths
    positions = first_row + jnp.arange(row_count, dtype=jnp.int32)
    begun_at = starts[None, :] <= positions[:, None]
    doc_ids = jnp.sum(begun_at.astype(jnp.int32), axis=1)
    order_idx = jnp.arange(row_count, dtype=jnp.int32)
    same_doc = (
        (doc_ids[:, None] == doc_ids[None, :]) & (order_idx[None, :] <= order_idx[:, None])
    ).astype(jnp.float32)
    inside = (starts >= first_row) & (starts < first_row + row_count)
    mask_per_head = (jnp.sum((begun_at & inside[None, :]).astype(jnp.int32), axis=1) == 0).astype(
        jnp.float32
    )
    tail_mask = (jnp.sum((~begun_at & inside[None, :]).astype(jnp.int32), axis=1) == 0).astype(
        jnp.float32
    )
    kept_flag = (jnp.sum(inside.astype(jnp.int32)) == 0).astype(jnp.float32)
    return (same_doc, mask_per_head, tail_mask, kept_flag)


def attend(query_features, feats_k, value_heads, incoming_state, norm_in, same_doc, mask_per_head):
    scores = (
        jnp.einsum("thm,shm->hts", query_features, feats_k, precision=HIGH_PRECISION)
        * same_doc[None]
    )
    attention_numerator = jnp.einsum("hts,shd->thd", scores, value_heads, precision=HIGH_PRECISION)
    attention_numerator = attention_numerator + mask_per_head[:, None, None] * jnp.einsum(
        "kec,ecz->kez", query_features, incoming_state, precision=HIGH_PRECISION
    )
    denominator = jnp.sum(scores, axis=2).T + mask_per_head[:, None] * jnp.einsum(
        "thm,hm->th", query_features, norm_in, precision=HIGH_PRECISION
    )
    return (attention_numerator / denominator[:, :, None]).reshape(query_features.shape[0], -1)


def tail_sums(feats_k, value_heads, tail_mask):
    weighted_values = feats_k * tail_mask[:, None, None]
    return (
        jnp.einsum("zlu,zlv->luv", weighted_values, value_heads, precision=HIGH_PRECISION),
        jnp.sum(weighted_values, axis=0),
    )


def combine_carry(earlier, later_part):
    return (
        earlier[0] * later_part[0],
        later_part[1] + later_part[0] * earlier[1],
        later_part[2] + later_part[0] * earlier[2],
    )


def run_forward(layer_in, weights, projection, lengths, first_row):
    w_query, w_key, w_value, w_out, w_up, w_down, gain_attn, gain_ffn = weights
    row_count = layer_in.shape[0]
    same_doc, mask_per_head, tail_mask, kept_flag = doc_masks(lengths, first_row, row_count)
    h_attn = (norm_rows(layer_in) * gain_attn.astype(jnp.float32)).astype(jnp.bfloat16)
    query_features = lift(matmul(h_attn, w_query), projection)
    feats_k = lift(matmul(h_attn, w_key), projection)
    value_heads = matmul(h_attn, w_value).reshape(row_count, projection.shape[0], -1)
    state_tail, norm_tail = tail_sums(feats_k, value_heads, tail_mask)
    identity = (jnp.ones((), jnp.float32), jnp.zeros_like(state_tail), jnp.zeros_like(norm_tail))
    _, incoming_state, norm_in = prefix(
        (kept_flag, state_tail, norm_tail), "seq", combine_carry, identity
    )
    mixed_heads = attend(
        query_features, feats_k, value_heads, incoming_state, norm_in, same_doc, mask_per_head
    ).astype(jnp.bfloat16)
    branch = layer_in + matmul(mixed_heads, w_out)
    h_ffn = (norm_rows(branch) * gain_ffn.astype(jnp.float32)).astype(jnp.bfloat16)
    hidden = jax.nn.gelu(matmul(h_ffn, w_up)).astype(jnp.bfloat16)
    return (branch + matmul(hidden, w_down), incoming_state, norm_in)


def run_backward(
    layer_in, incoming_state, norm_in, grad_out, weights, projection, lengths, first_row
):
    w_query, w_key, w_value, w_out, w_up, w_down, gain_attn, gain_ffn = weights
    row_count = layer_in.shape[0]
    same_doc, mask_per_head, tail_mask, kept_flag = doc_masks(lengths, first_row, row_count)
    gain_a = gain_attn.astype(jnp.float32)
    gain_f = gain_ffn.astype(jnp.float32)
    normed_a, norm_a_back = jax.vjp(norm_rows, layer_in)
    h_attn = (normed_a * gain_a).astype(jnp.bfloat16)
    query_features, lift_q_back = jax.vjp(lambda z: lift(z, projection), matmul(h_attn, w_query))
    feats_k, lift_k_back = jax.vjp(lambda z: lift(z, projection), matmul(h_attn, w_key))
    value_heads = matmul(h_attn, w_value).reshape(row_count, projection.shape[0], -1)
    attended, attend_back = jax.vjp(
        lambda a, b, c, d, e: attend(a, b, c, d, e, same_doc, mask_per_head),
        query_features,
        feats_k,
        value_heads,
        incoming_state,
        norm_in,
    )
    mixed_heads = attended.astype(jnp.bfloat16)
    branch = layer_in + matmul(mixed_heads, w_out)
    normed_f, norm_f_back = jax.vjp(norm_rows, branch)
    h_ffn = (normed_f * gain_f).astype(jnp.bfloat16)
    activated, gelu_back = jax.vjp(jax.nn.gelu, matmul(h_ffn, w_up))
    hidden = activated.astype(jnp.bfloat16)
    grad_low = grad_out.astype(jnp.bfloat16)
    grad_wdown = matmul(hidden.T, grad_low)
    grad_pre = gelu_back(matmul(grad_low, w_down.T))[0].astype(jnp.bfloat16)
    grad_wup = matmul(h_ffn.T, grad_pre)
    grad_hffn = matmul(grad_pre, w_up.T)
    grad_gain_f = jnp.sum(grad_hffn * normed_f, axis=0)
    ffn_terms = (grad_wup, grad_wdown, grad_gain_f)
    grad_branch = grad_out + norm_f_back(grad_hffn * gain_f)[0]
    grad_blow = grad_branch.astype(jnp.bfloat16)
    grad_wout = matmul(mixed_heads.T, grad_blow)
    grad_fq, grad_fk, grad_vals, grad_state, grad_norm = attend_back(matmul(grad_blow, w_out.T))
    identity = (jnp.ones((), jnp.float32), jnp.zeros_like(grad_state), jnp.zeros_like(grad_norm))
    _, carry_state, carry_norm = entering(
        (kept_flag, grad_state, grad_norm), "seq", combine_carry, identity
    )
    _, tail_back = jax.vjp(lambda a, b: tail_sums(a, b, tail_mask), feats_k, value_heads)
    more_k, more_v = tail_back((carry_state, carry_norm))
    grad_q = lift_q_back(grad_fq)[0].astype(jnp.bfloat16)
    grad_k = lift_k_back(grad_fk + more_k)[0].astype(jnp.bfloat16)
    grad_v = (grad_vals + more_v).reshape(row_count, -1).astype(jnp.bfloat16)
    grad_hattn = matmul(grad_q, w_query.T) + matmul(grad_k, w_key.T) + matmul(grad_v, w_value.T)
    grad_gain_a = jnp.sum(grad_hattn * normed_a, axis=0)
    grad_in = grad_branch + norm_a_back(grad_hattn * gain_a)[0]
    attn_grads = (
        matmul(h_attn.T, grad_q),
        matmul(h_attn.T, grad_k),
        matmul(h_attn.T, grad_v),
        grad_wout,
        grad_gain_a,
    )
    return (grad_in, attn_grads, ffn_terms)


def local(
    inputs,
    cotangent,
    doc_lengths,
    feature_proj,
    w_query,
    w_key,
    w_value,
    w_out,
    w_up,
    w_down,
    gain_attn,
    gain_ffn,
):
    section_idx = lax.axis_index("section")
    seq_idx = lax.axis_index("seq")
    micro_count, _, row_count, feat_width = inputs.shape
    first_row = seq_idx * row_count
    projection = feature_proj[0]
    lengths_all = doc_lengths[:, 0, :]
    masters = (
        w_query[0],
        w_key[0],
        w_value[0],
        w_out[0],
        w_up[0],
        w_down[0],
        gain_attn[0],
        gain_ffn[0],
    )
    lowered = tuple((master.astype(jnp.bfloat16) for master in masters))
    gathered = jax.tree.map(
        lambda part, own: part.astype(own.dtype),
        lax.all_gather(as_sent(lowered), ("dp", "seq"), axis=0, tiled=True),
        lowered,
    )
    batch_range = jnp.arange(micro_count, dtype=jnp.int32)
    received = jnp.zeros((row_count, feat_width), jnp.bfloat16)
    outputs = jnp.zeros((micro_count, row_count, feat_width), jnp.float32)
    kept_inputs, kept_states, kept_norms = ([], [], [])
    for step_no in range(micro_count + 1):
        batch_no = step_no - section_idx
        is_valid = ((batch_no >= 0) & (batch_no < micro_count)).astype(jnp.float32)
        batch_idx = jnp.clip(batch_no, 0, micro_count - 1)
        own_input = inputs[min(step_no, micro_count - 1), 0].astype(jnp.float32)
        layer_in = jnp.where(section_idx == 0, own_input, received.astype(jnp.float32))
        lengths = lax.dynamic_index_in_dim(lengths_all, batch_idx, 0, keepdims=False)
        layer_out, incoming_state, norm_in = run_forward(
            layer_in, gathered, projection, lengths, first_row
        )
        sent_out = layer_out.astype(jnp.bfloat16)
        chosen = (batch_range == batch_idx).astype(jnp.float32) * is_valid
        outputs = outputs + chosen[:, None, None] * sent_out.astype(jnp.float32)[None]
        kept_inputs.append(layer_in)
        kept_states.append(incoming_state)
        kept_norms.append(norm_in)
        if step_no < micro_count:
            received = passed_along(sent_out, "section", 1)
    weights_back = jax.tree.map(
        lambda part, own: part.astype(own.dtype),
        lax.all_gather(as_sent(lowered), ("dp", "seq"), axis=0, tiled=True),
        lowered,
    )
    stacked_inputs = jnp.stack(kept_inputs)
    stacked_states = jnp.stack(kept_states)
    stacked_norms = jnp.stack(kept_norms)
    grad_recv = jnp.zeros((row_count, feat_width), jnp.bfloat16)
    grad_inputs = jnp.zeros((micro_count, row_count, feat_width), jnp.float32)
    totals = tuple((jnp.zeros(part.shape, jnp.float32) for part in weights_back))
    for step_no in range(micro_count + 1):
        batch_no = step_no - 1 + section_idx
        is_valid = ((batch_no >= 0) & (batch_no < micro_count)).astype(jnp.float32)
        batch_idx = jnp.clip(batch_no, 0, micro_count - 1)
        slot_idx = jnp.clip(step_no - 1 + 2 * section_idx, 0, micro_count)
        layer_in = lax.dynamic_index_in_dim(stacked_inputs, slot_idx, 0, keepdims=False)
        incoming_state = lax.dynamic_index_in_dim(stacked_states, slot_idx, 0, keepdims=False)
        norm_in = lax.dynamic_index_in_dim(stacked_norms, slot_idx, 0, keepdims=False)
        own_grad = cotangent[min(step_no, micro_count - 1), 0].astype(jnp.float32)
        grad_out = jnp.where(section_idx == 1, own_grad, grad_recv.astype(jnp.float32))
        lengths = lax.dynamic_index_in_dim(lengths_all, batch_idx, 0, keepdims=False)
        grad_in, attn_grads, ffn_terms = run_backward(
            layer_in,
            incoming_state,
            norm_in,
            grad_out,
            weights_back,
            projection,
            lengths,
            first_row,
        )
        grads = (
            attn_grads[0],
            attn_grads[1],
            attn_grads[2],
            attn_grads[3],
            ffn_terms[0],
            ffn_terms[1],
            attn_grads[4],
            ffn_terms[2],
        )
        totals = tuple(
            (total_part + is_valid * grad_part for total_part, grad_part in zip(totals, grads))
        )
        sent_back = grad_in.astype(jnp.bfloat16)
        chosen = (batch_range == batch_idx).astype(jnp.float32) * is_valid
        grad_inputs = grad_inputs + chosen[:, None, None] * sent_back.astype(jnp.float32)[None]
        if step_no < micro_count:
            grad_recv = passed_along(sent_back, "section", -1)
    shares = lax.psum_scatter(totals, ("dp", "seq"), scatter_dimension=0, tiled=True)
    activations = outputs.astype(jnp.bfloat16)[None, :, None]
    input_grad = grad_inputs.astype(jnp.bfloat16)[None, :, None]
    return (activations, input_grad) + tuple((share_part[None] for share_part in shares))


def solution(mesh):
    in_specs = (
        P(None, "dp", "seq", None),
        P(None, "dp", "seq", None),
        P(None, "dp", None),
        P("section", None, None, None),
        P("section", ("dp", "seq"), None),
        P("section", ("dp", "seq"), None),
        P("section", ("dp", "seq"), None),
        P("section", ("dp", "seq"), None),
        P("section", ("dp", "seq"), None),
        P("section", ("dp", "seq"), None),
        P("section", ("dp", "seq")),
        P("section", ("dp", "seq")),
    )
    out_specs = (
        P("section", None, "dp", "seq", None),
        P("section", None, "dp", "seq", None),
        P("section", ("dp", "seq"), None),
        P("section", ("dp", "seq"), None),
        P("section", ("dp", "seq"), None),
        P("section", ("dp", "seq"), None),
        P("section", ("dp", "seq"), None),
        P("section", ("dp", "seq"), None),
        P("section", ("dp", "seq")),
        P("section", ("dp", "seq")),
    )
    fits = mesh.shape["section"] == 2 and mesh.shape["dp"] == 4 and mesh.shape["seq"] == 4
    body = fast_local if fits else local
    return jax.shard_map(body, mesh=mesh, in_specs=in_specs, out_specs=out_specs, check_vma=False)
```

```python
import functools

import jax
import jax.numpy as jnp
from jax import lax
from jax.experimental import pallas as pl
from jax.experimental.pallas import tpu as pltpu
from jax.sharding import PartitionSpec as P

MESH = pl.DeviceIdType.MESH
F32 = jnp.float32
BF16 = jnp.bfloat16
VMEM_LIMIT = 63 << 20

ROW_Q, ROW_K, ROW_V, ROW_O, ROW_UP, ROW_DOWN, SLAB = 0, 32, 64, 96, 128, 256, 384
PORTIONS = ((0, 48), (96, 144))


def dot(a, b):
    return lax.dot_general(a, b, (((1,), (0,)), ((), ())), preferred_element_type=F32)


def dot_nt(a, b):
    return lax.dot_general(a, b, (((1,), (1,)), ((), ())), preferred_element_type=F32)


def dot_tn(a, b):
    return lax.dot_general(a, b, (((0,), (0,)), ((), ())), preferred_element_type=F32)


def remote(src, dst, ssem, rsem, dev):
    return pltpu.make_async_remote_copy(
        src_ref=src, dst_ref=dst, send_sem=ssem, recv_sem=rsem, device_id=dev, device_id_type=MESH
    )


class Place:
    def __init__(self):
        self.c = lax.axis_index("section")
        self.d = lax.axis_index("dp")
        self.z = lax.axis_index("seq")
        self.o = 1 - self.c
        self.xn = self.d + 1 - 2 * lax.rem(self.d, 2)
        self.yn = lax.rem(self.d + 2, 4)
        self.first = self.xn + self.c * (self.yn - self.xn)
        self.second = self.yn + self.c * (self.xn - self.yn)
        self.diag = 3 - self.d
        self.me = self.d * 4 + self.z

    def at(self, d, z):
        return (self.c, d, z)

    def sibling(self):
        return (self.o, self.d, self.z)

    def peers(self):
        out = [self.sibling(), self.at(self.xn, self.z), self.at(self.yn, self.z)]
        return out + [self.at(self.d, lax.rem(self.z + k, 4)) for k in (1, 2, 3)]

    def greet(self):
        for dev in self.peers():
            pl.semaphore_signal(pltpu.get_barrier_semaphore(), inc=1, device_id=dev, device_id_type=MESH)

    def meet(self):
        pl.semaphore_wait(pltpu.get_barrier_semaphore(), len(self.peers()))


def weight(G, l, row, n=32):
    return G[l, :, row : row + n, :].reshape(16 * n, 512)


def nearest(k):
    return k + (k // 2 if isinstance(k, int) else lax.div(k, 2)) * (5 - 2 * k)


class Gather:
    def __init__(self, pc, G, l, por, ssem, rsem, dsend, drecv, tiles=None):
        base, self.n = PORTIONS[por]
        self.pc, self.G, self.l, self.por = pc, G, l, por
        self.sems = ssem, rsem, dsend, drecv
        self.tiles = tiles
        self.start = pl.multiple_of(base + pc.c * self.n, 16)
        self.other = pl.multiple_of(base + pc.o * self.n, 16)

    def ref(self, g):
        return self.G.at[self.l, g, pl.ds(self.start, self.n)]

    def link(self, g, i, dev):
        ssem, rsem, _, _ = self.sems
        return remote(self.ref(g), self.ref(g), ssem.at[self.l, self.por, i], rsem.at[self.l, self.por, g], dev)

    def tile(self, g, i, dev):
        ref, tsend, trecv = self.tiles
        return remote(ref.at[g], ref.at[g], tsend.at[i], trecv.at[g], dev)

    def pass_to(self, g, i, dev):
        self.link(g, i, dev).start()
        if self.tiles:
            self.tile(g, i, dev).start()

    def sib(self, g):
        _, _, dsend, drecv = self.sems
        return remote(
            self.ref(g), self.ref(g), dsend.at[self.l, self.por, g], drecv.at[self.l, self.por, g], self.pc.sibling()
        )

    def arrive(self, g):
        self.link(g, 0, self.pc.sibling()).wait_recv()
        if self.tiles:
            self.tile(g, 0, self.pc.sibling()).wait_recv()

    def own(self):
        pc = self.pc
        for k in (1, 3, 2):
            self.pass_to(pc.me, k, pc.at(pc.d, lax.rem(pc.z + k, 4)))
        self.pass_to(pc.me, 4, pc.at(pc.first, pc.z))
        self.pass_to(pc.me, 8, pc.at(pc.second, pc.z))

    def column(self, k):
        pc = self.pc

        def step():
            g = pc.d * 4 + lax.rem(pc.z + nearest(k), 4)
            self.arrive(g)
            self.pass_to(g, 4 + k, pc.at(pc.first, pc.z))
            self.pass_to(g, 8 + k, pc.at(pc.second, pc.z))
            self.sib(g).start()

        if not isinstance(k, int):
            pl.when(k > 0)(step)
        elif k > 0:
            step()

    def across(self, k):
        pc = self.pc
        g = pc.first * 4 + lax.rem(pc.z + nearest(k), 4)
        self.arrive(g)
        self.pass_to(g, 12 + k, pc.at(pc.second, pc.z))
        self.sib(g).start()

    def far(self, k):
        pc = self.pc
        zz = lax.rem(pc.z + nearest(k), 4)
        for dp in (pc.second, pc.diag):
            g = dp * 4 + zz
            self.arrive(g)
            self.sib(g).start()

    def finish(self):
        _, _, dsend, drecv = self.sems
        pc = self.pc

        def wait(g):
            ref = self.G.at[self.l, g, pl.ds(self.other, self.n)]
            remote(ref, ref, dsend.at[self.l, self.por, g], drecv.at[self.l, self.por, g], pc.sibling()).wait_recv()

        def step(i, _):
            wait(lax.rem(pc.me + 1 + i, 16))
            return 0

        lax.fori_loop(0, 15, step, 0)

    def drain(self):
        pc = self.pc

        def step(i, _):
            self.link(pc.me, 1 + i, pc.at(pc.first, pc.z)).wait_send()
            if self.tiles:
                self.tile(pc.me, 1 + i, pc.at(pc.first, pc.z)).wait_send()
            self.sib(lax.rem(pc.me + 1 + i, 16)).wait_send()
            return 0

        lax.fori_loop(0, 15, step, 0)


def last_start(lengths, c, first_row, pos):
    starts = []
    at = 0
    for i in range(3):
        at = at + lengths[c, 0, i]
        starts.append(at - first_row)
    out = jnp.full(pos.shape, -first_row, jnp.int32)
    for s in starts:
        out = jnp.where(pos >= s, s, out)
    return out, starts


def norm(x):
    c = x - jnp.mean(x, axis=-1, keepdims=True)
    rstd = lax.rsqrt(jnp.mean(c * c, axis=-1, keepdims=True) + 1e-05)
    return c * rstd, rstd


def lane_low(shape):
    return lax.rem(lax.broadcasted_iota(jnp.int32, shape, 1), 128) < 64


def lift_pair(w, proj):
    hi = w.astype(BF16)
    low = (w - hi.astype(F32)).astype(BF16)
    sq = (w * w).astype(BF16)
    e = dot(jnp.concatenate([hi, sq, low, hi], axis=1), proj)
    return (jnp.exp(e) * 0.0625).astype(BF16)


def forward_kernel(
    inputs, lengths, wq_in, wk_in, wv_in, wo_in, wup_in, wdown_in, ga_in, gf_in, proj,
    act, G_out, fq_out, fk_out, v_out, att_out, rden_out, branch_out, w_out, x_out, sin_out, pb_out, gains_out,
    G, px, pk, mask, xbuf, hbuf, qbuf, kbuf, fq, fk, vext, att, rden, branch, wqk, xin, sin, tail, sbuf,
    gains, ybuf, hf, acc, tile_a, tile_b, tiles,
    ssem, rsem, dsend, drecv, osem, osem2, psem, csend, crecv, asem, wsem, gsend, grecv,
):
    pc = Place()
    c, z = pc.c, pc.z
    pc.greet()
    tile_a[...] = jnp.zeros_like(tile_a)
    tile_a[0:1, 0:32] = ga_in[...]
    tile_a[1:2, 0:32] = gf_in[...]
    placed = pltpu.roll(pltpu.roll(tile_a[...], 32 * z, 1), 2 * c, 0)
    tile_b[0] = placed.astype(BF16)
    for ref, row in ((wq_in, ROW_Q), (wk_in, ROW_K), (wv_in, ROW_V), (wo_in, ROW_O)):
        G[c, pc.me, row : row + 32, :] = ref[0].astype(BF16)
    for j in range(4):
        row = ROW_UP + 32 * j
        G[c, pc.me, row : row + 32, :] = wup_in[0, :, 512 * j : 512 * j + 512].astype(BF16)
    G[c, pc.me, ROW_DOWN:SLAB, :] = wdown_in[0].astype(BF16)
    hi = proj[0].astype(BF16)
    px[c, 0] = hi
    px[c, 1] = (proj[0] - hi.astype(F32)).astype(BF16)
    pc.meet()
    halves = {}
    for por, (base, n) in enumerate(PORTIONS):
        for half, at in ((0, pc.o), (1, c)):
            ref = G.at[c, pc.me, pl.ds(pl.multiple_of(base + at * n, 16), n)]
            halves[por, half] = remote(ref, ref, osem2.at[0, por, half], osem2.at[1, por, half], pc.sibling())
            halves[por, half].start()
    tsend = remote(tile_b.at[0], tile_b.at[1], psem.at[2], psem.at[3], pc.sibling())
    tsend.start()
    psend = remote(px.at[c], px.at[c], psem.at[0], psem.at[1], pc.sibling())
    psend.start()
    moves = {
        (l, por): Gather(
            pc, G, l, por, ssem, rsem, dsend, drecv, (tiles, gsend, grecv) if l == 0 and por == 0 else None
        )
        for l in (0, 1)
        for por in range(2)
    }

    def four(step):
        for k in range(4):
            step(k)

    for por in (0, 1):
        for half in (0, 1):
            halves[por, half].wait()
    tsend.wait()
    tiles[pc.me] = (tile_b[0].astype(F32) + tile_b[1].astype(F32)).astype(BF16)
    moves[0, 0].own()

    first_row = z * 512
    rows = lax.broadcasted_iota(jnp.int32, (512, 512), 0)
    cols = lax.broadcasted_iota(jnp.int32, (512, 512), 1)
    begin, starts = last_start(lengths, c, first_row, rows)
    mask[...] = ((cols <= rows) & (cols >= begin)).astype(F32)
    prow = lax.broadcasted_iota(jnp.int32, (512, 1), 0)
    begin_col, _ = last_start(lengths, c, first_row, prow)
    head_mask = (begin_col < 0).astype(F32)
    lane = lax.broadcasted_iota(jnp.int32, (1, 512), 1)
    inner = [jnp.where((s < 512) & (s >= 0), s, 0) for s in starts]
    cut = jnp.maximum(jnp.maximum(inner[0], inner[1]), inner[2])
    tail_mask = (lane >= cut).astype(F32)

    moves[0, 1].own()
    psend.wait()
    pk[...] = jnp.zeros_like(pk)
    for l in (0, 1):
        for p in range(4):
            for h in (0, 1):
                at = slice(64 * h, 64 * h + 64)
                to = slice(256 * h, 256 * h + 256)
                pk[l, p, at, to] = px[l, 0, 2 * p + h]
                pk[l, p, 128 + 64 * h : 192 + 64 * h, to] = jnp.full((64, 256), -0.5, BF16)
                pk[l, p, 256 + 64 * h : 320 + 64 * h, to] = px[l, 0, 2 * p + h]
                pk[l, p, 384 + 64 * h : 448 + 64 * h, to] = px[l, 1, 2 * p + h]
    keep = pltpu.make_async_copy(pk.at[:, :, 0:256, :], pb_out, osem)
    keep.start()
    vext[:, :, :, 128:] = jnp.ones((2, 4, 512, 128), BF16)

    @pl.when(z == 0)
    def _():
        sin[...] = jnp.zeros_like(sin)

    xbuf[...] = inputs[c, 0].astype(F32)
    four(moves[0, 0].column)
    moves[1, 0].own()
    four(moves[0, 0].across)
    moves[1, 1].own()
    four(moves[0, 1].column)
    four(moves[0, 0].far)
    four(moves[0, 1].across)
    moves[0, 0].finish()
    for dp in range(4):
        gains[:, 128 * dp : 128 * dp + 128] = jnp.sum(tiles[4 * dp : 4 * dp + 4].astype(F32), axis=0)
    gains_out[...] = gains[...]
    below = (c, pc.d, jnp.minimum(z + 1, 3))
    low = lane_low((512, 128))
    row_low = lax.broadcasted_iota(jnp.int32, (144, 256), 0)
    tail_is_first = (row_low < 64) | ((row_low >= 128) & (row_low < 136))
    low256 = lane_low((256, 128))

    def chain(l, p):
        return remote(sbuf.at[l, p], sin.at[l, p], csend.at[l, p], crecv.at[l, p], below)

    saved = (
        (G, G_out), (fq, fq_out), (fk, fk_out), (vext, v_out), (att, att_out), (rden, rden_out),
        (branch, branch_out), (wqk, w_out), (xin, x_out), (sin, sin_out),
    )

    def save(l, *refs):
        for i, (src, dst) in enumerate(saved):
            if any(src is ref for ref in refs):
                pltpu.make_async_copy(src.at[l], dst.at[l], wsem.at[l, i]).start()

    def give_own(l):
        return pltpu.make_async_copy(ybuf.at[l], act.at[c], asem.at[0])

    def give_far(l):
        return remote(ybuf.at[l], act.at[c], asem.at[1], asem.at[2], pc.sibling())

    def give(l):
        pl.when(c == l)(lambda: give_own(l).start())
        pl.when(c != l)(lambda: give_far(l).start())

    def layer(l, during):
        def norm_tile(i, _):
            at = pl.ds(pl.multiple_of(i * 128, 128), 128)
            x = xbuf[at, :]
            xin[l, at, :] = x.astype(BF16)
            hbuf[at, :] = (norm(x)[0] * gains[2 * l : 2 * l + 1, :]).astype(BF16)
            return 0

        lax.fori_loop(0, 4, norm_tile, 0)
        scale = 64 ** (-0.25)
        kbuf[...] = dot(hbuf[...], weight(G, l, ROW_K)) * scale
        qbuf[...] = dot(hbuf[...], weight(G, l, ROW_V))

        def pass_on(p):
            chain(l, p).wait_recv()
            sbuf[l, p] = (tail[p] + sin[l, p].astype(F32)).astype(BF16)
            chain(l, p).start()

        def key_pair(p, _):
            if "key" in during:
                during["key"](p)
            at = pl.ds(pl.multiple_of(p * 128, 128), 128)
            w = kbuf[:, at]
            wqk[l, 1, p] = w.astype(BF16)
            f = lift_pair(w, pk[l, p])
            fk[l, p] = f
            v = qbuf[:, at]
            vext[l, p, :, 0:128] = v.astype(BF16)
            vt = jnp.concatenate([v.T * tail_mask, jnp.broadcast_to(tail_mask, (16, 512))], axis=0).astype(BF16)
            t = jnp.where(tail_is_first, dot(vt, f[:, 0:256]), dot(vt, f[:, 256:512]))
            tail[p] = t

            @pl.when(z == 0)
            def _():
                sbuf[l, p] = t.astype(BF16)
                chain(l, p).start()

            @pl.when((z == 1) & (p >= 2))
            def _():
                pass_on(p - 2)

            return 0

        lax.fori_loop(0, 4, key_pair, 0)
        save(l, fk, vext, xin)
        qbuf[...] = dot(hbuf[...], weight(G, l, ROW_Q)) * scale

        def query_pair(p, _):
            if "query" in during:
                during["query"](p)
            at = pl.ds(pl.multiple_of(p * 128, 128), 128)
            w = qbuf[:, at]
            wqk[l, 0, p] = w.astype(BF16)
            fq[l, p] = lift_pair(w, pk[l, p])

            @pl.when((z == 1) & (p < 2))
            def _():
                pass_on(p + 2)

            @pl.when((z == 2) & (p >= 1))
            def _():
                pass_on(p - 1)

            return 0

        lax.fori_loop(0, 4, query_pair, 0)
        save(l, fq, wqk)

        def attend_pair(p, _):
            if "attend" in during:
                during["attend"](p)
            at = pl.ds(pl.multiple_of(p * 128, 128), 128)

            @pl.when((z == 2) & (p == 0))
            def _():
                pass_on(3)

            @pl.when(z == 3)
            def _():
                chain(l, p).wait_recv()

            for t in (0, 1):
                n = 256 * (t + 1)
                tr = slice(256 * t, 256 * t + 256)
                res = []
                for h in (0, 1):
                    fl = slice(256 * h, 256 * h + 256)
                    fqh = fq[l, p, tr, fl]
                    a = (dot_nt(fqh, fk[l, p, 0:n, fl]) * mask[tr, 0:n]).astype(BF16)
                    zrow = sin[l, p, 128:144, :].astype(F32)[8 * h : 8 * h + 1, :]
                    st = jnp.concatenate(
                        [sin[l, p, 0:128, :], jnp.broadcast_to(zrow, (128, 256)).astype(BF16)], axis=0
                    )
                    res.append(dot(a, vext[l, p, 0:n, :]) + head_mask[tr, :] * dot_nt(fqh, st))
                num = jnp.where(low256, res[0][:, 0:128], res[1][:, 0:128])
                den = jnp.where(low256, res[0][:, 128:256], res[1][:, 128:256])
                r = 1.0 / den
                att[l, tr, at] = num * r
                rden[l, tr, at] = r
            return 0

        lax.fori_loop(0, 4, attend_pair, 0)
        save(l, att, rden, sin)

        if "branch" in during:
            during["branch"]()

        def branch_tile(i, _):
            at = pl.ds(pl.multiple_of(i * 256, 256), 256)
            b = xbuf[at, :] + dot(att[l, at, :].astype(BF16), weight(G, l, ROW_O))
            branch[l, at, :] = b
            hf[at, :] = (norm(b)[0] * gains[2 * l + 1 : 2 * l + 2, :]).astype(BF16)
            acc[at, :] = b
            return 0

        save(l, G)
        lax.fori_loop(0, 2, branch_tile, 0)
        save(l, branch)

        def ffn_tile(j, _):
            if "ffn" in during:
                during["ffn"](j)
            up = G[l, :, pl.ds(pl.multiple_of(ROW_UP + 32 * j, 32), 32), :].reshape(512, 512)
            down = G[l, pl.ds(4 * j, 4), ROW_DOWN:SLAB, :].reshape(512, 512)
            for i in (0, 1):
                at = slice(256 * i, 256 * i + 256)
                pre = dot(hf[at, :], up)
                hid = jax.nn.gelu(pre).astype(BF16)
                acc[at, :] += dot(hid, down)
            return 0

        lax.fori_loop(0, 4, ffn_tile, 0)
        y = acc[...].astype(BF16)
        ybuf[l] = y
        xbuf[...] = y.astype(F32)
        give(l)

    def before_branch(l):
        if l == 0:
            four(moves[1, 0].across)
        else:
            for key in ((0, 0), (0, 1), (1, 0)):
                moves[key].drain()
        moves[l, 1].finish()

    layer(0, {"key": moves[1, 0].column, "query": moves[1, 1].column, "attend": moves[0, 1].far,
              "branch": lambda: before_branch(0), "ffn": moves[1, 1].across})
    four(moves[1, 0].far)
    moves[1, 0].finish()
    layer(1, {"query": moves[1, 1].far, "branch": lambda: before_branch(1)})
    give_own(0).wait()
    give_far(0).wait()
    keep.wait()
    for l in (0, 1):
        for i, (src, dst) in enumerate(saved):
            pltpu.make_async_copy(src.at[l], dst.at[l], wsem.at[l, i]).wait()

    @pl.when(z < 3)
    def _():
        for l in (0, 1):
            for p in range(4):
                chain(l, p).wait_send()

    moves[1, 1].drain()


def forward_call(inputs, lengths, weights, proj):
    sds = jax.ShapeDtypeStruct
    dma = pltpu.SemaphoreType.DMA
    vm = pl.BlockSpec(memory_space=pltpu.VMEM)
    hbm = pl.BlockSpec(memory_space=pl.ANY)
    saved = [
        sds((2, 16, SLAB, 512), BF16), sds((2, 4, 512, 512), BF16), sds((2, 4, 512, 512), BF16),
        sds((2, 4, 512, 256), BF16), sds((2, 512, 512), F32), sds((2, 512, 512), F32), sds((2, 512, 512), F32),
        sds((2, 2, 4, 512, 128), BF16), sds((2, 512, 512), BF16), sds((2, 4, 144, 256), BF16),
        sds((2, 4, 256, 512), BF16), sds((16, 512), F32),
    ]
    scratch = [
        pltpu.VMEM((2, 16, SLAB, 512), BF16),
        pltpu.VMEM((2, 2, 8, 64, 256), BF16),
        pltpu.VMEM((2, 4, 512, 512), BF16),
        pltpu.VMEM((512, 512), F32),
        pltpu.VMEM((512, 512), F32),
        pltpu.VMEM((512, 512), BF16),
        pltpu.VMEM((512, 512), F32),
        pltpu.VMEM((512, 512), F32),
        pltpu.VMEM((2, 4, 512, 512), BF16),
        pltpu.VMEM((2, 4, 512, 512), BF16),
        pltpu.VMEM((2, 4, 512, 256), BF16),
        pltpu.VMEM((2, 512, 512), F32),
        pltpu.VMEM((2, 512, 512), F32),
        pltpu.VMEM((2, 512, 512), F32),
        pltpu.VMEM((2, 2, 4, 512, 128), BF16),
        pltpu.VMEM((2, 512, 512), BF16),
        pltpu.VMEM((2, 4, 144, 256), BF16),
        pltpu.VMEM((4, 144, 256), F32),
        pltpu.VMEM((2, 4, 144, 256), BF16),
        pltpu.VMEM((16, 512), F32),
        pltpu.VMEM((2, 512, 512), BF16),
        pltpu.VMEM((512, 512), BF16),
        pltpu.VMEM((512, 512), F32),
        pltpu.VMEM((16, 128), F32),
        pltpu.VMEM((2, 16, 128), BF16),
        pltpu.VMEM((16, 16, 128), BF16),
        dma((2, 2, 16)), dma((2, 2, 16)), dma((2, 2, 16)), dma((2, 2, 16)), dma, dma((2, 2, 2)), dma((4,)),
        dma((2, 4)), dma((2, 4)), dma((3,)), dma((2, 10)), dma((16,)), dma((16,)),
    ]
    return pl.pallas_call(
        forward_kernel,
        out_shape=[sds((2, 512, 512), BF16)] + saved,
        in_specs=[vm, pl.BlockSpec(memory_space=pltpu.SMEM)] + [vm] * 9,
        out_specs=[vm] + [hbm] * (len(saved) - 1) + [vm],
        scratch_shapes=scratch,
        compiler_params=pltpu.CompilerParams(
            collective_id=0, has_side_effects=True, vmem_limit_bytes=VMEM_LIMIT
        ),
        name="forward",
    )(inputs, lengths, *weights, proj)


def gelu_parts(x):
    k = 0.7978845608028654
    x2 = x * x
    t = jnp.tanh(k * x * (1.0 + 0.044715 * x2))
    half = 0.5 * (1.0 + t)
    return x * half, half + 0.5 * x * (1.0 - t * t) * k * (1.0 + 0.134145 * x2)


def norm_back(y, rstd, dy):
    m1 = jnp.mean(dy, axis=-1, keepdims=True)
    m2 = jnp.mean(dy * y, axis=-1, keepdims=True)
    return rstd * (dy - m1 - y * m2)


HALF = (SLAB - ROW_Q) // 2
SUM_PORTIONS = ((ROW_O, 144), (ROW_Q, 48))


class Sums:
    def __init__(self, pc, slabs, bufs, sems, l, por):
        base, self.n = SUM_PORTIONS[por]
        self.pc, self.slabs, self.l, self.por = pc, slabs, l, por
        self.sb, self.r1, self.r2, self.r3, self.keep = bufs
        self.sems = sems
        self.mine = pl.multiple_of(base + pc.c * self.n, 16)
        self.other = pl.multiple_of(base + pc.o * self.n, 16)
        self.at = pl.ds(sum(2 * n for _, n in SUM_PORTIONS[:por]) // 2, self.n)

    def copy(self, i, j, src, dst, dev):
        ssem, rsem = self.sems
        return remote(src, dst, ssem.at[self.l, self.por, i, j], rsem.at[self.l, self.por, i, j], dev)

    def to_sibling(self, g):
        src = self.slabs.at[self.l, g, pl.ds(self.other, self.n)]
        return self.copy(0, g, src, self.sb.at[self.l, g, self.at], self.pc.sibling())

    def to_second(self, j, zz, g):
        src, dst = self.sb.at[self.l, g, self.at], self.r1.at[self.l, j, zz, self.at]
        return self.copy(1, 4 * j + zz, src, dst, self.pc.at(self.pc.second, self.pc.z))

    def to_first(self, zz, g):
        src, dst = self.sb.at[self.l, g, self.at], self.r2.at[self.l, zz, self.at]
        return self.copy(2, zz, src, dst, self.pc.at(self.pc.first, self.pc.z))

    def along(self, k, g):
        src, dst = self.sb.at[self.l, g, self.at], self.r3.at[self.l, 3 - k, self.at]
        return self.copy(3, 3 - k, src, dst, self.pc.at(self.pc.d, lax.rem(self.pc.z + k, 4)))

    def begin(self):
        pc = self.pc
        for k in (1, 2, 3, 0):
            for col in (pc.diag, pc.second, pc.first, pc.d):
                self.to_sibling(col * 4 + lax.rem(pc.z + k, 4)).start()

    def pair(self, g):
        self.to_sibling(g).wait_recv()
        own = self.slabs[self.l, g, pl.ds(self.mine, self.n), :]
        return own.astype(F32) + self.sb[self.l, g, self.at, :].astype(F32)

    def stage1(self, j, i):
        pc = self.pc
        zz = lax.rem(pc.z + 1 + i, 4)
        g = (pc.diag if j == 0 else pc.second) * 4 + zz
        self.sb[self.l, g, self.at, :] = self.pair(g).astype(BF16)
        self.to_second(j, zz, g).start()

    def stage2(self, i):
        pc = self.pc
        zz = lax.rem(pc.z + 1 + i, 4)
        g = pc.first * 4 + zz
        s = self.pair(g)
        self.to_second(0, zz, g).wait_recv()
        self.sb[self.l, g, self.at, :] = (s + self.r1[self.l, 0, zz, self.at, :].astype(F32)).astype(BF16)
        self.to_first(zz, g).start()

    def stage3(self, k):
        pc = self.pc
        zz = lax.rem(pc.z + k, 4)
        g = pc.d * 4 + zz
        s = self.pair(g)
        self.to_second(1, zz, g).wait_recv()
        s = s + self.r1[self.l, 1, zz, self.at, :].astype(F32)
        self.to_first(zz, g).wait_recv()
        s = s + self.r2[self.l, zz, self.at, :].astype(F32)
        if k:
            self.sb[self.l, g, self.at, :] = s.astype(BF16)
            self.along(k, g).start()
        else:
            self.keep[self.l, self.at, :] = s

    def stage4(self, l):
        s = self.keep[l, self.at, :]
        for i in range(3):
            s = s + self.r3[l, i, self.at, :].astype(F32)
        return s

    def arrive(self):
        for k in (1, 2, 3):
            self.along(k, self.pc.me).wait_recv()

    def drain(self):
        for i in range(16):
            self.to_sibling(i).wait_send()
        for j in (0, 1):
            for zz in range(4):
                self.to_second(j, zz, 0).wait_send()
        for zz in range(4):
            self.to_first(zz, 0).wait_send()
        for k in (1, 2, 3):
            self.along(k, 0).wait_send()


def backward_kernel(
    cotangent, lengths, wq_in, wk_in, wv_in, wup_in, G_in, fq_in, fk_in, v_in, att_in, rden_in, branch_in, w_in, x_in, sin_in, pb_in, gains_in,
    gin, gq_out, gk_out, gv_out, go_out, gup_out, gdown_out, gg_out,
    G, fq, fk, vext, att, rden, branch, wqk, xin, sin, pb,
    mask, mask_t, gbuf, gbr, hbuf, hT, gb, dh, gq, gk, gv, le, rin, rtail, rbuf, gains, xout, slabs,
    sb, r1, r2, r3, keep, total,
    lsem, csend, crecv, asem, ssem, rsem, fsem,
):
    pc = Place()
    c, z = pc.c, pc.z
    attn, ffn = pl.ds(ROW_Q, ROW_UP - ROW_Q), pl.ds(ROW_UP, SLAB - ROW_UP)
    loads = {
        "branch": (lambda l: branch_in.at[l], branch),         "ffn": (lambda l: G_in.at[l, :, ffn], G.at[:, ffn]), "att": (lambda l: att_in.at[l], att),
        "attn": (lambda l: G_in.at[l, :, attn], G.at[:, attn]), "rden": (lambda l: rden_in.at[l], rden),
        "fq": (lambda l: fq_in.at[l], fq), "sin": (lambda l: sin_in.at[l], sin), "fk": (lambda l: fk_in.at[l], fk),
        "vext": (lambda l: v_in.at[l], vext), "pb": (lambda l: pb_in.at[l], pb), "wqk": (lambda l: w_in.at[l], wqk),
        "xin": (lambda l: x_in.at[l], xin),
    }

    def load(l, name):
        src, dst = loads[name]
        return pltpu.make_async_copy(src(l), dst, lsem.at[list(loads).index(name)])

    def needs(l, *names):
        for name in names:
            load(l, name).wait()

    def done(l, *names):
        if l == 1:
            for name in names:
                load(0, name).start()

    pc.greet()
    gains[...] = gains_in[...]
    for name in loads:
        load(1, name).start()

    first_row = z * 512
    rows = lax.broadcasted_iota(jnp.int32, (512, 512), 0)
    cols = lax.broadcasted_iota(jnp.int32, (512, 512), 1)
    begin, starts = last_start(lengths, c, first_row, rows)
    mask[...] = ((cols <= rows) & (cols >= begin)).astype(F32).astype(BF16)
    begin, _ = last_start(lengths, c, first_row, cols)
    mask_t[...] = ((rows <= cols) & (rows >= begin)).astype(F32).astype(BF16)
    prow = lax.broadcasted_iota(jnp.int32, (512, 1), 0)
    begin_col, _ = last_start(lengths, c, first_row, prow)
    head_col = (begin_col < 0).astype(F32)
    lane = lax.broadcasted_iota(jnp.int32, (1, 512), 1)
    begin_row, _ = last_start(lengths, c, first_row, lane)
    head_row = (begin_row < 0).astype(F32)
    inner = [jnp.where((s < 512) & (s >= 0), s, 0) for s in starts]
    cut = jnp.maximum(jnp.maximum(inner[0], inner[1]), inner[2])
    tail_col = (prow >= cut).astype(F32)

    @pl.when(z == 3)
    def _():
        rin[...] = jnp.zeros_like(rin)

    gbuf[...] = cotangent[c, 0].astype(F32)
    pc.meet()
    above = (c, pc.d, jnp.maximum(z - 1, 0))
    row_low = lax.broadcasted_iota(jnp.int32, (144, 256), 0)
    tail_is_first = (row_low < 64) | ((row_low >= 128) & (row_low < 136))
    low = lane_low((512, 128))
    ones_i = lax.broadcasted_iota(jnp.int32, (256, 128), 0)
    ones_j = lax.broadcasted_iota(jnp.int32, (256, 128), 1)
    head_ones = (lax.rem(ones_i, 128) // 64 == ones_j // 64).astype(BF16)
    scale = 64 ** (-0.25)

    def chain(l, p):
        return remote(rbuf.at[l, p], rin.at[l, p], csend.at[l, p], crecv.at[l, p], above)

    sums = {(l, por): Sums(pc, slabs, (sb, r1, r2, r3, keep), (ssem, rsem), l, por) for l in (0, 1) for por in (0, 1)}

    def put(l, row, n, value):
        slabs[l, :, row : row + n, :] = value.astype(BF16).reshape(16, n, 512)

    def layer(l, during):
        def at_point(name, *args):
            if name in during:
                during[name](*args)

        needs(l, "branch")

        def norm_tile(i, _):
            at = pl.ds(pl.multiple_of(i * 128, 128), 128)
            hbuf[at, :] = (norm(branch[at, :])[0] * gains[2 * l + 1 : 2 * l + 2, :]).astype(BF16)
            gb[at, :] = gbuf[at, :].astype(BF16)
            return 0

        lax.fori_loop(0, 4, norm_tile, 0)
        hT[...] = hbuf[...].T
        dh[...] = jnp.zeros_like(dh)

        def ffn_tile(j, _):
            at_point("ffn", j)
            up_at = pl.ds(pl.multiple_of(ROW_UP + 32 * j, 32), 32)
            up = G[:, up_at, :].reshape(512, 512)
            down = G[pl.ds(4 * j, 4), ROW_DOWN:SLAB, :].reshape(512, 512)
            for i in (0, 1):
                at = slice(256 * i, 256 * i + 256)
                hid, slope = gelu_parts(dot(hbuf[at, :], up))
                gq[at, :] = hid.astype(BF16)
                gk[at, :] = (slope * dot_nt(gb[at, :], down)).astype(BF16)
            slabs[l, pl.ds(4 * j, 4), ROW_DOWN:SLAB, :] = dot_tn(gq[...], gb[...]).astype(BF16).reshape(4, 128, 512)
            g = gk[...]
            slabs[l, :, up_at, :] = dot(hT[...], g).astype(BF16).reshape(16, 32, 512)
            dh[...] += dot_nt(g, up)
            return 0

        needs(l, "ffn")
        lax.fori_loop(0, 4, ffn_tile, 0)
        done(l, "ffn")
        needs(l, "att")

        def branch_tile(i, _):
            at_point("branch", i)
            at = pl.ds(pl.multiple_of(i * 128, 128), 128)
            y, rstd = norm(branch[at, :])
            d = dh[at, :]
            g = gbuf[at, :] + norm_back(y, rstd, d * gains[2 * l + 1 : 2 * l + 2, :])
            gbr[at, :] = g
            gb[at, :] = g.astype(BF16)
            hbuf[at, :] = att[at, :].astype(BF16)
            return 0

        lax.fori_loop(0, 4, branch_tile, 0)
        done(l, "branch")
        put(l, ROW_O, 32, dot_tn(hbuf[...], gb[...]))
        sums[l, 0].begin()
        at_point("middle")
        needs(l, "attn", "rden", "fq")
        dh[...] = dot_nt(gb[...], G[:, ROW_O : ROW_O + 32, :].reshape(512, 512))

        def pass_on(p):
            chain(l, p).wait_recv()
            rbuf[l, p] = (rtail[p] + rin[l, p].astype(F32)).astype(BF16)
            chain(l, p).start()

        def tail_pair(p, _):
            at_point("tail", p)
            at = pl.ds(pl.multiple_of(p * 128, 128), 128)
            g = dh[:, at]
            r = rden[:, at]
            t = g * att[:, at]
            hi = t.astype(BF16)
            lo = (t - hi.astype(F32)).astype(BF16)
            dden = -dot(jnp.concatenate([hi, lo], axis=1), head_ones) * r
            dnum = g * r
            le[p] = jnp.concatenate([dnum, dden * (1.0 / 64.0)], axis=1).astype(BF16)
            dt = (dden.T) * head_row
            lhs = jnp.concatenate([dnum.T * head_row, dt[0:8], dt[64:72]], axis=0).astype(BF16)
            tl = jnp.where(tail_is_first, dot(lhs, fq[p, :, 0:256]), dot(lhs, fq[p, :, 256:512]))
            rtail[p] = tl

            @pl.when(z == 3)
            def _():
                rbuf[l, p] = tl.astype(BF16)
                chain(l, p).start()

            return 0

        lax.fori_loop(0, 4, tail_pair, 0)
        done(l, "att", "rden")
        needs(l, "sin", "fk", "vext", "pb", "wqk")

        def of_head(h, value):
            keep = lane_low(value.shape) if h == 0 else jnp.logical_not(lane_low(value.shape))
            return jnp.where(keep, value, jnp.zeros((), BF16))

        def through_lift(p, k, e):
            gw = dot_nt(jnp.concatenate(e, axis=1), pb[p])
            gw = gw[:, 0:128] + 2.0 * wqk[k, p].astype(F32) * gw[:, 128:256]
            return (gw * scale).astype(BF16)

        def query_pair(p, _):
            at_point("query", p)
            at = pl.ds(pl.multiple_of(p * 128, 128), 128)

            @pl.when((z == 2) & (p >= 1))
            def _():
                pass_on(p - 1)

            ve = vext[p]
            lep = le[p]
            dq = []
            for h in (0, 1):
                fl = slice(256 * h, 256 * h + 256)
                leh = of_head(h, lep)
                fkh = fk[p, :, fl]
                zrow = sin[p, 128:144, :].astype(F32)[8 * h : 8 * h + 1, :]
                st = jnp.concatenate([sin[p, 0:128, :], jnp.broadcast_to(zrow, (128, 256)).astype(BF16)], axis=0)
                dqh = head_col * dot(leh, st)
                da0 = dot_nt(leh[0:256], ve[0:256]).astype(BF16) * mask[0:256, 0:256]
                da1 = dot_nt(leh[256:512], ve).astype(BF16) * mask[256:512, :]
                dqh = dqh + jnp.concatenate([dot(da0, fkh[0:256]), dot(da1, fkh)], axis=0)
                dq.append((dqh * fq[p, :, fl].astype(F32)).astype(BF16))
            gq[:, at] = through_lift(p, 0, dq)
            return 0

        lax.fori_loop(0, 4, query_pair, 0)

        needs(l, "xin")

        def norm_tile2(i, _):
            at = pl.ds(pl.multiple_of(i * 128, 128), 128)
            hbuf[at, :] = (norm(xin[at, :].astype(F32))[0] * gains[2 * l : 2 * l + 1, :]).astype(BF16)
            return 0

        lax.fori_loop(0, 4, norm_tile2, 0)
        hT[...] = hbuf[...].T
        def attend_pair(p, _):
            at_point("attend", p)
            at = pl.ds(pl.multiple_of(p * 128, 128), 128)

            @pl.when((z == 2) & (p == 0))
            def _():
                pass_on(3)

            ve = vext[p]
            lep = le[p]
            dk, dv = [], []
            for h in (0, 1):
                if h == 1:
                    @pl.when(z == 1)
                    def _():
                        pass_on(p)

                fl = slice(256 * h, 256 * h + 256)
                leh = of_head(h, lep)
                fqh, fkh = fq[p, :, fl], fk[p, :, fl]
                at0 = dot_nt(fkh[0:256], fqh).astype(BF16) * mask_t[0:256, :]
                at1 = dot_nt(fkh[256:512], fqh[256:512]).astype(BF16) * mask_t[256:512, 256:512]
                dv.append(jnp.concatenate([dot(at0, lep[:, 0:128]), dot(at1, lep[256:512, 0:128])], axis=0))
                dt0 = dot_nt(ve[0:256], leh).astype(BF16) * mask_t[0:256, :]
                dt1 = dot_nt(ve[256:512], leh[256:512]).astype(BF16) * mask_t[256:512, 256:512]
                dk.append(jnp.concatenate([dot(dt0, fqh), dot(dt1, fqh[256:512])], axis=0))

            @pl.when(z == 0)
            def _():
                chain(l, p).wait_recv()

            for h in (0, 1):
                fkh = fk[p, :, 256 * h : 256 * h + 256]
                rrow = rin[l, p, 128:144, :].astype(F32)[8 * h : 8 * h + 1, :] * (1.0 / 128.0)
                rows_h = lax.broadcasted_iota(jnp.int32, (128, 256), 0) // 64 == h
                rt = jnp.where(rows_h, rin[l, p, 0:128, :], jnp.zeros((), BF16))
                rte = jnp.concatenate([rt, jnp.broadcast_to(rrow, (128, 256)).astype(BF16)], axis=0)
                dv[h] = dv[h] + tail_col * dot_nt(fkh, rin[l, p, 0:128, :])
                dk[h] = ((dk[h] + tail_col * dot(ve, rte)) * fkh.astype(F32)).astype(BF16)
            gv[:, at] = jnp.where(low, dv[0], dv[1]).astype(BF16)
            gk[:, at] = through_lift(p, 1, dk)
            return 0

        lax.fori_loop(0, 4, attend_pair, 0)
        done(l, "fq", "sin", "fk", "vext", "pb", "wqk")

        at_point("norm")
        for row, g in ((ROW_Q, gq), (ROW_K, gk), (ROW_V, gv)):
            put(l, row, 32, dot(hT[...], g[...]))
        sums[l, 1].begin()
        dh[...] = dot_nt(gq[...], G[:, ROW_Q : ROW_Q + 32, :].reshape(512, 512))
        dh[...] += dot_nt(gk[...], G[:, ROW_K : ROW_K + 32, :].reshape(512, 512))
        dh[...] += dot_nt(gv[...], G[:, ROW_V : ROW_V + 32, :].reshape(512, 512))

        done(l, "attn")
        at_point("late")

        def out_tile(i, _):
            at_point("out", i)
            at = pl.ds(pl.multiple_of(i * 128, 128), 128)
            y, rstd = norm(xin[at, :].astype(F32))
            d = dh[at, :]
            g = (gbr[at, :] + norm_back(y, rstd, d * gains[2 * l : 2 * l + 1, :])).astype(BF16)
            xout[l, at, :] = g
            gbuf[at, :] = g.astype(F32)
            return 0

        lax.fori_loop(0, 4, out_tile, 0)
        done(l, "xin")

    def four(step, *args):
        for i in range(4):
            step(*args, i)

    def along_z(m):
        for k in (1, 2, 3, 0):
            m.stage3(k)

    def both(m):
        return lambda i: (m.stage1(0, i), m.stage1(1, i))

    def at_steps(**steps):
        def run(i):
            for name, step in steps.items():
                pl.when(i == int(name[1:]))(step)

        return run

    def larger(l, extra=lambda: None):
        m = sums[l, 0]
        return {
            "tail": both(m),
            "attend": at_steps(i1=lambda: m.stage2(0), i2=lambda: m.stage2(1), i3=lambda: extra()),
            "norm": lambda: (m.stage3(1), m.stage2(2)),
            "late": lambda: m.stage3(2),
            "out": at_steps(i1=lambda: m.stage2(3)),
        }

    m1, m0 = sums[1, 0], sums[0, 0]
    layer(1, {"tail": both(m1), "attend": at_steps(i1=lambda: m1.stage2(0), i3=lambda: m1.stage2(1)),
              "norm": lambda: m1.stage2(2), "out": at_steps(i1=lambda: m1.stage2(3), i3=lambda: m1.stage3(1))})
    early = at_steps(i0=lambda: m1.stage3(2), i1=lambda: m1.stage3(3), i2=lambda: m1.stage3(0))
    hooks = larger(0, lambda: four(sums[1, 1].stage2))
    late_steps = hooks["out"]
    hooks["out"] = lambda i: (both(sums[0, 1])(i), late_steps(i))
    layer(0, {"ffn": lambda i: (early(i), both(sums[1, 1])(i)), **hooks})
    own_act = pltpu.make_async_copy(xout.at[c], gin.at[c], asem.at[0])
    own_act.start()
    far_act = remote(xout.at[pc.o], gin.at[c], asem.at[1], asem.at[2], pc.sibling())
    far_act.start()
    own_act.wait()
    far_act.wait()

    along_z(sums[1, 1])
    sums[1, 0].drain()
    sums[0, 0].stage3(3)
    sums[0, 0].stage3(0)
    four(sums[0, 1].stage2)
    along_z(sums[0, 1])
    for m in sums.values():
        m.arrive()
    for por in (0, 1):
        m = sums[0, por]
        gbr[m.at, :] = m.stage4(pc.o)
    parts = []
    for por in (0, 1):
        m = sums[0, por]
        part = remote(gbr.at[m.at], total.at[pl.ds(m.mine, m.n)], fsem.at[0, por], fsem.at[1, por], pc.sibling())
        part.start()
        parts.append(part)
    for por in (0, 1):
        m = sums[0, por]
        total[pl.ds(m.mine, m.n), :] = m.stage4(c)
    for part in parts:
        part.wait()
    for ref, row in ((gq_out, ROW_Q), (gk_out, ROW_K), (gv_out, ROW_V), (go_out, ROW_O)):
        ref[...] = total[row : row + 32, :]
    for j in range(4):
        gup_out[:, 512 * j : 512 * j + 512] = total[ROW_UP + 32 * j : ROW_UP + 32 * j + 32, :]
    gdown_out[...] = total[ROW_DOWN:SLAB, :]
    ga = jnp.zeros((32, 512), F32)
    for ref, row in ((wq_in, ROW_Q), (wk_in, ROW_K), (wv_in, ROW_V)):
        ga = ga + ref[0].astype(BF16).astype(F32) * total[row : row + 32, :]
    gf = jnp.zeros((32, 512), F32)
    for j in range(4):
        up = wup_in[0, :, 512 * j : 512 * j + 512].astype(BF16).astype(F32)
        gf = gf + up * total[ROW_UP + 32 * j : ROW_UP + 32 * j + 32, :]
    gg_out[0] = jnp.broadcast_to(jnp.sum(ga, axis=1, keepdims=True), (32, 128))
    gg_out[1] = jnp.broadcast_to(jnp.sum(gf, axis=1, keepdims=True), (32, 128))
    for key in ((1, 1), (0, 0), (0, 1)):
        sums[key].drain()

    @pl.when(z > 0)
    def _():
        for l in (0, 1):
            for p in range(4):
                chain(l, p).wait_send()


def backward_call(cotangent, lengths, weights, saved):
    sds = jax.ShapeDtypeStruct
    dma = pltpu.SemaphoreType.DMA
    vm = pl.BlockSpec(memory_space=pltpu.VMEM)
    hbm = pl.BlockSpec(memory_space=pl.ANY)
    bufs = [pltpu.VMEM(a.shape[1:], a.dtype) for a in saved[:-1]]
    full = (512, 512)
    scratch = bufs + [
        pltpu.VMEM(full, BF16),
        pltpu.VMEM(full, BF16),
        pltpu.VMEM(full, F32),
        pltpu.VMEM(full, F32),
        pltpu.VMEM(full, BF16),
        pltpu.VMEM(full, BF16),
        pltpu.VMEM(full, BF16),
        pltpu.VMEM(full, F32),
        pltpu.VMEM(full, BF16),
        pltpu.VMEM(full, BF16),
        pltpu.VMEM(full, BF16),
        pltpu.VMEM((4, 512, 256), BF16),
        pltpu.VMEM((2, 4, 144, 256), BF16),
        pltpu.VMEM((4, 144, 256), F32),
        pltpu.VMEM((2, 4, 144, 256), BF16),
        pltpu.VMEM((16, 512), F32),
        pltpu.VMEM((2, 512, 512), BF16),
        pltpu.VMEM((2, 16, SLAB, 512), BF16),
        pltpu.VMEM((2, 16, HALF, 512), BF16),
        pltpu.VMEM((2, 2, 4, HALF, 512), BF16),
        pltpu.VMEM((2, 4, HALF, 512), BF16),
        pltpu.VMEM((2, 3, HALF, 512), BF16),
        pltpu.VMEM((2, HALF, 512), F32),
        pltpu.VMEM((SLAB, 512), F32),
        dma((13,)), dma((2, 4)), dma((2, 4)), dma((3,)), dma((2, 2, 4, 16)), dma((2, 2, 4, 16)), dma((2, 2)),
    ]
    return pl.pallas_call(
        backward_kernel,
        out_shape=[sds((2, 512, 512), BF16)]
        + [sds((32, 512), F32)] * 4
        + [sds((32, 2048), F32), sds((128, 512), F32), sds((2, 32, 128), F32)],
        in_specs=[vm, pl.BlockSpec(memory_space=pltpu.SMEM)] + [vm] * 4 + [hbm] * (len(saved) - 1) + [vm],
        out_specs=[vm] * 8,
        scratch_shapes=scratch,
        compiler_params=pltpu.CompilerParams(
            collective_id=1, has_side_effects=True, vmem_limit_bytes=VMEM_LIMIT
        ),
        name="backward",
    )(cotangent, lengths, *weights, *saved)


def finish_kernel(*refs):
    n = len(refs) // 2
    ins, outs, sems = refs[:n], refs[n : 2 * n - 1], refs[2 * n - 1 :]
    sums, ga, gf = ins[n - 3 :]
    copies = [pltpu.make_async_copy(src, dst, sems[0].at[i]) for i, (src, dst) in enumerate(zip(ins[: n - 3], outs))]
    for copy in copies:
        copy.start()
    for i, gain in ((0, ga), (1, gf)):
        outs[n - 3 + i][...] = sums[i].T[0:1, 0:32] / gain[...].astype(BF16).astype(F32)
    for copy in copies:
        copy.wait()


def finish_call(results, sums, gain_attn, gain_ffn):
    vm = pl.BlockSpec(memory_space=pltpu.VMEM)
    hbm = pl.BlockSpec(memory_space=pl.ANY)
    n = len(results)
    return pl.pallas_call(
        finish_kernel,
        out_shape=[jax.ShapeDtypeStruct(r.shape, r.dtype) for r in results + [gain_attn, gain_ffn]],
        in_specs=[hbm] * n + [vm] * 3,
        out_specs=[vm] * (n + 2),
        scratch_shapes=[pltpu.SemaphoreType.DMA((n,))],
        name="finish",
    )(*results, sums, gain_attn, gain_ffn)


def fast_local(inputs, cotangent, doc_lengths, feature_proj, *weights):
    act, *saved = forward_call(inputs, doc_lengths, weights, feature_proj)
    w_query, w_key, w_value, _, w_up = weights[:5]
    gin, *grads = backward_call(cotangent, doc_lengths, (w_query, w_key, w_value, w_up), saved)
    done = finish_call([act, gin] + grads[:6], grads[6], weights[6], weights[7])
    return (done[0][None, :, None], done[1][None, :, None]) + tuple(g[None] for g in done[2:8]) + tuple(done[8:])


HIGH_PRECISION = lax.Precision.HIGHEST


def prefix(shard, axis, join, neutral):
    place = lax.axis_index(axis)
    gathered = jax.tree.map(
        lambda a, kind: lax.all_gather(a.astype(kind), axis),
        shard,
        (jnp.bfloat16, jnp.bfloat16, jnp.bfloat16),
    )
    state = jax.tree.map(lambda a, e: jnp.zeros_like(a) + jnp.asarray(e, a.dtype), shard, neutral)

    def prefix_one(lap, state):
        return join(
            state,
            jax.tree.map(
                lambda a, own: lax.dynamic_index_in_dim(a, lap, 0, False).astype(own.dtype),
                gathered,
                shard,
            ),
        )

    return lax.fori_loop(0, place, prefix_one, state)


def entering(shard, axis, join, neutral):
    count = lax.axis_size(axis)
    place = lax.axis_index(axis)
    ahead = count - 1 - place
    gathered = jax.tree.map(
        lambda a, kind: lax.all_gather(a.astype(kind), axis),
        shard,
        jax.tree.map(lambda a: jnp.bfloat16 if a.dtype == jnp.float32 else a.dtype, shard),
    )
    state = jax.tree.map(lambda a, e: jnp.zeros_like(a) + jnp.asarray(e, a.dtype), shard, neutral)

    def entering_one(lap, state):
        source = count - 1 - lap
        return join(
            state,
            jax.tree.map(
                lambda a, own: lax.dynamic_index_in_dim(a, source, 0, False).astype(own.dtype),
                gathered,
                shard,
            ),
        )

    return lax.fori_loop(0, ahead, entering_one, state)


def as_sent(shard):

    def short(part):
        return part.astype(jnp.bfloat16) if part.dtype == jnp.float32 else part

    return jax.tree.map(short, shard)


def passed_along(block, axis, distance):
    devices = range(lax.axis_size(axis))
    route = [(i - distance, i) for i in devices if i - distance in devices]
    return lax.ppermute(block, axis, route)


def matmul(left, right):
    return jnp.dot(left, right, preferred_element_type=jnp.float32)


def norm_rows(values):
    centre = values - jnp.mean(values, axis=-1, keepdims=True)
    return centre * lax.rsqrt(jnp.mean(centre * centre, axis=-1, keepdims=True) + 1e-05)


def lift(values, projection):
    heads, depth, feats = projection.shape
    scaled = values.reshape(values.shape[0], heads, depth) * depth ** (-0.25)
    raised = jnp.einsum("nhd,hdm->nhm", scaled, projection, precision=HIGH_PRECISION)
    return jnp.exp(raised - 0.5 * jnp.sum(scaled * scaled, axis=-1, keepdims=True)) * feats ** (
        -0.5
    )


def doc_masks(lengths, first_row, row_count):
    doc_ends = jnp.cumsum(lengths, dtype=jnp.int32)
    starts = doc_ends - lengths
    positions = first_row + jnp.arange(row_count, dtype=jnp.int32)
    begun_at = starts[None, :] <= positions[:, None]
    doc_ids = jnp.sum(begun_at.astype(jnp.int32), axis=1)
    order_idx = jnp.arange(row_count, dtype=jnp.int32)
    same_doc = (
        (doc_ids[:, None] == doc_ids[None, :]) & (order_idx[None, :] <= order_idx[:, None])
    ).astype(jnp.float32)
    inside = (starts >= first_row) & (starts < first_row + row_count)
    mask_per_head = (jnp.sum((begun_at & inside[None, :]).astype(jnp.int32), axis=1) == 0).astype(
        jnp.float32
    )
    tail_mask = (jnp.sum((~begun_at & inside[None, :]).astype(jnp.int32), axis=1) == 0).astype(
        jnp.float32
    )
    kept_flag = (jnp.sum(inside.astype(jnp.int32)) == 0).astype(jnp.float32)
    return (same_doc, mask_per_head, tail_mask, kept_flag)


def attend(query_features, feats_k, value_heads, incoming_state, norm_in, same_doc, mask_per_head):
    scores = (
        jnp.einsum("thm,shm->hts", query_features, feats_k, precision=HIGH_PRECISION)
        * same_doc[None]
    )
    attention_numerator = jnp.einsum("hts,shd->thd", scores, value_heads, precision=HIGH_PRECISION)
    attention_numerator = attention_numerator + mask_per_head[:, None, None] * jnp.einsum(
        "kec,ecz->kez", query_features, incoming_state, precision=HIGH_PRECISION
    )
    denominator = jnp.sum(scores, axis=2).T + mask_per_head[:, None] * jnp.einsum(
        "thm,hm->th", query_features, norm_in, precision=HIGH_PRECISION
    )
    return (attention_numerator / denominator[:, :, None]).reshape(query_features.shape[0], -1)


def tail_sums(feats_k, value_heads, tail_mask):
    weighted_values = feats_k * tail_mask[:, None, None]
    return (
        jnp.einsum("zlu,zlv->luv", weighted_values, value_heads, precision=HIGH_PRECISION),
        jnp.sum(weighted_values, axis=0),
    )


def combine_carry(earlier, later_part):
    return (
        earlier[0] * later_part[0],
        later_part[1] + later_part[0] * earlier[1],
        later_part[2] + later_part[0] * earlier[2],
    )


def run_forward(layer_in, weights, projection, lengths, first_row):
    w_query, w_key, w_value, w_out, w_up, w_down, gain_attn, gain_ffn = weights
    row_count = layer_in.shape[0]
    same_doc, mask_per_head, tail_mask, kept_flag = doc_masks(lengths, first_row, row_count)
    h_attn = (norm_rows(layer_in) * gain_attn.astype(jnp.float32)).astype(jnp.bfloat16)
    query_features = lift(matmul(h_attn, w_query), projection)
    feats_k = lift(matmul(h_attn, w_key), projection)
    value_heads = matmul(h_attn, w_value).reshape(row_count, projection.shape[0], -1)
    state_tail, norm_tail = tail_sums(feats_k, value_heads, tail_mask)
    identity = (jnp.ones((), jnp.float32), jnp.zeros_like(state_tail), jnp.zeros_like(norm_tail))
    _, incoming_state, norm_in = prefix(
        (kept_flag, state_tail, norm_tail), "seq", combine_carry, identity
    )
    mixed_heads = attend(
        query_features, feats_k, value_heads, incoming_state, norm_in, same_doc, mask_per_head
    ).astype(jnp.bfloat16)
    branch = layer_in + matmul(mixed_heads, w_out)
    h_ffn = (norm_rows(branch) * gain_ffn.astype(jnp.float32)).astype(jnp.bfloat16)
    hidden = jax.nn.gelu(matmul(h_ffn, w_up)).astype(jnp.bfloat16)
    return (branch + matmul(hidden, w_down), incoming_state, norm_in)


def run_backward(
    layer_in, incoming_state, norm_in, grad_out, weights, projection, lengths, first_row
):
    w_query, w_key, w_value, w_out, w_up, w_down, gain_attn, gain_ffn = weights
    row_count = layer_in.shape[0]
    same_doc, mask_per_head, tail_mask, kept_flag = doc_masks(lengths, first_row, row_count)
    gain_a = gain_attn.astype(jnp.float32)
    gain_f = gain_ffn.astype(jnp.float32)
    normed_a, norm_a_back = jax.vjp(norm_rows, layer_in)
    h_attn = (normed_a * gain_a).astype(jnp.bfloat16)
    query_features, lift_q_back = jax.vjp(lambda z: lift(z, projection), matmul(h_attn, w_query))
    feats_k, lift_k_back = jax.vjp(lambda z: lift(z, projection), matmul(h_attn, w_key))
    value_heads = matmul(h_attn, w_value).reshape(row_count, projection.shape[0], -1)
    attended, attend_back = jax.vjp(
        lambda a, b, c, d, e: attend(a, b, c, d, e, same_doc, mask_per_head),
        query_features,
        feats_k,
        value_heads,
        incoming_state,
        norm_in,
    )
    mixed_heads = attended.astype(jnp.bfloat16)
    branch = layer_in + matmul(mixed_heads, w_out)
    normed_f, norm_f_back = jax.vjp(norm_rows, branch)
    h_ffn = (normed_f * gain_f).astype(jnp.bfloat16)
    activated, gelu_back = jax.vjp(jax.nn.gelu, matmul(h_ffn, w_up))
    hidden = activated.astype(jnp.bfloat16)
    grad_low = grad_out.astype(jnp.bfloat16)
    grad_wdown = matmul(hidden.T, grad_low)
    grad_pre = gelu_back(matmul(grad_low, w_down.T))[0].astype(jnp.bfloat16)
    grad_wup = matmul(h_ffn.T, grad_pre)
    grad_hffn = matmul(grad_pre, w_up.T)
    grad_gain_f = jnp.sum(grad_hffn * normed_f, axis=0)
    ffn_terms = (grad_wup, grad_wdown, grad_gain_f)
    grad_branch = grad_out + norm_f_back(grad_hffn * gain_f)[0]
    grad_blow = grad_branch.astype(jnp.bfloat16)
    grad_wout = matmul(mixed_heads.T, grad_blow)
    grad_fq, grad_fk, grad_vals, grad_state, grad_norm = attend_back(matmul(grad_blow, w_out.T))
    identity = (jnp.ones((), jnp.float32), jnp.zeros_like(grad_state), jnp.zeros_like(grad_norm))
    _, carry_state, carry_norm = entering(
        (kept_flag, grad_state, grad_norm), "seq", combine_carry, identity
    )
    _, tail_back = jax.vjp(lambda a, b: tail_sums(a, b, tail_mask), feats_k, value_heads)
    more_k, more_v = tail_back((carry_state, carry_norm))
    grad_q = lift_q_back(grad_fq)[0].astype(jnp.bfloat16)
    grad_k = lift_k_back(grad_fk + more_k)[0].astype(jnp.bfloat16)
    grad_v = (grad_vals + more_v).reshape(row_count, -1).astype(jnp.bfloat16)
    grad_hattn = matmul(grad_q, w_query.T) + matmul(grad_k, w_key.T) + matmul(grad_v, w_value.T)
    grad_gain_a = jnp.sum(grad_hattn * normed_a, axis=0)
    grad_in = grad_branch + norm_a_back(grad_hattn * gain_a)[0]
    attn_grads = (
        matmul(h_attn.T, grad_q),
        matmul(h_attn.T, grad_k),
        matmul(h_attn.T, grad_v),
        grad_wout,
        grad_gain_a,
    )
    return (grad_in, attn_grads, ffn_terms)


def local(
    inputs,
    cotangent,
    doc_lengths,
    feature_proj,
    w_query,
    w_key,
    w_value,
    w_out,
    w_up,
    w_down,
    gain_attn,
    gain_ffn,
):
    section_idx = lax.axis_index("section")
    seq_idx = lax.axis_index("seq")
    micro_count, _, row_count, feat_width = inputs.shape
    first_row = seq_idx * row_count
    projection = feature_proj[0]
    lengths_all = doc_lengths[:, 0, :]
    masters = (
        w_query[0],
        w_key[0],
        w_value[0],
        w_out[0],
        w_up[0],
        w_down[0],
        gain_attn[0],
        gain_ffn[0],
    )
    lowered = tuple((master.astype(jnp.bfloat16) for master in masters))
    gathered = jax.tree.map(
        lambda part, own: part.astype(own.dtype),
        lax.all_gather(as_sent(lowered), ("dp", "seq"), axis=0, tiled=True),
        lowered,
    )
    batch_range = jnp.arange(micro_count, dtype=jnp.int32)
    received = jnp.zeros((row_count, feat_width), jnp.bfloat16)
    outputs = jnp.zeros((micro_count, row_count, feat_width), jnp.float32)
    kept_inputs, kept_states, kept_norms = ([], [], [])
    for step_no in range(micro_count + 1):
        batch_no = step_no - section_idx
        is_valid = ((batch_no >= 0) & (batch_no < micro_count)).astype(jnp.float32)
        batch_idx = jnp.clip(batch_no, 0, micro_count - 1)
        own_input = inputs[min(step_no, micro_count - 1), 0].astype(jnp.float32)
        layer_in = jnp.where(section_idx == 0, own_input, received.astype(jnp.float32))
        lengths = lax.dynamic_index_in_dim(lengths_all, batch_idx, 0, keepdims=False)
        layer_out, incoming_state, norm_in = run_forward(
            layer_in, gathered, projection, lengths, first_row
        )
        sent_out = layer_out.astype(jnp.bfloat16)
        chosen = (batch_range == batch_idx).astype(jnp.float32) * is_valid
        outputs = outputs + chosen[:, None, None] * sent_out.astype(jnp.float32)[None]
        kept_inputs.append(layer_in)
        kept_states.append(incoming_state)
        kept_norms.append(norm_in)
        if step_no < micro_count:
            received = passed_along(sent_out, "section", 1)
    weights_back = jax.tree.map(
        lambda part, own: part.astype(own.dtype),
        lax.all_gather(as_sent(lowered), ("dp", "seq"), axis=0, tiled=True),
        lowered,
    )
    stacked_inputs = jnp.stack(kept_inputs)
    stacked_states = jnp.stack(kept_states)
    stacked_norms = jnp.stack(kept_norms)
    grad_recv = jnp.zeros((row_count, feat_width), jnp.bfloat16)
    grad_inputs = jnp.zeros((micro_count, row_count, feat_width), jnp.float32)
    totals = tuple((jnp.zeros(part.shape, jnp.float32) for part in weights_back))
    for step_no in range(micro_count + 1):
        batch_no = step_no - 1 + section_idx
        is_valid = ((batch_no >= 0) & (batch_no < micro_count)).astype(jnp.float32)
        batch_idx = jnp.clip(batch_no, 0, micro_count - 1)
        slot_idx = jnp.clip(step_no - 1 + 2 * section_idx, 0, micro_count)
        layer_in = lax.dynamic_index_in_dim(stacked_inputs, slot_idx, 0, keepdims=False)
        incoming_state = lax.dynamic_index_in_dim(stacked_states, slot_idx, 0, keepdims=False)
        norm_in = lax.dynamic_index_in_dim(stacked_norms, slot_idx, 0, keepdims=False)
        own_grad = cotangent[min(step_no, micro_count - 1), 0].astype(jnp.float32)
        grad_out = jnp.where(section_idx == 1, own_grad, grad_recv.astype(jnp.float32))
        lengths = lax.dynamic_index_in_dim(lengths_all, batch_idx, 0, keepdims=False)
        grad_in, attn_grads, ffn_terms = run_backward(
            layer_in,
            incoming_state,
            norm_in,
            grad_out,
            weights_back,
            projection,
            lengths,
            first_row,
        )
        grads = (
            attn_grads[0],
            attn_grads[1],
            attn_grads[2],
            attn_grads[3],
            ffn_terms[0],
            ffn_terms[1],
            attn_grads[4],
            ffn_terms[2],
        )
        totals = tuple(
            (total_part + is_valid * grad_part for total_part, grad_part in zip(totals, grads))
        )
        sent_back = grad_in.astype(jnp.bfloat16)
        chosen = (batch_range == batch_idx).astype(jnp.float32) * is_valid
        grad_inputs = grad_inputs + chosen[:, None, None] * sent_back.astype(jnp.float32)[None]
        if step_no < micro_count:
            grad_recv = passed_along(sent_back, "section", -1)
    shares = lax.psum_scatter(totals, ("dp", "seq"), scatter_dimension=0, tiled=True)
    activations = outputs.astype(jnp.bfloat16)[None, :, None]
    input_grad = grad_inputs.astype(jnp.bfloat16)[None, :, None]
    return (activations, input_grad) + tuple((share_part[None] for share_part in shares))


def solution(mesh):
    in_specs = (
        P(None, "dp", "seq", None),
        P(None, "dp", "seq", None),
        P(None, "dp", None),
        P("section", None, None, None),
        P("section", ("dp", "seq"), None),
        P("section", ("dp", "seq"), None),
        P("section", ("dp", "seq"), None),
        P("section", ("dp", "seq"), None),
        P("section", ("dp", "seq"), None),
        P("section", ("dp", "seq"), None),
        P("section", ("dp", "seq")),
        P("section", ("dp", "seq")),
    )
    out_specs = (
        P("section", None, "dp", "seq", None),
        P("section", None, "dp", "seq", None),
        P("section", ("dp", "seq"), None),
        P("section", ("dp", "seq"), None),
        P("section", ("dp", "seq"), None),
        P("section", ("dp", "seq"), None),
        P("section", ("dp", "seq"), None),
        P("section", ("dp", "seq"), None),
        P("section", ("dp", "seq")),
        P("section", ("dp", "seq")),
    )
    fits = mesh.shape["section"] == 2 and mesh.shape["dp"] == 4 and mesh.shape["seq"] == 4
    body = fast_local if fits else local
    return jax.shard_map(body, mesh=mesh, in_specs=in_specs, out_specs=out_specs, check_vma=False)
```
